128 devices in a mesh: dp: 16 (over x, y), tp: 8 (over z, core).
Axes of the slice: x: 4, y: 4, z: 4, core: 2. Of those that a mesh axis runs over, the one named last changes fastest.
Arguments:
- hidden: bfloat16 [32768, 8192], P('dp', 'tp'), may hold values from -6 to 6
- value_weight: bfloat16 [8192, 1024], P('tp'), may hold values from -0.0625 to 0.0625
- down_weights: bfloat16 [2048, 64, 8192], P('dp', None, 'tp'), may hold values from -0.0625 to 0.0625
- up_weights: bfloat16 [2048, 64, 1024], P('dp', None, 'tp'), may hold values from -0.75 to 0.75
- group_adapter_id: int32 [512], replicated, may hold values from 0 to 2047, as said below
- adapter_storage_row: int32 [2048], replicated, may hold values from 0 to 2047, as said below
- group_live_count: int32 [512], replicated, may hold values from 1 to 64, as said below
Outputs:
- projected: bfloat16 [32768, 1024], P('dp', 'tp')
The draws below stay inside these ranges and needn't reach their ends.
Inputs may be any that keep to these rules, and one draw needn't show every extreme that they name: Adapter a is stored at row adapter_storage_row[a] of down_weights and up_weights, that is on index adapter_storage_row[a] // 128 of dp; a permutation. `group_adapter_id`: the 32 groups of one index of dp name different adapters; at most 6 of them are stored on one index of dp, and some index of dp stores exactly 6 of every index's groups. `group_live_count`: slots of a group at and beyond its count are padding; every index of dp has a group of 64 live slots.
All inputs are finite; a program needn't handle non-finite values.
Results may differ from the reference program's by a relative error of at most 0.0029.
Values may be sent and summed in bfloat16 or wider, within the bound.
No kernel may reach another device: no remote copies, remote signals or barrier semaphores. Data moves between devices by JAX's collectives and lax.ppermute only.
A program may use at most 192 MiB of HBM per device.

```python
import jax
import jax.numpy as jnp
from jax import lax

MODEL_WIDTH = 8192
VALUE_WIDTH = 1024
ADAPTER_RANK = 64
ADP_OWN = 128
NG = 32
CAP = 64
ADAPTER_TOTAL = 2048
TOTAL = 32768
N_DP = 16


def adapter_plan(key):
    keys = jax.random.split(key, 5)
    home = jax.random.permutation(keys[0], ADAPTER_TOTAL).astype(jnp.int32)
    inverse = jnp.argsort(home).astype(jnp.int32)
    share = NG // N_DP
    hot_owner = jax.random.randint(keys[1], (), 0, N_DP)
    owner_ids = jnp.arange(N_DP).astype(jnp.int32)
    scores = jax.random.randint(keys[2], (N_DP, N_DP), 0, 2 ** 20) * N_DP + owner_ids[None, :]
    scores = jnp.where(owner_ids[None, :] == hot_owner, -1, scores)
    coldest = lax.top_k(scores, 2)[1]
    is_cold = jnp.any(owner_ids[None, :, None] == coldest[:, None, :], axis=2)
    loads = jnp.where(owner_ids[None, :] == hot_owner, 3 * share, jnp.where(is_cold, 0, share)).astype(jnp.int32)
    ends = jnp.cumsum(loads, axis=1)
    starts = ends - loads
    positions = jnp.arange(NG).astype(jnp.int32)
    owner_at = jnp.sum(positions[None, :, None] >= ends[:, None, :], axis=2).astype(jnp.int32)
    rank_at = positions[None, :] - jnp.take_along_axis(starts, owner_at, axis=1)
    slot_scores = jax.random.randint(keys[3], (N_DP, N_DP, ADP_OWN), 0, 2 ** 20) * ADP_OWN + jnp.arange(ADP_OWN)[None, None, :]
    slot_perm = jnp.argsort(slot_scores, axis=2).astype(jnp.int32)
    source_ids = jnp.arange(N_DP)[:, None]
    slot_at = slot_perm[source_ids, owner_at, rank_at]
    rows = owner_at * ADP_OWN + slot_at
    order_scores = jax.random.randint(keys[4], (N_DP, NG), 0, 2 ** 20) * NG + positions[None, :]
    shuffle = jnp.argsort(order_scores, axis=1)
    rows = jnp.take_along_axis(rows, shuffle, axis=1)
    return (home, inverse[rows.reshape(-1)].astype(jnp.int32))


def draw_group_adapter_id(key, part):
    plan = adapter_plan(key)
    return plan[1]


def draw_adapter_storage_row(key, part):
    plan = adapter_plan(key)
    return plan[0]


def draw_group_live_count(key, part):
    key = jax.random.fold_in(key, 7)
    first_key, second_key = jax.random.split(key)
    counts = jax.random.randint(first_key, (N_DP, NG), 1, CAP + 1)
    full_at = jax.random.randint(second_key, (N_DP,), 0, NG)
    positions = jnp.arange(NG)[None, :]
    counts = jnp.where(positions == full_at[:, None], CAP, counts)
    return counts.reshape(-1).astype(jnp.int32)


def steps_of(stream_key, shape, pieces, smallest, largest):
    gain = 1.0
    for dim, shards_of in pieces:
        draws = jax.random.uniform(jax.random.fold_in(jax.random.fold_in(stream_key, 6), dim), (shards_of,), jnp.float32, smallest / len(pieces), largest / len(pieces))
        gain = gain * jnp.repeat(jnp.exp(draws), shape[dim] // shards_of).reshape((-1,) + (1,) * (len(shape) - 1 - dim))
    return gain


def noise(rng, extent, scale, bound, pieces=(), dtype=jnp.bfloat16):
    array = scale * jax.random.normal(rng, extent, jnp.float32)
    if pieces:
        array = array * steps_of(rng, extent, pieces, -0.22, 0.18)
    return jnp.clip(array, -bound, bound).astype(dtype)


def setup_inputs(seed: int = 0) -> dict:
    key_list = jax.random.split(jax.random.key(seed), 8)
    return {
        "hidden": noise(key_list[0], (TOTAL, MODEL_WIDTH), 1.0, 6.0, ((0, 16), (1, 8))),
        "value_weight": noise(key_list[1], (MODEL_WIDTH, VALUE_WIDTH), MODEL_WIDTH ** -0.5, 0.0625, ((0, 8),)),
        "down_weights": noise(key_list[2], (ADAPTER_TOTAL, ADAPTER_RANK, MODEL_WIDTH), MODEL_WIDTH ** -0.5, 0.0625, ((0, 16), (2, 8))),
        "up_weights": noise(key_list[3], (ADAPTER_TOTAL, ADAPTER_RANK, VALUE_WIDTH), ADAPTER_RANK ** -0.5, 0.75, ((0, 16), (2, 8))),
        "group_adapter_id": draw_group_adapter_id(jax.random.fold_in(key_list[7], 71), 0),
        "adapter_storage_row": draw_adapter_storage_row(jax.random.fold_in(key_list[7], 71), 0),
        "group_live_count": draw_group_live_count(jax.random.fold_in(key_list[7], 71), 0),
    }


ADAPTER_SCALE = 0.5


def reference(hidden, value_weight, down_weights, up_weights, group_adapter_id, adapter_storage_row, group_live_count):
    stored_rows = adapter_storage_row[group_adapter_id].astype(jnp.int32)
    grouped = hidden.reshape(N_DP * NG, CAP, MODEL_WIDTH)

    def per_group(operands):
        rows_x, storage_row_index, live_count = operands
        down_block = lax.dynamic_index_in_dim(down_weights, storage_row_index, 0, keepdims=False)
        up_block = lax.dynamic_index_in_dim(up_weights, storage_row_index, 0, keepdims=False)
        low_rank = jnp.dot(rows_x, down_block.T, preferred_element_type=jnp.float32).astype(jnp.bfloat16)
        adapter_delta_rows = jnp.dot(low_rank, up_block, preferred_element_type=jnp.float32)
        base_output = jnp.dot(rows_x, value_weight, preferred_element_type=jnp.float32)
        active_rows = (jnp.arange(CAP).astype(jnp.int32) < live_count)[:, None]
        return jnp.where(active_rows, base_output + ADAPTER_SCALE * adapter_delta_rows, jnp.float32(0.0)).astype(jnp.bfloat16)

    results = lax.map(per_group, (grouped, stored_rows, group_live_count))
    return results.reshape(N_DP * NG * CAP, VALUE_WIDTH)
```

```python
import jax
import jax.numpy as jnp
from jax import lax
from jax.sharding import PartitionSpec as P

ADAPTER_SCALE = 0.5
MAIN = 2
MOST = 6
EXTRA = MOST - MAIN


def low_rank_sum(partial):
    rows, rank = partial.shape
    tp_count = lax.axis_size("tp")
    pieces = lax.all_to_all(partial, "tp", split_axis=0, concat_axis=0, tiled=True)
    mine = jnp.sum(pieces.reshape(tp_count, rows // tp_count, rank), axis=0).astype(jnp.bfloat16)
    return lax.all_gather(mine, "tp", axis=0, tiled=True)


def finish(base, low, ups, counts):
    groups = counts.shape[0]
    cap = base.shape[0] // groups
    delta = jnp.einsum(
        "gcr,grv->gcv", low.reshape(groups, cap, -1), ups, preferred_element_type=jnp.float32
    )
    merged = base.reshape(groups, cap, -1) + ADAPTER_SCALE * delta
    active = jnp.arange(cap)[None, :, None] < counts[:, None, None]
    out = jnp.where(active, merged, jnp.float32(0.0)).astype(jnp.bfloat16)
    return out.reshape(base.shape)


def packed(down, up):
    count = down.shape[0]
    up_rows = up.reshape(count, 8, 8, up.shape[2]).transpose(0, 2, 1, 3)
    return jnp.concatenate([down, up_rows.reshape(count, 8, -1)], axis=1)


def unpacked(rows, rank):
    count = rows.shape[0]
    up = rows[:, rank:].reshape(count, 8, 8, -1).transpose(0, 2, 1, 3)
    return rows[:, :rank], up.reshape(count, rank, -1)


def on_device(
    hidden,
    value_weight,
    down_weights,
    up_weights,
    group_adapter_id,
    adapter_storage_row,
    group_live_count,
):
    dp_count = lax.axis_size("dp")
    me = lax.axis_index("dp")
    owned, rank, width = down_weights.shape
    groups = group_adapter_id.shape[0] // dp_count
    cap = hidden.shape[0] // groups
    stored = adapter_storage_row[group_adapter_id]
    owners = (stored // owned).reshape(dp_count, groups)
    slots = (stored % owned).reshape(dp_count, groups)
    same = owners[:, :, None] == owners[:, None, :]
    earlier = jnp.arange(groups)[None, None, :] < jnp.arange(groups)[None, :, None]
    ranking = jnp.sum(same & earlier, axis=2)
    loads = jnp.sum(owners[:, :, None] == jnp.arange(dp_count)[None, None, :], axis=1)
    hot = jnp.argmax(jnp.sum(loads, axis=0)).astype(jnp.int32)
    fits = jnp.all((loads <= MAIN) | (jnp.arange(dp_count) == hot)[None, :])
    counts = lax.dynamic_slice_in_dim(group_live_count, me * groups, groups)
    my_owners = lax.dynamic_index_in_dim(owners, me, 0, keepdims=False)
    my_ranking = lax.dynamic_index_in_dim(ranking, me, 0, keepdims=False)

    def rows_for(owner, ranks):
        hits = (owners == owner)[:, :, None] & (ranking[:, :, None] == ranks[None, None, :])
        return jnp.sum(jnp.where(hits, slots[:, :, None], 0), axis=1)

    def wide(hidden, value_weight, down_weights, up_weights):
        base_terms = jnp.dot(hidden, value_weight, preferred_element_type=jnp.float32)
        base = lax.psum_scatter(base_terms, "tp", scatter_dimension=1, tiled=True)
        rows = rows_for(me, jnp.arange(MOST)).reshape(-1)
        downs = lax.all_to_all(down_weights[rows], "dp", 0, 0, tiled=True)
        ups = lax.all_to_all(up_weights[rows], "dp", 0, 0, tiled=True)
        picked = my_owners * MOST + my_ranking
        partial = jnp.einsum(
            "gcd,grd->gcr",
            hidden.reshape(groups, cap, width),
            downs[picked],
            preferred_element_type=jnp.float32,
        )
        low = low_rank_sum(partial.reshape(groups * cap, rank))
        return finish(base, low, ups[picked], counts)

    def narrow(hidden, value_weight, down_weights, up_weights):
        main_rows = rows_for(me, jnp.arange(MAIN)).reshape(-1)
        main_sent = packed(down_weights[main_rows], up_weights[main_rows])
        extra_rows = rows_for(hot, MAIN + jnp.arange(EXTRA)).reshape(-1)
        extra_sent = jnp.where(
            me == hot, packed(down_weights[extra_rows], up_weights[extra_rows]), jnp.bfloat16(0)
        )
        extra = lax.psum_scatter(extra_sent, "dp", scatter_dimension=0, tiled=True)
        main = lax.all_to_all(main_sent, "dp", 0, 0, tiled=True)
        base_terms = jnp.dot(hidden, value_weight, preferred_element_type=jnp.float32)
        base = lax.psum_scatter(base_terms, "tp", scatter_dimension=1, tiled=True)
        picked = jnp.where(
            my_ranking < MAIN,
            my_owners * MAIN + my_ranking,
            dp_count * MAIN + my_ranking - MAIN,
        )
        arrived = jnp.concatenate([main, extra], axis=0)[picked]
        downs, ups = unpacked(arrived, rank)
        partial = jnp.einsum(
            "gcd,grd->gcr",
            hidden.reshape(groups, cap, width),
            downs,
            preferred_element_type=jnp.float32,
        )
        low = low_rank_sum(partial.reshape(groups * cap, rank))
        return finish(base, low, ups, counts)

    return lax.cond(fits, narrow, wide, hidden, value_weight, down_weights, up_weights)


def solution(mesh):
    return jax.shard_map(
        on_device,
        mesh=mesh,
        in_specs=(
            P("dp", "tp"),
            P("tp", None),
            P("dp", None, "tp"),
            P("dp", None, "tp"),
            P(),
            P(),
            P(),
        ),
        out_specs=P("dp", "tp"),
        check_vma=False,
    )
```

```python
import math

import jax
import jax.numpy as jnp
from jax import lax
from jax.experimental import pallas as pl
from jax.experimental.pallas import tpu as pltpu
from jax.sharding import PartitionSpec as P

ADAPTER_SCALE = 0.5
MAIN = 2
MOST = 6
EXTRA = MOST - MAIN


def low_rank_sum(partial):
    rows, rank = partial.shape
    tp_count = lax.axis_size("tp")
    pieces = lax.all_to_all(partial, "tp", split_axis=0, concat_axis=0, tiled=True)
    mine = jnp.sum(pieces.reshape(tp_count, rows // tp_count, rank), axis=0).astype(jnp.bfloat16)
    return lax.all_gather(mine, "tp", axis=0, tiled=True)


def finish(base, low, ups, counts):
    groups = counts.shape[0]
    cap = base.shape[0] // groups
    delta = jnp.einsum(
        "gcr,grv->gcv", low.reshape(groups, cap, -1), ups, preferred_element_type=jnp.float32
    )
    merged = base.reshape(groups, cap, -1) + ADAPTER_SCALE * delta
    active = jnp.arange(cap)[None, :, None] < counts[:, None, None]
    out = jnp.where(active, merged, jnp.float32(0.0)).astype(jnp.bfloat16)
    return out.reshape(base.shape)


def shift(value, dx, dy):
    side = math.isqrt(lax.axis_size("dp"))
    pairs = [
        (x * side + y, (x + dx) % side * side + (y + dy) % side)
        for x in range(side)
        for y in range(side)
    ]
    return lax.ppermute(value, "dp", pairs)


def copy_units(rows, down, up, out, up_in, up_out, down_sem, up_sem, out_sem):
    units = out.shape[0]
    rank = down.shape[1]
    lanes = up.shape[2]
    down_copies, up_copies = [], []
    for i in range(units * 2):
        row = rows[i]
        unit, half = i // 2, i % 2
        up_copies.append(pltpu.make_async_copy(up.at[row], up_in.at[i], up_sem.at[i]))
        down_copies.append(
            pltpu.make_async_copy(
                down.at[row], out.at[unit, pl.ds(half * rank, rank)], down_sem.at[i]
            )
        )
        up_copies[-1].start()
        down_copies[-1].start()
    for i in range(units * 2):
        unit, half = i // 2, i % 2
        up_copies[i].wait()
        for part in range(rank // 16):
            at = (half * (rank // 16) + part) * lanes
            up_out[unit, :, at : at + lanes] = up_in[i, part * 16 : part * 16 + 16, :]
    last = pltpu.make_async_copy(up_out, out.at[:, pl.ds(2 * rank, 16)], out_sem)
    last.start()
    for copy in down_copies:
        copy.wait()
    last.wait()


def gather_kernel(active, rows, down, up, out, *scratch):
    @pl.when(active[0] == 1)
    def _():
        copy_units(rows, down, up, out, *scratch)


def gather_units(active, rows, down, up):
    count = rows.shape[0]
    _, rank, width = down.shape
    lanes = up.shape[2]
    smem = pl.BlockSpec(memory_space=pltpu.SMEM)
    hbm = pl.BlockSpec(memory_space=pl.ANY)
    return pl.pallas_call(
        gather_kernel,
        out_shape=jax.ShapeDtypeStruct((count // 2, 2 * rank + 16, width), down.dtype),
        in_specs=[smem, smem, hbm, hbm],
        out_specs=hbm,
        scratch_shapes=[
            pltpu.VMEM((count, rank, lanes), up.dtype),
            pltpu.VMEM((count // 2, 16, width), up.dtype),
            pltpu.SemaphoreType.DMA((count,)),
            pltpu.SemaphoreType.DMA((count,)),
            pltpu.SemaphoreType.DMA,
        ],
        compiler_params=pltpu.CompilerParams(vmem_limit_bytes=12 << 20),
        cost_estimate=pl.CostEstimate(
            flops=0, bytes_accessed=count * rank * (width + lanes) * 4, transcendentals=0
        ),
    )(active, rows, down, up)


def low_kernel(order, sources, hidden, units, out):
    groups = order.shape[0]
    pairs = groups // 2
    rank = out.shape[1] // 2
    cap = out.shape[0] // pairs

    def one(j):
        g = pl.multiple_of(order[j] * cap, cap)
        at = pl.multiple_of(sources[j], 16)
        return lax.dot_general(
            hidden[pl.ds(g, cap), :],
            units[pl.ds(at, rank), :],
            (((1,), (1,)), ((), ())),
            preferred_element_type=jnp.float32,
        )

    def body(i, carry):
        both = jnp.concatenate([one(i), one(i + pairs)], axis=1)
        out[pl.ds(pl.multiple_of(i * cap, cap), cap), :] = both
        return carry

    lax.fori_loop(0, pairs, body, 0, unroll=2)


def low_partial(order, sources, hidden, units, cap, rank):
    groups = order.shape[0]
    smem = pl.BlockSpec(memory_space=pltpu.SMEM)
    vmem = pl.BlockSpec(memory_space=pltpu.VMEM)
    return pl.pallas_call(
        low_kernel,
        out_shape=jax.ShapeDtypeStruct((groups // 2 * cap, 2 * rank), jnp.float32),
        in_specs=[smem, smem, vmem, vmem],
        out_specs=vmem,
        compiler_params=pltpu.CompilerParams(vmem_limit_bytes=24 << 20),
        cost_estimate=pl.CostEstimate(
            flops=groups * cap * rank * 2 * hidden.shape[1],
            bytes_accessed=(hidden.size + units.size) * 2,
            transcendentals=0,
        ),
    )(order, sources, hidden, units)


def out_kernel(order, places, counts, base, low, packs, out):
    groups = order.shape[0]
    pairs = groups // 2
    rank = low.shape[1] // 2
    cap = base.shape[0] // groups
    lanes = base.shape[1]
    rows = lax.broadcasted_iota(jnp.int32, (cap, lanes), 0)

    def one(j, factor):
        g = order[j]
        place = places[j]
        unit = place // 2
        at = (place % 2) * (rank // 16) * lanes
        up = jnp.concatenate(
            [
                packs[unit, :, pl.ds(pl.multiple_of(at + part * lanes, lanes), lanes)]
                for part in range(rank // 16)
            ],
            axis=0,
        )
        delta = jnp.dot(factor, up, preferred_element_type=jnp.float32)
        here = pl.ds(pl.multiple_of(g * cap, cap), cap)
        merged = base[here, :] + ADAPTER_SCALE * delta
        out[here, :] = jnp.where(rows < counts[g], merged, 0.0).astype(out.dtype)

    def body(i, carry):
        both = low[pl.ds(pl.multiple_of(i * cap, cap), cap), :]
        one(i, both[:, :rank])
        one(i + pairs, both[:, rank:])
        return carry

    lax.fori_loop(0, pairs, body, 0, unroll=2)


def combine(order, places, counts, base, low, packs):
    smem = pl.BlockSpec(memory_space=pltpu.SMEM)
    vmem = pl.BlockSpec(memory_space=pltpu.VMEM)
    return pl.pallas_call(
        out_kernel,
        out_shape=jax.ShapeDtypeStruct(base.shape, jnp.bfloat16),
        in_specs=[smem, smem, smem, vmem, vmem, vmem],
        out_specs=vmem,
        compiler_params=pltpu.CompilerParams(vmem_limit_bytes=12 << 20),
        cost_estimate=pl.CostEstimate(
            flops=base.size * low.shape[1], bytes_accessed=base.size * 8, transcendentals=0
        ),
    )(order, places, counts, base, low, packs)


def spread(units, along, across, a, b):
    plus = along(units[2, :2], 1)
    minus = along(units[2, 2:], -1)
    plus = along(jnp.where(a == 0, units[1], jnp.concatenate([plus, plus])), 1)
    minus = along(jnp.where(a == 0, units[3], jnp.concatenate([minus, minus])), -1)
    far = jnp.concatenate([plus[:2], minus[2:]])
    line = jnp.where(a == 0, units[0], jnp.where(a == 1, plus, jnp.where(a == 3, minus, far)))
    back = across(line[3], -1)
    ahead = across(line[2], 1)
    ahead = across(jnp.where(b == 0, line[1], ahead), 1)
    return jnp.where(b == 0, line[0], jnp.where(b == 3, back, ahead))


def on_device(
    hidden,
    value_weight,
    down_weights,
    up_weights,
    group_adapter_id,
    adapter_storage_row,
    group_live_count,
):
    dp_count = lax.axis_size("dp")
    me = lax.axis_index("dp")
    owned, rank, width = down_weights.shape
    groups = group_adapter_id.shape[0] // dp_count
    cap = hidden.shape[0] // groups
    stored = adapter_storage_row[group_adapter_id]
    owners = (stored // owned).reshape(dp_count, groups)
    slots = (stored % owned).reshape(dp_count, groups)
    same = owners[:, :, None] == owners[:, None, :]
    earlier = jnp.arange(groups)[None, None, :] < jnp.arange(groups)[None, :, None]
    ranking = jnp.sum(same & earlier, axis=2)
    loads = jnp.sum(owners[:, :, None] == jnp.arange(dp_count)[None, None, :], axis=1)
    hot = jnp.argmax(jnp.sum(loads, axis=0)).astype(jnp.int32)
    fits = jnp.all((loads <= MAIN) | (jnp.arange(dp_count) == hot)[None, :])
    counts = lax.dynamic_slice_in_dim(group_live_count, me * groups, groups)
    my_owners = lax.dynamic_index_in_dim(owners, me, 0, keepdims=False)
    my_ranking = lax.dynamic_index_in_dim(ranking, me, 0, keepdims=False)

    def rows_for(owner, ranks):
        hits = (owners == owner)[:, :, None] & (ranking[:, :, None] == ranks[None, None, :])
        return jnp.sum(jnp.where(hits, slots[:, :, None], 0), axis=1)

    def wide(hidden, value_weight, down_weights, up_weights):
        base_terms = jnp.dot(hidden, value_weight, preferred_element_type=jnp.float32)
        base = lax.psum_scatter(base_terms, "tp", scatter_dimension=1, tiled=True)
        rows = rows_for(me, jnp.arange(MOST)).reshape(-1)
        downs = lax.all_to_all(down_weights[rows], "dp", 0, 0, tiled=True)
        ups = lax.all_to_all(up_weights[rows], "dp", 0, 0, tiled=True)
        picked = my_owners * MOST + my_ranking
        partial = jnp.einsum(
            "gcd,grd->gcr",
            hidden.reshape(groups, cap, width),
            downs[picked],
            preferred_element_type=jnp.float32,
        )
        low = low_rank_sum(partial.reshape(groups * cap, rank))
        return finish(base, low, ups[picked], counts)

    def narrow(hidden, value_weight, down_weights, up_weights):
        side = math.isqrt(dp_count)
        always = jnp.ones((1,), jnp.int32)
        main_rows = rows_for(me, jnp.arange(MAIN)).reshape(-1)
        main_sent = gather_units(always, main_rows, down_weights, up_weights)
        main = lax.all_to_all(main_sent, "dp", 0, 0, tiled=True)
        extra_rows = rows_for(hot, MAIN + jnp.arange(EXTRA))
        steps = jnp.arange(side)
        xs = (hot // side + steps) % side
        ys = (hot % side + steps) % side
        by_x = (xs[:, None] * side + ys[None, :]).reshape(-1)
        by_y = (xs[None, :] * side + ys[:, None]).reshape(-1)
        is_hot = (me == hot).astype(jnp.int32).reshape(1)
        asked = jnp.concatenate([extra_rows[by_x, :2].reshape(-1), extra_rows[by_y, 2:].reshape(-1)])
        sent = gather_units(is_hot, asked, down_weights, up_weights)
        sent = sent.reshape(2, side, side, *sent.shape[1:])
        a = (me // side - hot // side) % side
        b = (me % side - hot % side) % side
        along_x = lambda value, step: shift(value, step, 0)
        along_y = lambda value, step: shift(value, 0, step)
        extra_x = spread(sent[0], along_x, along_y, a, b)
        extra_y = spread(sent[1], along_y, along_x, b, a)
        base_terms = jnp.dot(hidden, value_weight, preferred_element_type=jnp.float32)
        base = lax.psum_scatter(base_terms, "tp", scatter_dimension=1, tiled=True)
        unit_rows = main.shape[1]
        late = (my_owners == hot) & (my_ranking >= MAIN)
        place = jnp.where(
            late, dp_count * MAIN + my_ranking - MAIN, my_owners * MAIN + my_ranking
        )
        turn = jnp.where(late, groups - EXTRA + my_ranking - MAIN, jnp.cumsum(~late) - 1)
        here = turn[None, :] == jnp.arange(groups)[:, None]
        order = jnp.sum(jnp.where(here, jnp.arange(groups)[None, :], 0), axis=1)
        places = jnp.sum(jnp.where(here, place[None, :], 0), axis=1)
        units = jnp.concatenate([main, extra_x[None], extra_y[None]], axis=0)
        sources = places // 2 * unit_rows + places % 2 * rank
        partial = low_partial(order, sources, hidden, units.reshape(-1, width), cap, rank)
        low = low_rank_sum(partial)
        return combine(order, places, counts, base, low, units[:, 2 * rank :])

    return lax.cond(fits, narrow, wide, hidden, value_weight, down_weights, up_weights)


def solution(mesh):
    return jax.shard_map(
        on_device,
        mesh=mesh,
        in_specs=(
            P("dp", "tp"),
            P("tp", None),
            P("dp", None, "tp"),
            P("dp", None, "tp"),
            P(),
            P(),
            P(),
        ),
        out_specs=P("dp", "tp"),
        check_vma=False,
    )
```

```python
import functools
import math

import jax
import jax.numpy as jnp
from jax import lax
from jax.experimental import pallas as pl
from jax.experimental.pallas import tpu as pltpu
from jax.sharding import PartitionSpec as P

ADAPTER_SCALE = 0.5
MAIN = 2
MOST = 6
EXTRA = MOST - MAIN


def low_rank_sum(partial):
    rows, rank = partial.shape
    tp_count = lax.axis_size("tp")
    pieces = lax.all_to_all(partial, "tp", split_axis=0, concat_axis=0, tiled=True)
    mine = jnp.sum(pieces.reshape(tp_count, rows // tp_count, rank), axis=0).astype(jnp.bfloat16)
    return lax.all_gather(mine, "tp", axis=0, tiled=True)


def finish(base, low, ups, counts):
    groups = counts.shape[0]
    cap = base.shape[0] // groups
    delta = jnp.einsum(
        "gcr,grv->gcv", low.reshape(groups, cap, -1), ups, preferred_element_type=jnp.float32
    )
    merged = base.reshape(groups, cap, -1) + ADAPTER_SCALE * delta
    active = jnp.arange(cap)[None, :, None] < counts[:, None, None]
    out = jnp.where(active, merged, jnp.float32(0.0)).astype(jnp.bfloat16)
    return out.reshape(base.shape)


SMEM = pl.BlockSpec(memory_space=pltpu.SMEM)
VMEM = pl.BlockSpec(memory_space=pltpu.VMEM)
HBM = pl.BlockSpec(memory_space=pl.ANY)
LANES = 128
ORDER, PLACE, FLAGS = 0, 1, 2
HOT, FITS = 0, 1


def shift(value, dx, dy):
    side = math.isqrt(lax.axis_size("dp"))
    pairs = [
        (x * side + y, (x + dx) % side * side + (y + dy) % side)
        for x in range(side)
        for y in range(side)
    ]
    return lax.ppermute(value, "dp", pairs)


def index_kernel(me_ref, ids_ref, table_ref, served_ref, mine_ref, owner_ref, rank_ref):
    total = ids_ref.shape[0]
    dp_count = served_ref.shape[0]
    groups = total // dp_count
    chunks = table_ref.shape[0]
    owned = chunks * LANES // dp_count
    me = me_ref[0]
    f32, bf16 = jnp.float32, jnp.bfloat16
    ids = ids_ref[...]
    lane = lax.broadcasted_iota(jnp.int32, (total, LANES), 1)
    found = jnp.zeros((total, LANES), jnp.int32)
    for c in range(chunks):
        found += jnp.where(ids == lane + c * LANES, table_ref[c : c + 1, :], 0)
    stored = jnp.sum(found, axis=1, keepdims=True)
    owner = lax.div(stored, owned)
    slot = stored - owner * owned
    holds = jnp.where(owner == lane, 1.0, 0.0)
    low = lax.broadcasted_iota(jnp.int32, (groups, groups), 0)
    low = jnp.where(low > lax.broadcasted_iota(jnp.int32, (groups, groups), 1), 1.0, 0.0)
    low = low.astype(bf16)
    holds16 = holds.astype(bf16)
    before = jnp.concatenate(
        [
            jnp.dot(low, holds16[r * groups : (r + 1) * groups], preferred_element_type=f32)
            for r in range(dp_count)
        ],
        axis=0,
    )
    ranking = jnp.sum(before * holds, axis=1, keepdims=True).astype(jnp.int32)
    owner_ref[...] = jnp.broadcast_to(owner, (total, LANES))
    rank_ref[...] = jnp.broadcast_to(ranking, (total, LANES))
    block_of = lax.div(lax.broadcasted_iota(jnp.int32, (dp_count, total), 1), groups)
    block = block_of == lax.broadcasted_iota(jnp.int32, (dp_count, total), 0)
    block = jnp.where(block, 1.0, 0.0).astype(bf16)
    loads = jnp.dot(block, holds16, preferred_element_type=f32)
    kept = jnp.where((owner == me) & (ranking == lane), slot, 0).astype(f32).astype(bf16)
    served_ref[...] = jnp.dot(block, kept, preferred_element_type=f32).astype(jnp.int32)
    least = jnp.min(loads, axis=0, keepdims=True)
    row_lane = lax.broadcasted_iota(jnp.int32, (1, LANES), 1)
    hot = jnp.min(jnp.where(least >= MOST, row_lane, LANES), axis=1, keepdims=True)
    spare = jnp.where(row_lane == hot, 0.0, loads)
    most = jnp.max(jnp.max(spare, axis=0, keepdims=True), axis=1, keepdims=True)
    fits = jnp.where(most <= MAIN, 1, 0)
    at = pl.ds(pl.multiple_of(me * groups, groups), groups)
    my_owner = owner_ref[at, :]
    my_rank = rank_ref[at, :]
    late = (my_owner == hot) & (my_rank >= MAIN)
    place = jnp.where(late, dp_count * MAIN + my_rank - MAIN, my_owner * MAIN + my_rank)
    early = jnp.where(late, 0.0, 1.0).astype(bf16)
    ahead = jnp.dot(low, early, preferred_element_type=f32).astype(jnp.int32)
    turn = jnp.where(late, groups - EXTRA + my_rank - MAIN, ahead)
    group_lane = lax.broadcasted_iota(jnp.int32, (groups, LANES), 1)
    group = lax.broadcasted_iota(jnp.int32, (groups, LANES), 0)
    here = turn == group_lane
    mine_ref[...] = jnp.zeros(mine_ref.shape, jnp.int32)
    mine_ref[ORDER : ORDER + 1, :] = jnp.sum(jnp.where(here, group, 0), axis=0, keepdims=True)
    mine_ref[PLACE : PLACE + 1, :] = jnp.sum(jnp.where(here, place, 0), axis=0, keepdims=True)
    mine_ref[FLAGS : FLAGS + 1, :] = jnp.where(
        row_lane == HOT, hot, jnp.where(row_lane == FITS, fits, 0)
    )


def index_tables(me, ids, table, dp_count):
    total = ids.shape[0]
    return pl.pallas_call(
        index_kernel,
        out_shape=(
            jax.ShapeDtypeStruct((dp_count, LANES), jnp.int32),
            jax.ShapeDtypeStruct((8, LANES), jnp.int32),
        ),
        in_specs=[SMEM, VMEM, VMEM],
        out_specs=(VMEM, VMEM),
        scratch_shapes=[pltpu.VMEM((total, LANES), jnp.int32)] * 2,
        compiler_params=pltpu.CompilerParams(vmem_limit_bytes=8 << 20),
    )(me, ids.reshape(total, 1), table.reshape(-1, LANES))


def copy_units(wanted, down, up, up_in, up_out, down_sem, up_sem, out_sem):
    rank = down.shape[1]
    lanes = up.shape[2]
    steps = rank // 16
    waits = []
    ups = []
    for i, (dest, index, rows) in enumerate(wanted):
        for half in range(2):
            n = 2 * i + half
            ups.append(pltpu.make_async_copy(up.at[rows[half]], up_in.at[n], up_sem.at[n]))
            ups[-1].start()
            waits.append(
                pltpu.make_async_copy(
                    down.at[rows[half]], dest.at[index, pl.ds(half * rank, rank)], down_sem.at[n]
                )
            )
            waits[-1].start()
    for i, (dest, index, rows) in enumerate(wanted):
        for half in range(2):
            n = 2 * i + half
            ups[n].wait()
            for part in range(steps):
                at = (half * steps + part) * lanes
                up_out[i, :, at : at + lanes] = up_in[n, part * 16 : part * 16 + 16, :]
        waits.append(
            pltpu.make_async_copy(
                up_out.at[i], dest.at[index, pl.ds(2 * rank, 16)], out_sem.at[i]
            )
        )
        waits[-1].start()
    for copy in waits:
        copy.wait()


def main_kernel(served, down, up, out, *scratch):
    wanted = [(out, p, (served[p, 0], served[p, 1])) for p in range(out.shape[0])]
    copy_units(wanted, down, up, *scratch)


def extra_kernel(lines, me, served, mine, down, up, *refs):
    outs, scratch = refs[: len(lines)], refs[len(lines) :]
    dp_count = served.shape[0]
    side = math.isqrt(dp_count)
    hot = mine[FLAGS, HOT]

    @pl.when(hot == me[0])
    def _():
        hot_x, hot_y = lax.div(hot, side), lax.rem(hot, side)
        wanted = []
        for out, (x_first, a, units) in zip(outs, lines):
            for i, b in enumerate(units):
                dx, dy = (a, b) if x_first else (b, a)
                peer = lax.rem(hot_x + dx, side) * side + lax.rem(hot_y + dy, side)
                first = MAIN if x_first else MAIN + 2
                wanted.append((out, i, (served[peer, first], served[peer, first + 1])))
        copy_units(wanted, down, up, *scratch)


def gather_call(kernel, shapes, count, scalars, down, up):
    _, rank, width = down.shape
    lanes = up.shape[2]
    return pl.pallas_call(
        kernel,
        out_shape=[jax.ShapeDtypeStruct((n, 2 * rank + 16, width), down.dtype) for n in shapes],
        in_specs=[SMEM] * len(scalars) + [HBM, HBM],
        out_specs=[HBM] * len(shapes),
        scratch_shapes=[
            pltpu.VMEM((2 * count, rank, lanes), up.dtype),
            pltpu.VMEM((count, 16, width), up.dtype),
            pltpu.SemaphoreType.DMA((2 * count,)),
            pltpu.SemaphoreType.DMA((2 * count,)),
            pltpu.SemaphoreType.DMA((count,)),
        ],
        compiler_params=pltpu.CompilerParams(vmem_limit_bytes=12 << 20),
        cost_estimate=pl.CostEstimate(
            flops=0, bytes_accessed=count * rank * (width + lanes) * 8, transcendentals=0
        ),
    )(*scalars, down, up)


def local_copies(when, copies, sems):
    @pl.when(when)
    def _():
        started = [
            pltpu.make_async_copy(src, dst, sems.at[i]) for i, (src, dst) in enumerate(copies)
        ]
        for copy in started:
            copy.start()
        for copy in started:
            copy.wait()


def relay_kernel(offsets, *refs):
    sems = refs[-1]
    fresh = refs[:4]
    outs = refs[8:12]
    for i in range(4):
        near = 1 if i % 2 == 0 else 3
        local_copies(offsets[i // 2] == near, [(fresh[i], outs[i].at[pl.ds(0, 2)])], sems)


def relay(offsets, fresh, kept):
    return pl.pallas_call(
        relay_kernel,
        out_shape=[jax.ShapeDtypeStruct(k.shape, k.dtype) for k in kept],
        in_specs=[SMEM] + [HBM] * 8,
        out_specs=[HBM] * 4,
        input_output_aliases={5 + i: i for i in range(4)},
        scratch_shapes=[pltpu.SemaphoreType.DMA((4,))],
        cost_estimate=pl.CostEstimate(flops=0, bytes_accessed=1 << 21, transcendentals=0),
    )(offsets, *fresh, *kept)


def line_kernel(offsets, *refs):
    sems = refs[-1]
    ins, outs = refs[:6], refs[6:14]
    for h in range(2):
        own, plus, minus = ins[3 * h : 3 * h + 3]
        out = outs[4 * h : 4 * h + 4]
        far = [plus.at[0], plus.at[1], minus.at[0], minus.at[1]]
        for a, source in ((0, own), (1, plus), (2, None), (3, minus)):
            copies = [(far[i] if a == 2 else source.at[i], out[i]) for i in range(4)]
            local_copies(offsets[h] == a, copies, sems)


def line(offsets, ins):
    unit = ins[0].shape[1:]
    return pl.pallas_call(
        line_kernel,
        out_shape=[jax.ShapeDtypeStruct(unit, ins[0].dtype)] * 8,
        in_specs=[SMEM] + [HBM] * 6,
        out_specs=[HBM] * 8,
        scratch_shapes=[pltpu.SemaphoreType.DMA((4,))],
        cost_estimate=pl.CostEstimate(flops=0, bytes_accessed=5 << 20, transcendentals=0),
    )(offsets, *ins)


def pass_kernel(offsets, *refs):
    sems = refs[-1]
    for h in range(2):
        local_copies(offsets[1 - h] == 1, [(refs[h], refs[4 + h])], sems)


def pass_on(offsets, fresh, kept):
    return pl.pallas_call(
        pass_kernel,
        out_shape=[jax.ShapeDtypeStruct(k.shape, k.dtype) for k in kept],
        in_specs=[SMEM] + [HBM] * 4,
        out_specs=[HBM] * 2,
        input_output_aliases={3: 0, 4: 1},
        scratch_shapes=[pltpu.SemaphoreType.DMA((2,))],
        cost_estimate=pl.CostEstimate(flops=0, bytes_accessed=1 << 20, transcendentals=0),
    )(offsets, *fresh, *kept)


def low_kernel(mine, hidden, main, *refs):
    extras, out = refs[:-1], refs[-1]
    rank = out.shape[1] // 2
    dp_count = main.shape[0]
    pairs = dp_count
    cap = out.shape[0] // pairs

    def product(j, weights):
        g = pl.multiple_of(mine[ORDER, j] * cap, cap)
        return lax.dot_general(
            hidden[pl.ds(g, cap), :],
            weights,
            (((1,), (1,)), ((), ())),
            preferred_element_type=jnp.float32,
        )

    def one(j):
        place = mine[PLACE, j]
        unit = lax.div(place, 2)
        at = pl.multiple_of((place - 2 * unit) * rank, rank)
        return product(j, main[unit, pl.ds(at, rank), :])

    def store(i, first, second):
        out[pl.ds(pl.multiple_of(i * cap, cap), cap), :] = jnp.concatenate([first, second], axis=1)

    def body(i, carry):
        store(i, one(i), one(i + pairs))
        return carry

    full = pairs - 2 * len(extras)
    lax.fori_loop(0, full, body, 0, unroll=2)
    for e in range(2 * len(extras)):
        weights = extras[e // 2][e % 2 * rank : (e % 2 + 1) * rank, :]
        store(full + e, one(full + e), product(full + e + pairs, weights))


def low_partial(mine, hidden, main, extras, cap, rank):
    pairs = main.shape[0]
    return pl.pallas_call(
        low_kernel,
        out_shape=jax.ShapeDtypeStruct((pairs * cap, 2 * rank), jnp.float32),
        in_specs=[SMEM] + [VMEM] * (2 + len(extras)),
        out_specs=VMEM,
        compiler_params=pltpu.CompilerParams(vmem_limit_bytes=24 << 20),
        cost_estimate=pl.CostEstimate(
            flops=hidden.size * rank * 2,
            bytes_accessed=(hidden.size + main.size) * 2,
            transcendentals=0,
        ),
    )(mine, hidden, main, *extras)


def low_rank_rounds(partial):
    tp_count = lax.axis_size("tp")
    chips = tp_count // 2
    t = lax.axis_index("tp")
    z, core = t // 2, t % 2
    half = partial.shape[0] // 2
    piece = half // chips
    swap = [(i, i ^ 1) for i in range(tp_count)]
    turn = lambda d: [(i, (i + 2 * d) % tp_count) for i in range(tp_count)]
    cut = lambda array, start, size: lax.dynamic_slice_in_dim(array, start, size, 0)
    total = cut(partial, core * half, half) + lax.ppermute(
        cut(partial, (1 - core) * half, half), "tp", swap
    )
    pieces = [
        lax.ppermute(cut(total, (z + d) % chips * piece, piece), "tp", turn(d))
        for d in range(1, chips)
    ]
    summed = (cut(total, z * piece, piece) + sum(pieces)).astype(jnp.bfloat16)
    own = jnp.stack([summed] + [lax.ppermute(summed, "tp", turn(d)) for d in range(1, chips)])
    return own, lax.ppermute(own, "tp", swap)


def out_kernel(where, mine, counts, base, own, other, main, *refs):
    extras, out = refs[:-1], refs[-1]
    groups = counts.shape[0]
    pairs = groups // 2
    cap = base.shape[0] // groups
    chips, piece, rank = own.shape[0], own.shape[1], own.shape[2] // 2
    lanes = base.shape[1]
    z, core = where[0], where[1]
    steps = rank // 16
    rows = lax.broadcasted_iota(jnp.int32, (cap, lanes), 0)
    per_piece = piece // cap

    def factors(i):
        half = lax.div(i, pairs // 2)
        rest = i - half * (pairs // 2)
        quarter = lax.div(rest, per_piece)
        at = pl.multiple_of((rest - quarter * per_piece) * cap, cap)
        slot = lax.rem(z - quarter + chips, chips)
        pick = pl.ds(at, cap)
        return jnp.where(half == core, own[slot, pick, :], other[slot, pick, :])

    def one(j, factor, up):
        g = mine[ORDER, j]
        delta = jnp.dot(factor, up, preferred_element_type=jnp.float32)
        here = pl.ds(pl.multiple_of(g * cap, cap), cap)
        merged = base[here, :] + ADAPTER_SCALE * delta
        out[here, :] = jnp.where(rows < counts[g], merged, 0.0).astype(out.dtype)

    def up_main(j):
        place = mine[PLACE, j]
        unit = lax.div(place, 2)
        at = (place - 2 * unit) * steps * lanes
        parts = [
            main[unit, :, pl.ds(pl.multiple_of(at + part * lanes, lanes), lanes)]
            for part in range(steps)
        ]
        return jnp.concatenate(parts, axis=0)

    def body(i, carry):
        both = factors(i)
        one(i, both[:, :rank], up_main(i))
        one(i + pairs, both[:, rank:], up_main(i + pairs))
        return carry

    full = pairs - 2 * len(extras)
    lax.fori_loop(0, full, body, 0, unroll=2)
    for e in range(2 * len(extras)):
        both = factors(jnp.int32(full + e))
        one(full + e, both[:, :rank], up_main(full + e))
        starts = [(e % 2 * steps + part) * lanes for part in range(steps)]
        up = jnp.concatenate([extras[e // 2][:, s : s + lanes] for s in starts], axis=0)
        one(full + e + pairs, both[:, rank:], up)


def combine(where, mine, counts, base, own, other, main, extras, rank):
    packs = pl.BlockSpec((main.shape[0], 16, main.shape[2]), lambda i: (0, rank // 8, 0))
    pack = pl.BlockSpec((16, main.shape[2]), lambda i: (rank // 8, 0))
    whole = lambda array: pl.BlockSpec(array.shape, lambda i: (0,) * array.ndim)
    return pl.pallas_call(
        out_kernel,
        grid=(1,),
        out_shape=jax.ShapeDtypeStruct(base.shape, jnp.bfloat16),
        in_specs=[SMEM, SMEM, SMEM, whole(base), whole(own), whole(other), packs]
        + [pack] * len(extras),
        out_specs=whole(base),
        compiler_params=pltpu.CompilerParams(vmem_limit_bytes=12 << 20),
        cost_estimate=pl.CostEstimate(
            flops=base.size * rank * 2, bytes_accessed=base.size * 8, transcendentals=0
        ),
    )(where, mine, counts, base, own, other, main, *extras)


def on_device(
    hidden,
    value_weight,
    down_weights,
    up_weights,
    group_adapter_id,
    adapter_storage_row,
    group_live_count,
):
    dp_count = lax.axis_size("dp")
    me = lax.axis_index("dp")
    owned, rank, width = down_weights.shape
    groups = group_adapter_id.shape[0] // dp_count
    cap = hidden.shape[0] // groups
    me_row = me.astype(jnp.int32).reshape(1)
    served, mine = index_tables(me_row, group_adapter_id, adapter_storage_row, dp_count)
    counts = lax.dynamic_slice_in_dim(group_live_count, me * groups, groups)

    def wide(hidden, value_weight, down_weights, up_weights):
        stored = adapter_storage_row[group_adapter_id]
        owners = (stored // owned).reshape(dp_count, groups)
        slots = (stored % owned).reshape(dp_count, groups)
        same = owners[:, :, None] == owners[:, None, :]
        earlier = jnp.arange(groups)[None, None, :] < jnp.arange(groups)[None, :, None]
        ranking = jnp.sum(same & earlier, axis=2)
        hits = (owners == me)[:, :, None] & (ranking[:, :, None] == jnp.arange(MOST))
        rows = jnp.sum(jnp.where(hits, slots[:, :, None], 0), axis=1).reshape(-1)
        my_owners = lax.dynamic_index_in_dim(owners, me, 0, keepdims=False)
        my_ranking = lax.dynamic_index_in_dim(ranking, me, 0, keepdims=False)
        base_terms = jnp.dot(hidden, value_weight, preferred_element_type=jnp.float32)
        base = lax.psum_scatter(base_terms, "tp", scatter_dimension=1, tiled=True)
        downs = lax.all_to_all(down_weights[rows], "dp", 0, 0, tiled=True)
        ups = lax.all_to_all(up_weights[rows], "dp", 0, 0, tiled=True)
        picked = my_owners * MOST + my_ranking
        partial = jnp.einsum(
            "gcd,grd->gcr",
            hidden.reshape(groups, cap, width),
            downs[picked],
            preferred_element_type=jnp.float32,
        )
        low = low_rank_sum(partial.reshape(groups * cap, rank))
        return finish(base, low, ups[picked], counts)

    def narrow(hidden, value_weight, down_weights, up_weights):
        side = math.isqrt(dp_count)
        hot = mine[FLAGS, HOT]
        a = (me // side - hot // side) % side
        b = (me % side - hot % side) % side
        offsets = jnp.stack([a, b]).astype(jnp.int32)
        ends = ((True, 2, (0, 1)), (True, 2, (2, 3)), (False, 2, (0, 1)), (False, 2, (2, 3)))
        rest = tuple((x_first, far, (0, 1, 2, 3)) for x_first in (True, False) for far in (1, 3, 0))
        scalars = (me_row, served, mine)
        first = gather_call(
            functools.partial(extra_kernel, ends), (2,) * 4, 8, scalars, down_weights, up_weights
        )
        moves = ((1, 0), (-1, 0), (0, 1), (0, -1))
        send = lambda values, ways: [shift(v, *way) for v, way in zip(values, ways)]
        fresh = send(first, moves)
        (main_sent,) = gather_call(
            main_kernel, (dp_count,), dp_count, (served,), down_weights, up_weights
        )
        main = lax.all_to_all(main_sent, "dp", 0, 0, tiled=True)
        after, _ = lax.optimization_barrier((served, main_sent))
        later = gather_call(
            functools.partial(extra_kernel, rest),
            (4,) * 6,
            24,
            (me_row, after, mine),
            down_weights,
            up_weights,
        )
        x_plus, x_minus, x_own, y_plus, y_minus, y_own = later
        hidden, _ = lax.optimization_barrier((hidden, after))
        base_terms = jnp.dot(hidden, value_weight, preferred_element_type=jnp.float32)
        base = lax.psum_scatter(base_terms, "tp", scatter_dimension=1, tiled=True)
        fresh = lax.optimization_barrier(fresh)
        got = send(relay(offsets, fresh, (x_plus, x_minus, y_plus, y_minus)), moves)
        got = lax.optimization_barrier(got)
        lines = line(offsets, (x_own, got[0], got[1], y_own, got[2], got[3]))
        x0, x1, x2, x3, y0, y1, y2, y3 = lines
        x_ahead, x_back, y_ahead, y_back = lax.optimization_barrier(
            send((x2, x3, y2, y3), ((0, 1), (0, -1), (1, 0), (-1, 0)))
        )
        x_next, y_next = send(pass_on(offsets, (x_ahead, y_ahead), (x1, y1)), ((0, 1), (1, 0)))
        extra_x = jnp.where(b == 0, x0, jnp.where(b == 3, x_back, x_next))
        extra_y = jnp.where(a == 0, y0, jnp.where(a == 3, y_back, y_next))
        extras = (extra_x, extra_y)
        partial = low_partial(mine, hidden, main, extras, cap, rank)
        own, other = low_rank_rounds(partial)
        t = lax.axis_index("tp")
        where = jnp.stack([t // 2, t % 2]).astype(jnp.int32)
        return combine(where, mine, counts, base, own, other, main, extras, rank)

    return lax.cond(
        mine[FLAGS, FITS] == 1, narrow, wide, hidden, value_weight, down_weights, up_weights
    )


def solution(mesh):
    return jax.shard_map(
        on_device,
        mesh=mesh,
        in_specs=(
            P("dp", "tp"),
            P("tp", None),
            P("dp", None, "tp"),
            P("dp", None, "tp"),
            P(),
            P(),
            P(),
        ),
        out_specs=P("dp", "tp"),
        check_vma=False,
    )
```

```python
import functools
import math

import jax
import jax.numpy as jnp
from jax import lax
from jax.experimental import pallas as pl
from jax.experimental.pallas import tpu as pltpu
from jax.sharding import PartitionSpec as P

ADAPTER_SCALE = 0.5
MAIN = 2
MOST = 6
EXTRA = MOST - MAIN


def low_rank_sum(partial):
    rows, rank = partial.shape
    tp_count = lax.axis_size("tp")
    pieces = lax.all_to_all(partial, "tp", split_axis=0, concat_axis=0, tiled=True)
    mine = jnp.sum(pieces.reshape(tp_count, rows // tp_count, rank), axis=0).astype(jnp.bfloat16)
    return lax.all_gather(mine, "tp", axis=0, tiled=True)


def finish(base, low, ups, counts):
    groups = counts.shape[0]
    cap = base.shape[0] // groups
    delta = jnp.einsum(
        "gcr,grv->gcv", low.reshape(groups, cap, -1), ups, preferred_element_type=jnp.float32
    )
    merged = base.reshape(groups, cap, -1) + ADAPTER_SCALE * delta
    active = jnp.arange(cap)[None, :, None] < counts[:, None, None]
    out = jnp.where(active, merged, jnp.float32(0.0)).astype(jnp.bfloat16)
    return out.reshape(base.shape)


SMEM = pl.BlockSpec(memory_space=pltpu.SMEM)
VMEM = pl.BlockSpec(memory_space=pltpu.VMEM)
HBM = pl.BlockSpec(memory_space=pl.ANY)
LANES = 128
ORDER, PLACE, FLAGS = 0, 1, 2
HOT, FITS = 0, 1


def shift(value, dx, dy):
    side = math.isqrt(lax.axis_size("dp"))
    pairs = [
        (x * side + y, (x + dx) % side * side + (y + dy) % side)
        for x in range(side)
        for y in range(side)
    ]
    return lax.ppermute(value, "dp", pairs)


def index_kernel(me_ref, ids_ref, table_ref, served_ref, mine_ref, owner_ref, rank_ref):
    total = ids_ref.shape[0]
    dp_count = served_ref.shape[0]
    groups = total // dp_count
    chunks = table_ref.shape[0]
    owned = chunks * LANES // dp_count
    me = me_ref[0]
    f32, bf16 = jnp.float32, jnp.bfloat16
    ids = ids_ref[...]
    lane = lax.broadcasted_iota(jnp.int32, (total, LANES), 1)
    found = jnp.zeros((total, LANES), jnp.int32)
    for c in range(chunks):
        found += jnp.where(ids == lane + c * LANES, table_ref[c : c + 1, :], 0)
    stored = jnp.sum(found, axis=1, keepdims=True)
    owner = lax.div(stored, owned)
    slot = stored - owner * owned
    holds = jnp.where(owner == lane, 1.0, 0.0)
    low = lax.broadcasted_iota(jnp.int32, (groups, groups), 0)
    low = jnp.where(low > lax.broadcasted_iota(jnp.int32, (groups, groups), 1), 1.0, 0.0)
    low = low.astype(bf16)
    holds16 = holds.astype(bf16)
    before = jnp.concatenate(
        [
            jnp.dot(low, holds16[r * groups : (r + 1) * groups], preferred_element_type=f32)
            for r in range(dp_count)
        ],
        axis=0,
    )
    ranking = jnp.sum(before * holds, axis=1, keepdims=True).astype(jnp.int32)
    owner_ref[...] = jnp.broadcast_to(owner, (total, LANES))
    rank_ref[...] = jnp.broadcast_to(ranking, (total, LANES))
    block_of = lax.div(lax.broadcasted_iota(jnp.int32, (dp_count, total), 1), groups)
    block = block_of == lax.broadcasted_iota(jnp.int32, (dp_count, total), 0)
    block = jnp.where(block, 1.0, 0.0).astype(bf16)
    loads = jnp.dot(block, holds16, preferred_element_type=f32)
    kept = jnp.where((owner == me) & (ranking == lane), slot, 0).astype(f32).astype(bf16)
    served_ref[...] = jnp.dot(block, kept, preferred_element_type=f32).astype(jnp.int32)
    least = jnp.min(loads, axis=0, keepdims=True)
    row_lane = lax.broadcasted_iota(jnp.int32, (1, LANES), 1)
    hot = jnp.min(jnp.where(least >= MOST, row_lane, LANES), axis=1, keepdims=True)
    spare = jnp.where(row_lane == hot, 0.0, loads)
    most = jnp.max(jnp.max(spare, axis=0, keepdims=True), axis=1, keepdims=True)
    fits = jnp.where(most <= MAIN, 1, 0)
    at = pl.ds(pl.multiple_of(me * groups, groups), groups)
    my_owner = owner_ref[at, :]
    my_rank = rank_ref[at, :]
    late = (my_owner == hot) & (my_rank >= MAIN)
    place = jnp.where(late, dp_count * MAIN + my_rank - MAIN, my_owner * MAIN + my_rank)
    early = jnp.where(late, 0.0, 1.0).astype(bf16)
    ahead = jnp.dot(low, early, preferred_element_type=f32).astype(jnp.int32)
    turn = jnp.where(late, groups - EXTRA + my_rank - MAIN, ahead)
    group_lane = lax.broadcasted_iota(jnp.int32, (groups, LANES), 1)
    group = lax.broadcasted_iota(jnp.int32, (groups, LANES), 0)
    here = turn == group_lane
    mine_ref[...] = jnp.zeros(mine_ref.shape, jnp.int32)
    mine_ref[ORDER : ORDER + 1, :] = jnp.sum(jnp.where(here, group, 0), axis=0, keepdims=True)
    mine_ref[PLACE : PLACE + 1, :] = jnp.sum(jnp.where(here, place, 0), axis=0, keepdims=True)
    mine_ref[FLAGS : FLAGS + 1, :] = jnp.where(
        row_lane == HOT, hot, jnp.where(row_lane == FITS, fits, 0)
    )


def index_tables(me, ids, table, dp_count):
    total = ids.shape[0]
    return pl.pallas_call(
        index_kernel,
        out_shape=(
            jax.ShapeDtypeStruct((dp_count, LANES), jnp.int32),
            jax.ShapeDtypeStruct((8, LANES), jnp.int32),
        ),
        in_specs=[SMEM, VMEM, VMEM],
        out_specs=(VMEM, VMEM),
        scratch_shapes=[pltpu.VMEM((total, LANES), jnp.int32)] * 2,
        compiler_params=pltpu.CompilerParams(vmem_limit_bytes=8 << 20),
    )(me, ids.reshape(total, 1), table.reshape(-1, LANES))


def copy_units(wanted, down, up, up_in, up_out, down_sem, up_sem, out_sem):
    rank = down.shape[1]
    lanes = up.shape[2]
    steps = rank // 16
    waits = []
    ups = []
    for i, (dest, index, rows) in enumerate(wanted):
        for half in range(2):
            n = 2 * i + half
            ups.append(pltpu.make_async_copy(up.at[rows[half]], up_in.at[n], up_sem.at[n]))
            ups[-1].start()
            waits.append(
                pltpu.make_async_copy(
                    down.at[rows[half]], dest.at[index, pl.ds(half * rank, rank)], down_sem.at[n]
                )
            )
            waits[-1].start()
    for i, (dest, index, rows) in enumerate(wanted):
        for half in range(2):
            n = 2 * i + half
            ups[n].wait()
            for part in range(steps):
                at = (half * steps + part) * lanes
                up_out[i, :, at : at + lanes] = up_in[n, part * 16 : part * 16 + 16, :]
        waits.append(
            pltpu.make_async_copy(
                up_out.at[i], dest.at[index, pl.ds(2 * rank, 16)], out_sem.at[i]
            )
        )
        waits[-1].start()
    for copy in waits:
        copy.wait()


def main_kernel(served, down, up, out, *scratch):
    wanted = [(out, p, (served[p, 0], served[p, 1])) for p in range(out.shape[0])]
    copy_units(wanted, down, up, *scratch)


def extra_kernel(lines, me, served, mine, down, up, *refs):
    outs, scratch = refs[: len(lines)], refs[len(lines) :]
    dp_count = served.shape[0]
    side = math.isqrt(dp_count)
    hot = mine[FLAGS, HOT]

    @pl.when(hot == me[0])
    def _():
        hot_x, hot_y = lax.div(hot, side), lax.rem(hot, side)
        wanted = []
        for out, (x_first, a, units) in zip(outs, lines):
            for i, b in enumerate(units):
                dx, dy = (a, b) if x_first else (b, a)
                peer = lax.rem(hot_x + dx, side) * side + lax.rem(hot_y + dy, side)
                first = MAIN if x_first else MAIN + 2
                wanted.append((out, i, (served[peer, first], served[peer, first + 1])))
        copy_units(wanted, down, up, *scratch)


def gather_call(kernel, shapes, count, scalars, down, up):
    _, rank, width = down.shape
    lanes = up.shape[2]
    return pl.pallas_call(
        kernel,
        out_shape=[jax.ShapeDtypeStruct((n, 2 * rank + 16, width), down.dtype) for n in shapes],
        in_specs=[SMEM] * len(scalars) + [HBM, HBM],
        out_specs=[HBM] * len(shapes),
        scratch_shapes=[
            pltpu.VMEM((2 * count, rank, lanes), up.dtype),
            pltpu.VMEM((count, 16, width), up.dtype),
            pltpu.SemaphoreType.DMA((2 * count,)),
            pltpu.SemaphoreType.DMA((2 * count,)),
            pltpu.SemaphoreType.DMA((count,)),
        ],
        compiler_params=pltpu.CompilerParams(vmem_limit_bytes=12 << 20),
        cost_estimate=pl.CostEstimate(
            flops=0, bytes_accessed=count * rank * (width + lanes) * 8, transcendentals=0
        ),
    )(*scalars, down, up)


def vmem_call(kernel, shapes, dtype, scalars, arrays, limit=32):
    return pl.pallas_call(
        kernel,
        out_shape=[jax.ShapeDtypeStruct(shape, dtype) for shape in shapes],
        in_specs=[SMEM] * len(scalars) + [VMEM] * len(arrays),
        out_specs=[VMEM] * len(shapes),
        compiler_params=pltpu.CompilerParams(vmem_limit_bytes=limit << 20),
        cost_estimate=pl.CostEstimate(
            flops=0,
            bytes_accessed=sum(math.prod(shape) for shape in shapes) * 4,
            transcendentals=0,
        ),
    )(*scalars, *arrays)


def move(dst, src):
    rows = src.shape[0]

    def body(i, carry):
        at = pl.ds(pl.multiple_of(i * 16, 16), 16)
        dst[at, :] = src[at, :]
        return carry

    lax.fori_loop(0, rows // 16, body, 0, unroll=3)


def relay_kernel(offsets, *refs):
    fresh, near, outs = refs[:4], refs[4:8], refs[8:]
    for i in range(4):
        at = offsets[i // 2]
        close = 1 if i % 2 == 0 else 3
        for source, when in ((near[i], at != close), (fresh[i], at == close)):

            @pl.when(when)
            def _(source=source, out=outs[i]):
                for u in range(2):
                    move(out.at[u], source.at[u])


def line_kernel(offsets, *refs):
    outs = refs[10:]
    for h in range(2):
        own, plus_a, minus_a, plus_b, minus_b = refs[5 * h : 5 * h + 5]
        out = outs[4 * h : 4 * h + 4]
        at = offsets[h]
        low, high = own.at[pl.ds(0, 2)], own.at[pl.ds(2, 2)]
        picks = ((low, high), (plus_a, plus_b), (plus_a, minus_a), (minus_a, minus_b))
        for offset, (first, second) in enumerate(picks):

            @pl.when(at == offset)
            def _(first=first, second=second, out=out):
                for u in range(2):
                    move(out[u], first.at[u])
                    move(out[2 + u], second.at[u])


def pass_kernel(offsets, *refs):
    for h in range(2):
        at = offsets[1 - h]
        for source, when in ((refs[2 + h], at != 1), (refs[h], at == 1)):

            @pl.when(when)
            def _(source=source, out=refs[4 + h]):
                move(out, source)


def pick_kernel(offsets, *refs):
    for h in range(2):
        at = offsets[1 - h]
        own, back, ahead = refs[3 * h : 3 * h + 3]
        for source, when in ((own, at == 0), (back, at == 3), (ahead, (at == 1) | (at == 2))):

            @pl.when(when)
            def _(source=source, out=refs[6 + h]):
                move(out, source)


def paired(hidden, mine, i, pairs, cap, first, second):
    spots = [pl.multiple_of(mine[ORDER, j] * cap, cap) for j in (i, i + pairs)]
    rows = jnp.concatenate([hidden[pl.ds(spot, cap), :] for spot in spots], axis=0)
    product = lax.dot_general(
        rows,
        jnp.concatenate([first, second], axis=0),
        (((1,), (1,)), ((), ())),
        preferred_element_type=jnp.float32,
    )
    lane = lax.broadcasted_iota(jnp.int32, (cap, product.shape[1]), 1)
    return jnp.where(lane < first.shape[0], product[:cap], product[cap:])


def low_main_kernel(cap, mine, hidden, main, out):
    rank = out.shape[1] // 2
    pairs = out.shape[0] // cap

    def weights(j):
        place = mine[PLACE, j]
        unit = lax.div(place, 2)
        return main[unit, pl.ds(pl.multiple_of((place - 2 * unit) * rank, rank), rank), :]

    def body(i, carry):
        at = pl.ds(pl.multiple_of(i * cap, cap), cap)
        out[at, :] = paired(hidden, mine, i, pairs, cap, weights(i), weights(i + pairs))
        return carry

    lax.fori_loop(0, pairs, body, 0, unroll=2)


def low_extra_kernel(first, cap, mine, hidden, *refs):
    extras, out = refs[:-1], refs[-1]
    rank = out.shape[1] // 2
    for i in range(2):
        spots = [pl.multiple_of(mine[ORDER, first + 2 * u + i] * cap, cap) for u in range(2)]
        rows = jnp.concatenate([hidden[pl.ds(spot, cap), :] for spot in spots], axis=0)
        part = slice(i * rank, (i + 1) * rank)
        product = lax.dot_general(
            rows,
            jnp.concatenate([extras[0][part, :], extras[1][part, :]], axis=0),
            (((1,), (1,)), ((), ())),
            preferred_element_type=jnp.float32,
        )
        lane = lax.broadcasted_iota(jnp.int32, (cap, 2 * rank), 1)
        out[i * cap : (i + 1) * cap, :] = jnp.where(lane < rank, product[:cap], product[cap:])


def low_partial(kernel, pairs, cap, rank, mine, hidden, weights):
    return pl.pallas_call(
        kernel,
        out_shape=jax.ShapeDtypeStruct((pairs * cap, 2 * rank), jnp.float32),
        in_specs=[SMEM] + [VMEM] * (1 + len(weights)),
        out_specs=VMEM,
        compiler_params=pltpu.CompilerParams(vmem_limit_bytes=24 << 20),
        cost_estimate=pl.CostEstimate(
            flops=pairs * cap * rank * 4 * hidden.shape[1],
            bytes_accessed=sum(w.size for w in weights) * 2,
            transcendentals=0,
        ),
    )(mine, hidden, *weights)


def low_rank_rounds(partial):
    tp_count = lax.axis_size("tp")
    chips = tp_count // 2
    t = lax.axis_index("tp")
    z, core = t // 2, t % 2
    half = partial.shape[0] // 2
    piece = half // chips
    swap = [(i, i ^ 1) for i in range(tp_count)]
    turn = lambda d: [(i, (i + 2 * d) % tp_count) for i in range(tp_count)]
    cut = lambda array, start, size: lax.dynamic_slice_in_dim(array, start, size, 0)
    total = cut(partial, core * half, half) + lax.ppermute(
        cut(partial, (1 - core) * half, half), "tp", swap
    )
    pieces = [
        lax.ppermute(cut(total, (z + d) % chips * piece, piece), "tp", turn(d))
        for d in range(1, chips)
    ]
    summed = (cut(total, z * piece, piece) + sum(pieces)).astype(jnp.bfloat16)
    own = jnp.stack([summed] + [lax.ppermute(summed, "tp", turn(d)) for d in range(1, chips)])
    return own, lax.ppermute(own, "tp", swap)


def low_rank_doubling(partial):
    tp_count = lax.axis_size("tp")
    last = tp_count // 2 - 1
    z_of = lambda i: i // 2
    for partner in (
        lambda i: i ^ 1,
        lambda i: (z_of(i) ^ 1) * 2 + i % 2,
        lambda i: (last - z_of(i)) * 2 + i % 2,
    ):
        partial += lax.ppermute(partial, "tp", [(i, partner(i)) for i in range(tp_count)])
    return partial


def blend(base, out, counts, mine, j, both, ups, cap):
    rank = both.shape[1] // 2
    lane = lax.broadcasted_iota(jnp.int32, both.shape, 1)
    none = jnp.zeros_like(both)
    left = jnp.concatenate(
        [jnp.where(lane < rank, both, none), jnp.where(lane < rank, none, both)], axis=0
    )
    delta = jnp.dot(left, jnp.concatenate(ups, axis=0), preferred_element_type=jnp.float32)
    rows = lax.broadcasted_iota(jnp.int32, (cap, base.shape[1]), 0)
    for n in range(2):
        g = mine[ORDER, j[n]]
        here = pl.ds(pl.multiple_of(g * cap, cap), cap)
        merged = base[here, :] + ADAPTER_SCALE * delta[n * cap : (n + 1) * cap]
        out(n, here, jnp.where(rows < counts[g], merged, 0.0).astype(jnp.bfloat16))


def out_main_kernel(where, mine, counts, base, own, other, main, out, low):
    groups = counts.shape[0]
    cap = base.shape[0] // groups
    chips, piece, rank = own.shape[0], own.shape[1], own.shape[2] // 2
    lanes = base.shape[1]
    z, core = where[0], where[1]
    steps = rank // 16
    pairs = low.shape[0] // cap
    for d in range(chips):
        quarter = lax.rem(z - d + chips, chips)
        for ref, half in ((own, core), (other, 1 - core)):
            at = pl.multiple_of((half * chips + quarter) * piece, 16)
            low[pl.ds(at, piece), :] = ref[d]

    def up(j):
        place = mine[PLACE, j]
        unit = lax.div(place, 2)
        at = (place - 2 * unit) * steps * lanes
        return [
            main[unit, :, pl.ds(pl.multiple_of(at + part * lanes, lanes), lanes)]
            for part in range(steps)
        ]

    def store(n, here, value):
        out[here, :] = value

    def body(i, carry):
        both = low[pl.ds(pl.multiple_of(i * cap, cap), cap), :]
        spots = (i, i + pairs)
        blend(base, store, counts, mine, spots, both, up(i) + up(i + pairs), cap)
        return carry

    lax.fori_loop(0, pairs, body, 0, unroll=2)


def out_extra_kernel(mine, counts, base, low, first_pack, second_pack, _, out, blocks, sems):
    groups = counts.shape[0]
    cap = base.shape[0] // groups
    rank = low.shape[1] // 2
    lanes = base.shape[1]
    steps = rank // 16
    first = groups - EXTRA
    copies = []
    for i in range(2):
        both = low[i * cap : (i + 1) * cap, :].astype(jnp.bfloat16)
        ups = [
            pack[:, (i * steps + part) * lanes : (i * steps + part + 1) * lanes]
            for pack in (first_pack, second_pack)
            for part in range(steps)
        ]

        def store(n, here, value, i=i):
            blocks[2 * i + n] = value
            copy = pltpu.make_async_copy(
                blocks.at[2 * i + n], out.at[here, :], sems.at[2 * i + n]
            )
            copy.start()
            copies.append(copy)

        blend(base, store, counts, mine, (first + i, first + 2 + i), both, ups, cap)
    for copy in copies:
        copy.wait()


def whole(array):
    return pl.BlockSpec(array.shape, lambda i: (0,) * array.ndim)


def combine_main(where, mine, counts, base, own, other, main, rank):
    packs = pl.BlockSpec((main.shape[0], 16, main.shape[2]), lambda i: (0, rank // 8, 0))
    return pl.pallas_call(
        out_main_kernel,
        grid=(1,),
        out_shape=jax.ShapeDtypeStruct(base.shape, jnp.bfloat16),
        in_specs=[SMEM, SMEM, SMEM, whole(base), whole(own), whole(other), packs],
        out_specs=whole(base),
        scratch_shapes=[
            pltpu.VMEM((2 * own.shape[0] * own.shape[1], own.shape[2]), jnp.bfloat16)
        ],
        compiler_params=pltpu.CompilerParams(vmem_limit_bytes=12 << 20),
        cost_estimate=pl.CostEstimate(
            flops=base.size * rank * 2, bytes_accessed=base.size * 8, transcendentals=0
        ),
    )(where, mine, counts, base, own, other, main)


def combine_extra(mine, counts, base, low, extras, out, rank):
    pack = pl.BlockSpec((16, extras[0].shape[1]), lambda i: (rank // 8, 0))
    cap = base.shape[0] // counts.shape[0]
    return pl.pallas_call(
        out_extra_kernel,
        grid=(1,),
        out_shape=jax.ShapeDtypeStruct(out.shape, out.dtype),
        in_specs=[SMEM, SMEM, whole(base), whole(low), pack, pack, HBM],
        out_specs=HBM,
        input_output_aliases={6: 0},
        scratch_shapes=[
            pltpu.VMEM((EXTRA, cap, base.shape[1]), jnp.bfloat16),
            pltpu.SemaphoreType.DMA((EXTRA,)),
        ],
        compiler_params=pltpu.CompilerParams(vmem_limit_bytes=8 << 20),
        cost_estimate=pl.CostEstimate(
            flops=base.size * rank // 4, bytes_accessed=base.size * 4, transcendentals=0
        ),
    )(mine, counts, base, low, *extras, out)


def on_device(
    hidden,
    value_weight,
    down_weights,
    up_weights,
    group_adapter_id,
    adapter_storage_row,
    group_live_count,
):
    dp_count = lax.axis_size("dp")
    me = lax.axis_index("dp")
    owned, rank, width = down_weights.shape
    groups = group_adapter_id.shape[0] // dp_count
    cap = hidden.shape[0] // groups
    me_row = me.astype(jnp.int32).reshape(1)
    served, mine = index_tables(me_row, group_adapter_id, adapter_storage_row, dp_count)
    counts = lax.dynamic_slice_in_dim(group_live_count, me * groups, groups)

    def wide(hidden, value_weight, down_weights, up_weights):
        stored = adapter_storage_row[group_adapter_id]
        owners = (stored // owned).reshape(dp_count, groups)
        slots = (stored % owned).reshape(dp_count, groups)
        same = owners[:, :, None] == owners[:, None, :]
        earlier = jnp.arange(groups)[None, None, :] < jnp.arange(groups)[None, :, None]
        ranking = jnp.sum(same & earlier, axis=2)
        hits = (owners == me)[:, :, None] & (ranking[:, :, None] == jnp.arange(MOST))
        rows = jnp.sum(jnp.where(hits, slots[:, :, None], 0), axis=1).reshape(-1)
        my_owners = lax.dynamic_index_in_dim(owners, me, 0, keepdims=False)
        my_ranking = lax.dynamic_index_in_dim(ranking, me, 0, keepdims=False)
        base_terms = jnp.dot(hidden, value_weight, preferred_element_type=jnp.float32)
        base = lax.psum_scatter(base_terms, "tp", scatter_dimension=1, tiled=True)
        downs = lax.all_to_all(down_weights[rows], "dp", 0, 0, tiled=True)
        ups = lax.all_to_all(up_weights[rows], "dp", 0, 0, tiled=True)
        picked = my_owners * MOST + my_ranking
        partial = jnp.einsum(
            "gcd,grd->gcr",
            hidden.reshape(groups, cap, width),
            downs[picked],
            preferred_element_type=jnp.float32,
        )
        low = low_rank_sum(partial.reshape(groups * cap, rank))
        return finish(base, low, ups[picked], counts)

    def narrow(hidden, value_weight, down_weights, up_weights):
        side = math.isqrt(dp_count)
        hot = mine[FLAGS, HOT]
        a = (me // side - hot // side) % side
        b = (me % side - hot % side) % side
        offsets = jnp.stack([a, b]).astype(jnp.int32)
        trees = (True, False)
        soon = [(tree, 2, part) for tree in trees for part in ((0, 1), (2, 3))]
        soon += [(tree, near, (2, 3)) for tree in trees for near in (1, 3)]
        late = [(tree, near, (0, 1)) for tree in trees for near in (1, 3)]
        late += [(tree, 0, (0, 1, 2, 3)) for tree in trees]
        moves = ((1, 0), (-1, 0), (0, 1), (0, -1))
        turned = ((0, 1), (0, -1), (1, 0), (-1, 0))
        send = lambda values, ways: [shift(v, *way) for v, way in zip(values, ways)]
        barrier = lax.optimization_barrier
        scalars = (me_row, served, mine)
        gathered = gather_call(
            functools.partial(extra_kernel, soon), (2,) * 8, 16, scalars, down_weights, up_weights
        )
        fresh = send(gathered[:4], moves)
        near_b = send(gathered[4:], moves)
        later_served, _ = barrier((served, gathered))
        later = gather_call(
            functools.partial(extra_kernel, late),
            (2,) * 4 + (4,) * 2,
            16,
            (me_row, later_served, mine),
            down_weights,
            up_weights,
        )
        main_served, _ = barrier((served, later))
        (main_sent,) = gather_call(
            main_kernel, (dp_count,), dp_count, (main_served,), down_weights, up_weights
        )
        fresh, near, main_sent = barrier((fresh, later[:4], main_sent))
        unit = main_sent.shape[1:]
        two = (2,) + unit
        relayed = vmem_call(
            relay_kernel, (two,) * 4, main_sent.dtype, (offsets,), (*fresh, *near)
        )
        main_sent, relayed = barrier((main_sent, relayed))
        near_a = send(relayed, moves)
        main = lax.all_to_all(main_sent, "dp", 0, 0, tiled=True)
        base_hidden, _ = barrier((hidden, relayed))
        base_terms = jnp.dot(base_hidden, value_weight, preferred_element_type=jnp.float32)
        base = lax.psum_scatter(base_terms, "tp", scatter_dimension=1, tiled=True)
        near_a, near_b, base_terms = barrier((near_a, near_b, base_terms))
        tree_arrays = [
            (later[4 + h], near_a[2 * h], near_a[2 * h + 1], near_b[2 * h], near_b[2 * h + 1])
            for h in range(2)
        ]
        lines = vmem_call(
            line_kernel,
            (unit,) * 8,
            main_sent.dtype,
            (offsets,),
            tree_arrays[0] + tree_arrays[1],
        )
        x0, x1, x2, x3, y0, y1, y2, y3 = lines
        x_ahead, x_back, y_ahead, y_back = barrier(send((x2, x3, y2, y3), turned))
        passed = vmem_call(
            pass_kernel,
            (unit,) * 2,
            main_sent.dtype,
            (offsets,),
            (x_ahead, y_ahead, x1, y1),
        )
        passed, main = barrier((passed, main))
        x_next, y_next = send(passed, (turned[0], turned[2]))
        pairs = (groups - EXTRA) // 2
        partial = low_partial(
            functools.partial(low_main_kernel, cap), pairs, cap, rank, mine, hidden, (main,)
        )
        own, other = low_rank_rounds(partial)
        extras = vmem_call(
            pick_kernel,
            (unit,) * 2,
            main_sent.dtype,
            (offsets,),
            (x0, x_back, x_next, y0, y_back, y_next),
        )
        extra_partial = low_partial(
            functools.partial(low_extra_kernel, groups - EXTRA, cap),
            EXTRA // 2,
            cap,
            rank,
            mine,
            hidden,
            extras,
        )
        extra_low = low_rank_doubling(extra_partial)
        t = lax.axis_index("tp")
        where = jnp.stack([t // 2, t % 2]).astype(jnp.int32)
        out = combine_main(where, mine, counts, base, own, other, main, rank)
        return combine_extra(mine, counts, base, extra_low, extras, out, rank)

    return lax.cond(
        mine[FLAGS, FITS] == 1, narrow, wide, hidden, value_weight, down_weights, up_weights
    )


def solution(mesh):
    return jax.shard_map(
        on_device,
        mesh=mesh,
        in_specs=(
            P("dp", "tp"),
            P("tp", None),
            P("dp", None, "tp"),
            P("dp", None, "tp"),
            P(),
            P(),
            P(),
        ),
        out_specs=P("dp", "tp"),
        check_vma=False,
    )
```

```python
import functools
import math

import jax
import jax.numpy as jnp
from jax import lax
from jax.experimental import pallas as pl
from jax.experimental.pallas import tpu as pltpu
from jax.sharding import PartitionSpec as P

ADAPTER_SCALE = 0.5
MAIN = 2
MOST = 6
EXTRA = MOST - MAIN


def low_rank_sum(partial):
    rows, rank = partial.shape
    tp_count = lax.axis_size("tp")
    pieces = lax.all_to_all(partial, "tp", split_axis=0, concat_axis=0, tiled=True)
    mine = jnp.sum(pieces.reshape(tp_count, rows // tp_count, rank), axis=0).astype(jnp.bfloat16)
    return lax.all_gather(mine, "tp", axis=0, tiled=True)


def finish(base, low, ups, counts):
    groups = counts.shape[0]
    cap = base.shape[0] // groups
    delta = jnp.einsum(
        "gcr,grv->gcv", low.reshape(groups, cap, -1), ups, preferred_element_type=jnp.float32
    )
    merged = base.reshape(groups, cap, -1) + ADAPTER_SCALE * delta
    active = jnp.arange(cap)[None, :, None] < counts[:, None, None]
    out = jnp.where(active, merged, jnp.float32(0.0)).astype(jnp.bfloat16)
    return out.reshape(base.shape)


SMEM = pl.BlockSpec(memory_space=pltpu.SMEM)
VMEM = pl.BlockSpec(memory_space=pltpu.VMEM)
HBM = pl.BlockSpec(memory_space=pltpu.HBM)
LANES = 128
ORDER, PLACE, FLAGS = 0, 1, 2
HOT, FITS = 0, 1


def shift(value, dx, dy):
    side = math.isqrt(lax.axis_size("dp"))
    pairs = [
        (x * side + y, (x + dx) % side * side + (y + dy) % side)
        for x in range(side)
        for y in range(side)
    ]
    return lax.ppermute(value, "dp", pairs)


def index_kernel(me_ref, ids_ref, table_ref, served_ref, mine_ref, owner_ref, rank_ref):
    total = ids_ref.shape[0]
    dp_count = served_ref.shape[0]
    groups = total // dp_count
    chunks = table_ref.shape[0]
    owned = chunks * LANES // dp_count
    me = me_ref[0]
    f32, bf16 = jnp.float32, jnp.bfloat16
    ids = ids_ref[...]
    lane = lax.broadcasted_iota(jnp.int32, (total, LANES), 1)
    found = jnp.zeros((total, LANES), jnp.int32)
    for c in range(chunks):
        found += jnp.where(ids == lane + c * LANES, table_ref[c : c + 1, :], 0)
    stored = jnp.sum(found, axis=1, keepdims=True)
    owner = lax.div(stored, owned)
    slot = stored - owner * owned
    holds = jnp.where(owner == lane, 1.0, 0.0)
    low = lax.broadcasted_iota(jnp.int32, (groups, groups), 0)
    low = jnp.where(low > lax.broadcasted_iota(jnp.int32, (groups, groups), 1), 1.0, 0.0)
    low = low.astype(bf16)
    holds16 = holds.astype(bf16)
    before = jnp.concatenate(
        [
            jnp.dot(low, holds16[r * groups : (r + 1) * groups], preferred_element_type=f32)
            for r in range(dp_count)
        ],
        axis=0,
    )
    ranking = jnp.sum(before * holds, axis=1, keepdims=True).astype(jnp.int32)
    owner_ref[...] = jnp.broadcast_to(owner, (total, LANES))
    rank_ref[...] = jnp.broadcast_to(ranking, (total, LANES))
    block_of = lax.div(lax.broadcasted_iota(jnp.int32, (dp_count, total), 1), groups)
    block = block_of == lax.broadcasted_iota(jnp.int32, (dp_count, total), 0)
    block = jnp.where(block, 1.0, 0.0).astype(bf16)
    loads = jnp.dot(block, holds16, preferred_element_type=f32)
    kept = jnp.where((owner == me) & (ranking == lane), slot, 0).astype(f32).astype(bf16)
    served_ref[...] = jnp.dot(block, kept, preferred_element_type=f32).astype(jnp.int32)
    least = jnp.min(loads, axis=0, keepdims=True)
    row_lane = lax.broadcasted_iota(jnp.int32, (1, LANES), 1)
    hot = jnp.min(jnp.where(least >= MOST, row_lane, LANES), axis=1, keepdims=True)
    spare = jnp.where(row_lane == hot, 0.0, loads)
    most = jnp.max(jnp.max(spare, axis=0, keepdims=True), axis=1, keepdims=True)
    fits = jnp.where(most <= MAIN, 1, 0)
    at = pl.ds(pl.multiple_of(me * groups, groups), groups)
    my_owner = owner_ref[at, :]
    my_rank = rank_ref[at, :]
    late = (my_owner == hot) & (my_rank >= MAIN)
    place = jnp.where(late, dp_count * MAIN + my_rank - MAIN, my_owner * MAIN + my_rank)
    early = jnp.where(late, 0.0, 1.0).astype(bf16)
    ahead = jnp.dot(low, early, preferred_element_type=f32).astype(jnp.int32)
    turn = jnp.where(late, groups - EXTRA + my_rank - MAIN, ahead)
    group_lane = lax.broadcasted_iota(jnp.int32, (groups, LANES), 1)
    group = lax.broadcasted_iota(jnp.int32, (groups, LANES), 0)
    here = turn == group_lane
    mine_ref[...] = jnp.zeros(mine_ref.shape, jnp.int32)
    mine_ref[ORDER : ORDER + 1, :] = jnp.sum(jnp.where(here, group, 0), axis=0, keepdims=True)
    mine_ref[PLACE : PLACE + 1, :] = jnp.sum(jnp.where(here, place, 0), axis=0, keepdims=True)
    mine_ref[FLAGS : FLAGS + 1, :] = jnp.where(
        row_lane == HOT, hot, jnp.where(row_lane == FITS, fits, 0)
    )


def index_tables(me, ids, table, dp_count):
    total = ids.shape[0]
    return pl.pallas_call(
        index_kernel,
        out_shape=(
            jax.ShapeDtypeStruct((dp_count, LANES), jnp.int32),
            jax.ShapeDtypeStruct((8, LANES), jnp.int32),
        ),
        in_specs=[SMEM, VMEM, VMEM],
        out_specs=(VMEM, VMEM),
        scratch_shapes=[pltpu.VMEM((total, LANES), jnp.int32)] * 2,
        compiler_params=pltpu.CompilerParams(vmem_limit_bytes=8 << 20),
    )(me, ids.reshape(total, 1), table.reshape(-1, LANES))


def copy_units(wanted, down, up, up_in, down_sem, up_sem):
    rank = down.shape[1]
    lanes = up.shape[2]
    steps = rank // 16
    downs, ups = [], []
    for i, (dest, index, rows) in enumerate(wanted):
        for half in range(2):
            n = 2 * i + half
            ups.append(pltpu.make_async_copy(up.at[rows[half]], up_in.at[n], up_sem.at[n]))
            ups[-1].start()
            downs.append(
                pltpu.make_async_copy(
                    down.at[rows[half]], dest.at[index, pl.ds(half * rank, rank)], down_sem.at[n]
                )
            )
            downs[-1].start()
    for i, (dest, index, rows) in enumerate(wanted):
        for half in range(2):
            n = 2 * i + half
            ups[n].wait()
            for part in range(steps):
                at = (half * steps + part) * lanes
                dest[index, 2 * rank : 2 * rank + 16, at : at + lanes] = up_in[
                    n, part * 16 : part * 16 + 16, :
                ]
    for copy in downs:
        copy.wait()


def main_kernel(served, down, up, out, *scratch):
    wanted = [(out, p, (served[p, 0], served[p, 1])) for p in range(out.shape[0])]
    copy_units(wanted, down, up, *scratch)


def extra_kernel(lines, me, served, mine, down, up, *refs):
    outs, scratch = refs[: len(lines)], refs[len(lines) :]
    dp_count = served.shape[0]
    side = math.isqrt(dp_count)
    hot = mine[FLAGS, HOT]

    @pl.when(hot == me[0])
    def _():
        hot_x, hot_y = lax.div(hot, side), lax.rem(hot, side)
        wanted = []
        for out, (x_first, units) in zip(outs, lines):
            for i, (a, b) in enumerate(units):
                dx, dy = (a, b) if x_first else (b, a)
                peer = lax.rem(hot_x + dx, side) * side + lax.rem(hot_y + dy, side)
                first = MAIN if x_first else MAIN + 2
                wanted.append((out, i, (served[peer, first], served[peer, first + 1])))
        copy_units(wanted, down, up, *scratch)


def gather_call(kernel, shapes, count, scalars, down, up):
    _, rank, width = down.shape
    lanes = up.shape[2]
    return pl.pallas_call(
        kernel,
        out_shape=[jax.ShapeDtypeStruct((n, 2 * rank + 16, width), down.dtype) for n in shapes],
        in_specs=[SMEM] * len(scalars) + [HBM, HBM],
        out_specs=[VMEM] * len(shapes),
        scratch_shapes=[
            pltpu.VMEM((2 * count, rank, lanes), up.dtype),
            pltpu.SemaphoreType.DMA((2 * count,)),
            pltpu.SemaphoreType.DMA((2 * count,)),
        ],
        compiler_params=pltpu.CompilerParams(vmem_limit_bytes=8 << 20),
        cost_estimate=pl.CostEstimate(
            flops=0, bytes_accessed=count * rank * (width + lanes) * 8, transcendentals=0
        ),
    )(*scalars, down, up)


def vmem_call(kernel, shapes, dtype, scalars, arrays, limit=10):
    return pl.pallas_call(
        kernel,
        out_shape=[jax.ShapeDtypeStruct(shape, dtype) for shape in shapes],
        in_specs=[SMEM] * len(scalars) + [VMEM] * len(arrays),
        out_specs=[VMEM] * len(shapes),
        compiler_params=pltpu.CompilerParams(vmem_limit_bytes=limit << 20),
        cost_estimate=pl.CostEstimate(
            flops=0,
            bytes_accessed=sum(math.prod(shape) for shape in shapes) * 4,
            transcendentals=0,
        ),
    )(*scalars, *arrays)


def move(dst, src):
    rows = src.shape[0]

    def body(i, carry):
        at = pl.ds(pl.multiple_of(i * 16, 16), 16)
        dst[at, :] = src[at, :]
        return carry

    lax.fori_loop(0, rows // 16, body, 0, unroll=3)


def relay_kernel(offsets, *refs):
    fresh, near, outs = refs[:4], refs[4:8], refs[8:]
    for i in range(4):
        at = offsets[i // 2]
        close = 1 if i % 2 == 0 else 3
        for source, when in ((near[i], at != close), (fresh[i], at == close)):

            @pl.when(when)
            def _(source=source, out=outs[i]):
                for u in range(2):
                    move(out.at[u], source.at[u])


def line_kernel(offsets, *refs):
    outs = refs[10:]
    for h in range(2):
        own, plus_a, minus_a, plus_b, minus_b = refs[5 * h : 5 * h + 5]
        out = outs[4 * h : 4 * h + 4]
        at = offsets[h]
        low, high = own.at[pl.ds(0, 2)], own.at[pl.ds(2, 2)]
        plus_b, minus_b = plus_b.at[pl.ds(2, 2)], minus_b.at[pl.ds(2, 2)]
        picks = ((low, high), (plus_a, plus_b), (plus_a, minus_a), (minus_a, minus_b))
        for offset, (first, second) in enumerate(picks):

            @pl.when(at == offset)
            def _(first=first, second=second, out=out):
                for u in range(2):
                    move(out[u], first.at[u])
                    move(out[2 + u], second.at[u])


def pass_kernel(offsets, *refs):
    for h in range(2):
        at = offsets[1 - h]
        for source, when in ((refs[2 + h], at != 1), (refs[h], at == 1)):

            @pl.when(when)
            def _(source=source, out=refs[4 + h]):
                move(out, source)


def pick_kernel(offsets, *refs):
    for h in range(2):
        at = offsets[1 - h]
        own, back, ahead = refs[3 * h : 3 * h + 3]
        for source, when in ((own, at == 0), (back, at == 3), (ahead, (at == 1) | (at == 2))):

            @pl.when(when)
            def _(source=source, out=refs[6 + h]):
                move(out, source)


def paired(hidden, mine, i, pairs, cap, first, second):
    spots = [pl.multiple_of(mine[ORDER, j] * cap, cap) for j in (i, i + pairs)]
    rows = jnp.concatenate([hidden[pl.ds(spot, cap), :] for spot in spots], axis=0)
    product = lax.dot_general(
        rows,
        jnp.concatenate([first, second], axis=0),
        (((1,), (1,)), ((), ())),
        preferred_element_type=jnp.float32,
    )
    lane = lax.broadcasted_iota(jnp.int32, (cap, product.shape[1]), 1)
    return jnp.where(lane < first.shape[0], product[:cap], product[cap:])


def low_main_kernel(cap, mine, hidden, main, out):
    rank = out.shape[1] // 2
    pairs = out.shape[0] // cap

    def weights(j):
        place = mine[PLACE, j]
        unit = lax.div(place, 2)
        return main[unit, pl.ds(pl.multiple_of((place - 2 * unit) * rank, rank), rank), :]

    def body(i, carry):
        at = pl.ds(pl.multiple_of(i * cap, cap), cap)
        out[at, :] = paired(hidden, mine, i, pairs, cap, weights(i), weights(i + pairs))
        return carry

    lax.fori_loop(0, pairs, body, 0, unroll=2)


def low_extra_kernel(first, cap, mine, hidden, *refs):
    extras, out = refs[:-1], refs[-1]
    rank = out.shape[1] // 2
    for i in range(2):
        spots = [pl.multiple_of(mine[ORDER, first + 2 * u + i] * cap, cap) for u in range(2)]
        rows = jnp.concatenate([hidden[pl.ds(spot, cap), :] for spot in spots], axis=0)
        part = slice(i * rank, (i + 1) * rank)
        product = lax.dot_general(
            rows,
            jnp.concatenate([extras[0][part, :], extras[1][part, :]], axis=0),
            (((1,), (1,)), ((), ())),
            preferred_element_type=jnp.float32,
        )
        lane = lax.broadcasted_iota(jnp.int32, (cap, 2 * rank), 1)
        out[i * cap : (i + 1) * cap, :] = jnp.where(lane < rank, product[:cap], product[cap:])


def low_partial(kernel, pairs, cap, rank, mine, hidden, weights):
    return pl.pallas_call(
        kernel,
        out_shape=jax.ShapeDtypeStruct((pairs * cap, 2 * rank), jnp.float32),
        in_specs=[SMEM] + [VMEM] * (1 + len(weights)),
        out_specs=VMEM,
        compiler_params=pltpu.CompilerParams(vmem_limit_bytes=10 << 20),
        cost_estimate=pl.CostEstimate(
            flops=pairs * cap * rank * 4 * hidden.shape[1],
            bytes_accessed=sum(w.size for w in weights) * 2,
            transcendentals=0,
        ),
    )(mine, hidden, *weights)


def low_rank_rounds(partial):
    tp_count = lax.axis_size("tp")
    chips = tp_count // 2
    t = lax.axis_index("tp")
    z, core = t // 2, t % 2
    half = partial.shape[0] // 2
    piece = half // chips
    swap = [(i, i ^ 1) for i in range(tp_count)]
    turn = lambda d: [(i, (i + 2 * d) % tp_count) for i in range(tp_count)]
    cut = lambda array, start, size: lax.dynamic_slice_in_dim(array, start, size, 0)
    total = cut(partial, core * half, half) + lax.ppermute(
        cut(partial, (1 - core) * half, half), "tp", swap
    )
    pieces = [
        lax.ppermute(cut(total, (z + d) % chips * piece, piece), "tp", turn(d))
        for d in range(1, chips)
    ]
    summed = (cut(total, z * piece, piece) + sum(pieces)).astype(jnp.bfloat16)
    own = jnp.stack([summed] + [lax.ppermute(summed, "tp", turn(d)) for d in range(1, chips)])
    return own, lax.ppermute(own, "tp", swap)


def low_rank_doubling(partial):
    tp_count = lax.axis_size("tp")
    last = tp_count // 2 - 1
    z_of = lambda i: i // 2
    for partner in (
        lambda i: i ^ 1,
        lambda i: (z_of(i) ^ 1) * 2 + i % 2,
        lambda i: (last - z_of(i)) * 2 + i % 2,
    ):
        partial += lax.ppermute(partial, "tp", [(i, partner(i)) for i in range(tp_count)])
    return partial


def blend(base, out, counts, mine, j, both, ups, cap):
    rank = both.shape[1] // 2
    lane = lax.broadcasted_iota(jnp.int32, both.shape, 1)
    none = jnp.zeros_like(both)
    left = jnp.concatenate(
        [jnp.where(lane < rank, both, none), jnp.where(lane < rank, none, both)], axis=0
    )
    delta = jnp.dot(left, jnp.concatenate(ups, axis=0), preferred_element_type=jnp.float32)
    rows = lax.broadcasted_iota(jnp.int32, (cap, base.shape[1]), 0)
    for n in range(2):
        g = mine[ORDER, j[n]]
        here = pl.ds(pl.multiple_of(g * cap, cap), cap)
        merged = base[here, :] + ADAPTER_SCALE * delta[n * cap : (n + 1) * cap]
        out(n, here, jnp.where(rows < counts[g], merged, 0.0).astype(jnp.bfloat16))


def out_main_kernel(where, mine, counts, base, own, other, main, out, low):
    groups = counts.shape[0]
    cap = base.shape[0] // groups
    chips, piece, rank = own.shape[0], own.shape[1], own.shape[2] // 2
    lanes = base.shape[1]
    z, core = where[0], where[1]
    steps = rank // 16
    pairs = low.shape[0] // cap
    for d in range(chips):
        quarter = lax.rem(z - d + chips, chips)
        for ref, half in ((own, core), (other, 1 - core)):
            at = pl.multiple_of((half * chips + quarter) * piece, 16)
            low[pl.ds(at, piece), :] = ref[d]

    def up(j):
        place = mine[PLACE, j]
        unit = lax.div(place, 2)
        at = (place - 2 * unit) * steps * lanes
        return [
            main[unit, :, pl.ds(pl.multiple_of(at + part * lanes, lanes), lanes)]
            for part in range(steps)
        ]

    def store(n, here, value):
        out[here, :] = value

    def body(i, carry):
        both = low[pl.ds(pl.multiple_of(i * cap, cap), cap), :]
        spots = (i, i + pairs)
        blend(base, store, counts, mine, spots, both, up(i) + up(i + pairs), cap)
        return carry

    lax.fori_loop(0, pairs, body, 0, unroll=2)


def out_extra_kernel(mine, counts, base, low, first_pack, second_pack, _, out, blocks, sems):
    groups = counts.shape[0]
    cap = base.shape[0] // groups
    rank = low.shape[1] // 2
    lanes = base.shape[1]
    steps = rank // 16
    first = groups - EXTRA
    copies = []
    for i in range(2):
        both = low[i * cap : (i + 1) * cap, :].astype(jnp.bfloat16)
        ups = [
            pack[:, (i * steps + part) * lanes : (i * steps + part + 1) * lanes]
            for pack in (first_pack, second_pack)
            for part in range(steps)
        ]

        def store(n, here, value, i=i):
            blocks[2 * i + n] = value
            copy = pltpu.make_async_copy(
                blocks.at[2 * i + n], out.at[here, :], sems.at[2 * i + n]
            )
            copy.start()
            copies.append(copy)

        blend(base, store, counts, mine, (first + i, first + 2 + i), both, ups, cap)
    for copy in copies:
        copy.wait()


def whole(array):
    return pl.BlockSpec(array.shape, lambda i: (0,) * array.ndim)


def combine_main(where, mine, counts, base, own, other, main, rank):
    packs = pl.BlockSpec((main.shape[0], 16, main.shape[2]), lambda i: (0, rank // 8, 0))
    return pl.pallas_call(
        out_main_kernel,
        grid=(1,),
        out_shape=jax.ShapeDtypeStruct(base.shape, jnp.bfloat16),
        in_specs=[SMEM, SMEM, SMEM, whole(base), whole(own), whole(other), packs],
        out_specs=whole(base),
        scratch_shapes=[
            pltpu.VMEM((2 * own.shape[0] * own.shape[1], own.shape[2]), jnp.bfloat16)
        ],
        compiler_params=pltpu.CompilerParams(vmem_limit_bytes=6 << 20),
        cost_estimate=pl.CostEstimate(
            flops=base.size * rank * 2, bytes_accessed=base.size * 8, transcendentals=0
        ),
    )(where, mine, counts, base, own, other, main)


def combine_extra(mine, counts, base, low, extras, out, rank):
    pack = pl.BlockSpec((16, extras[0].shape[1]), lambda i: (rank // 8, 0))
    cap = base.shape[0] // counts.shape[0]
    return pl.pallas_call(
        out_extra_kernel,
        grid=(1,),
        out_shape=jax.ShapeDtypeStruct(out.shape, out.dtype),
        in_specs=[SMEM, SMEM, whole(base), whole(low), pack, pack, HBM],
        out_specs=HBM,
        input_output_aliases={6: 0},
        scratch_shapes=[
            pltpu.VMEM((EXTRA, cap, base.shape[1]), jnp.bfloat16),
            pltpu.SemaphoreType.DMA((EXTRA,)),
        ],
        compiler_params=pltpu.CompilerParams(vmem_limit_bytes=4 << 20),
        cost_estimate=pl.CostEstimate(
            flops=base.size * rank // 4, bytes_accessed=base.size * 4, transcendentals=0
        ),
    )(mine, counts, base, low, *extras, out)


def on_device(
    hidden,
    value_weight,
    down_weights,
    up_weights,
    group_adapter_id,
    adapter_storage_row,
    group_live_count,
):
    dp_count = lax.axis_size("dp")
    me = lax.axis_index("dp")
    owned, rank, width = down_weights.shape
    groups = group_adapter_id.shape[0] // dp_count
    cap = hidden.shape[0] // groups
    me_row = me.astype(jnp.int32).reshape(1)
    served, mine = index_tables(me_row, group_adapter_id, adapter_storage_row, dp_count)
    counts = lax.dynamic_slice_in_dim(group_live_count, me * groups, groups)

    def wide(hidden, value_weight, down_weights, up_weights):
        stored = adapter_storage_row[group_adapter_id]
        owners = (stored // owned).reshape(dp_count, groups)
        slots = (stored % owned).reshape(dp_count, groups)
        same = owners[:, :, None] == owners[:, None, :]
        earlier = jnp.arange(groups)[None, None, :] < jnp.arange(groups)[None, :, None]
        ranking = jnp.sum(same & earlier, axis=2)
        hits = (owners == me)[:, :, None] & (ranking[:, :, None] == jnp.arange(MOST))
        rows = jnp.sum(jnp.where(hits, slots[:, :, None], 0), axis=1).reshape(-1)
        my_owners = lax.dynamic_index_in_dim(owners, me, 0, keepdims=False)
        my_ranking = lax.dynamic_index_in_dim(ranking, me, 0, keepdims=False)
        base_terms = jnp.dot(hidden, value_weight, preferred_element_type=jnp.float32)
        base = lax.psum_scatter(base_terms, "tp", scatter_dimension=1, tiled=True)
        downs = lax.all_to_all(down_weights[rows], "dp", 0, 0, tiled=True)
        ups = lax.all_to_all(up_weights[rows], "dp", 0, 0, tiled=True)
        picked = my_owners * MOST + my_ranking
        partial = jnp.einsum(
            "gcd,grd->gcr",
            hidden.reshape(groups, cap, width),
            downs[picked],
            preferred_element_type=jnp.float32,
        )
        low = low_rank_sum(partial.reshape(groups * cap, rank))
        return finish(base, low, ups[picked], counts)

    def narrow(hidden, value_weight, down_weights, up_weights):
        side = math.isqrt(dp_count)
        hot = mine[FLAGS, HOT]
        a = (me // side - hot // side) % side
        b = (me % side - hot % side) % side
        offsets = jnp.stack([a, b]).astype(jnp.int32)
        trees = (True, False)
        soon = [
            (tree, ((2, part[0]), (2, part[1]), (near, 2), (near, 3)))
            for tree in trees
            for near, part in ((1, (0, 1)), (3, (2, 3)))
        ]
        late = [(tree, ((near, 0), (near, 1))) for tree in trees for near in (1, 3)]
        late += [(tree, ((0, 0), (0, 1), (0, 2), (0, 3))) for tree in trees]
        moves = ((1, 0), (-1, 0), (0, 1), (0, -1))
        turned = ((0, 1), (0, -1), (1, 0), (-1, 0))
        send = lambda values, ways: [shift(v, *way) for v, way in zip(values, ways)]
        barrier = lax.optimization_barrier
        scalars = (me_row, served, mine)
        gathered = gather_call(
            functools.partial(extra_kernel, soon), (4,) * 4, 16, scalars, down_weights, up_weights
        )
        fresh = send(gathered, moves)
        later_served, _ = barrier((served, gathered))
        later = gather_call(
            functools.partial(extra_kernel, late),
            (2,) * 4 + (4,) * 2,
            16,
            (me_row, later_served, mine),
            down_weights,
            up_weights,
        )
        main_served, _ = barrier((served, later))
        (main_sent,) = gather_call(
            main_kernel, (dp_count,), dp_count, (main_served,), down_weights, up_weights
        )
        fresh, near, main_sent = barrier((fresh, later[:4], main_sent))
        unit = main_sent.shape[1:]
        two = (2,) + unit
        relayed = vmem_call(
            relay_kernel, (two,) * 4, main_sent.dtype, (offsets,), (*fresh, *near)
        )
        near_a = send(relayed, moves)
        base_hidden, _ = barrier((hidden, relayed))
        base_terms = jnp.dot(base_hidden, value_weight, preferred_element_type=jnp.float32)
        base_terms, main_sent = barrier((base_terms, main_sent))
        main = lax.all_to_all(main_sent, "dp", 0, 0, tiled=True)
        base = lax.psum_scatter(base_terms, "tp", scatter_dimension=1, tiled=True)
        near_a, base_terms = barrier((near_a, base_terms))
        tree_arrays = [
            (later[4 + h], near_a[2 * h], near_a[2 * h + 1], fresh[2 * h], fresh[2 * h + 1])
            for h in range(2)
        ]
        lines = vmem_call(
            line_kernel,
            (unit,) * 8,
            main_sent.dtype,
            (offsets,),
            tree_arrays[0] + tree_arrays[1],
        )
        x0, x1, x2, x3, y0, y1, y2, y3 = lines
        x_ahead, x_back, y_ahead, y_back = barrier(send((x2, x3, y2, y3), turned))
        passed = vmem_call(
            pass_kernel,
            (unit,) * 2,
            main_sent.dtype,
            (offsets,),
            (x_ahead, y_ahead, x1, y1),
        )
        passed, main = barrier((passed, main))
        x_next, y_next = send(passed, (turned[0], turned[2]))
        pairs = (groups - EXTRA) // 2
        partial = low_partial(
            functools.partial(low_main_kernel, cap), pairs, cap, rank, mine, hidden, (main,)
        )
        own, other = low_rank_rounds(partial)
        extras = vmem_call(
            pick_kernel,
            (unit,) * 2,
            main_sent.dtype,
            (offsets,),
            (x0, x_back, x_next, y0, y_back, y_next),
        )
        extra_partial = low_partial(
            functools.partial(low_extra_kernel, groups - EXTRA, cap),
            EXTRA // 2,
            cap,
            rank,
            mine,
            hidden,
            extras,
        )
        extra_low = low_rank_doubling(extra_partial)
        t = lax.axis_index("tp")
        where = jnp.stack([t // 2, t % 2]).astype(jnp.int32)
        out = combine_main(where, mine, counts, base, own, other, main, rank)
        return combine_extra(mine, counts, base, extra_low, extras, out, rank)

    return lax.cond(
        mine[FLAGS, FITS] == 1, narrow, wide, hidden, value_weight, down_weights, up_weights
    )


def solution(mesh):
    return jax.shard_map(
        on_device,
        mesh=mesh,
        in_specs=(
            P("dp", "tp"),
            P("tp", None),
            P("dp", None, "tp"),
            P("dp", None, "tp"),
            P(),
            P(),
            P(),
        ),
        out_specs=P("dp", "tp"),
        check_vma=False,
    )
```

```python
import functools
import math

import jax
import jax.numpy as jnp
from jax import lax
from jax.experimental import pallas as pl
from jax.experimental.pallas import tpu as pltpu
from jax.sharding import PartitionSpec as P

ADAPTER_SCALE = 0.5
MAIN = 2
MOST = 6
EXTRA = MOST - MAIN


def low_rank_sum(partial):
    rows, rank = partial.shape
    tp_count = lax.axis_size("tp")
    pieces = lax.all_to_all(partial, "tp", split_axis=0, concat_axis=0, tiled=True)
    mine = jnp.sum(pieces.reshape(tp_count, rows // tp_count, rank), axis=0).astype(jnp.bfloat16)
    return lax.all_gather(mine, "tp", axis=0, tiled=True)


def finish(base, low, ups, counts):
    groups = counts.shape[0]
    cap = base.shape[0] // groups
    delta = jnp.einsum(
        "gcr,grv->gcv", low.reshape(groups, cap, -1), ups, preferred_element_type=jnp.float32
    )
    merged = base.reshape(groups, cap, -1) + ADAPTER_SCALE * delta
    active = jnp.arange(cap)[None, :, None] < counts[:, None, None]
    out = jnp.where(active, merged, jnp.float32(0.0)).astype(jnp.bfloat16)
    return out.reshape(base.shape)


SMEM = pl.BlockSpec(memory_space=pltpu.SMEM)
VMEM = pl.BlockSpec(memory_space=pltpu.VMEM)
HBM = pl.BlockSpec(memory_space=pltpu.HBM)
LANES = 128
ORDER, PLACE, FLAGS = 0, 1, 2
HOT, FITS = 0, 1


def shift(value, dx, dy):
    side = math.isqrt(lax.axis_size("dp"))
    pairs = [
        (x * side + y, (x + dx) % side * side + (y + dy) % side)
        for x in range(side)
        for y in range(side)
    ]
    return lax.ppermute(value, "dp", pairs)


def index_kernel(me_ref, ids_ref, table_ref, served_ref, mine_ref, owner_ref, rank_ref):
    total = ids_ref.shape[0]
    dp_count = served_ref.shape[0]
    groups = total // dp_count
    chunks = table_ref.shape[0]
    owned = chunks * LANES // dp_count
    me = me_ref[0]
    f32, bf16 = jnp.float32, jnp.bfloat16
    ids = ids_ref[...]
    lane = lax.broadcasted_iota(jnp.int32, (total, LANES), 1)
    found = jnp.zeros((total, LANES), jnp.int32)
    for c in range(chunks):
        found += jnp.where(ids == lane + c * LANES, table_ref[c : c + 1, :], 0)
    stored = jnp.sum(found, axis=1, keepdims=True)
    owner = lax.div(stored, owned)
    slot = stored - owner * owned
    holds = jnp.where(owner == lane, 1.0, 0.0)
    low = lax.broadcasted_iota(jnp.int32, (groups, groups), 0)
    low = jnp.where(low > lax.broadcasted_iota(jnp.int32, (groups, groups), 1), 1.0, 0.0)
    low = low.astype(bf16)
    holds16 = holds.astype(bf16)
    before = jnp.concatenate(
        [
            jnp.dot(low, holds16[r * groups : (r + 1) * groups], preferred_element_type=f32)
            for r in range(dp_count)
        ],
        axis=0,
    )
    ranking = jnp.sum(before * holds, axis=1, keepdims=True).astype(jnp.int32)
    owner_ref[...] = jnp.broadcast_to(owner, (total, LANES))
    rank_ref[...] = jnp.broadcast_to(ranking, (total, LANES))
    block_of = lax.div(lax.broadcasted_iota(jnp.int32, (dp_count, total), 1), groups)
    block = block_of == lax.broadcasted_iota(jnp.int32, (dp_count, total), 0)
    block = jnp.where(block, 1.0, 0.0).astype(bf16)
    loads = jnp.dot(block, holds16, preferred_element_type=f32)
    kept = jnp.where((owner == me) & (ranking == lane), slot, 0).astype(f32).astype(bf16)
    served_ref[...] = jnp.dot(block, kept, preferred_element_type=f32).astype(jnp.int32)
    least = jnp.min(loads, axis=0, keepdims=True)
    row_lane = lax.broadcasted_iota(jnp.int32, (1, LANES), 1)
    hot = jnp.min(jnp.where(least >= MOST, row_lane, LANES), axis=1, keepdims=True)
    spare = jnp.where(row_lane == hot, 0.0, loads)
    most = jnp.max(jnp.max(spare, axis=0, keepdims=True), axis=1, keepdims=True)
    fits = jnp.where(most <= MAIN, 1, 0)
    at = pl.ds(pl.multiple_of(me * groups, groups), groups)
    my_owner = owner_ref[at, :]
    my_rank = rank_ref[at, :]
    late = (my_owner == hot) & (my_rank >= MAIN)
    place = jnp.where(late, dp_count * MAIN + my_rank - MAIN, my_owner * MAIN + my_rank)
    early = jnp.where(late, 0.0, 1.0).astype(bf16)
    ahead = jnp.dot(low, early, preferred_element_type=f32).astype(jnp.int32)
    turn = jnp.where(late, groups - EXTRA + my_rank - MAIN, ahead)
    group_lane = lax.broadcasted_iota(jnp.int32, (groups, LANES), 1)
    group = lax.broadcasted_iota(jnp.int32, (groups, LANES), 0)
    here = turn == group_lane
    mine_ref[...] = jnp.zeros(mine_ref.shape, jnp.int32)
    mine_ref[ORDER : ORDER + 1, :] = jnp.sum(jnp.where(here, group, 0), axis=0, keepdims=True)
    mine_ref[PLACE : PLACE + 1, :] = jnp.sum(jnp.where(here, place, 0), axis=0, keepdims=True)
    mine_ref[FLAGS : FLAGS + 1, :] = jnp.where(
        row_lane == HOT, hot, jnp.where(row_lane == FITS, fits, 0)
    )


def index_tables(me, ids, table, dp_count):
    total = ids.shape[0]
    return pl.pallas_call(
        index_kernel,
        out_shape=(
            jax.ShapeDtypeStruct((dp_count, LANES), jnp.int32),
            jax.ShapeDtypeStruct((8, LANES), jnp.int32),
        ),
        in_specs=[SMEM, VMEM, VMEM],
        out_specs=(VMEM, VMEM),
        scratch_shapes=[pltpu.VMEM((total, LANES), jnp.int32)] * 2,
        compiler_params=pltpu.CompilerParams(vmem_limit_bytes=8 << 20),
    )(me, ids.reshape(total, 1), table.reshape(-1, LANES))


def copy_units(wanted, down, up, up_in, down_sem, up_sem):
    rank = down.shape[1]
    lanes = up.shape[2]
    steps = rank // 16
    downs, ups = [], []
    for i, (dest, index, rows) in enumerate(wanted):
        for half in range(2):
            n = 2 * i + half
            ups.append(pltpu.make_async_copy(up.at[rows[half]], up_in.at[n], up_sem.at[n]))
            ups[-1].start()
            downs.append(
                pltpu.make_async_copy(
                    down.at[rows[half]], dest.at[index, pl.ds(half * rank, rank)], down_sem.at[n]
                )
            )
            downs[-1].start()
    for i, (dest, index, rows) in enumerate(wanted):
        for half in range(2):
            n = 2 * i + half
            ups[n].wait()
            for part in range(steps):
                at = (half * steps + part) * lanes
                dest[index, 2 * rank : 2 * rank + 16, at : at + lanes] = up_in[
                    n, part * 16 : part * 16 + 16, :
                ]
    for copy in downs:
        copy.wait()


def main_kernel(served, down, up, out, *scratch):
    wanted = [(out, p, (served[p, 0], served[p, 1])) for p in range(out.shape[0])]
    copy_units(wanted, down, up, *scratch)


def extra_kernel(lines, me, served, mine, down, up, *refs):
    outs, scratch = refs[: len(lines)], refs[len(lines) :]
    dp_count = served.shape[0]
    side = math.isqrt(dp_count)
    hot = mine[FLAGS, HOT]

    @pl.when(hot == me[0])
    def _():
        hot_x, hot_y = lax.div(hot, side), lax.rem(hot, side)
        wanted = []
        for out, (x_first, units) in zip(outs, lines):
            for i, (a, b) in enumerate(units):
                dx, dy = (a, b) if x_first else (b, a)
                peer = lax.rem(hot_x + dx, side) * side + lax.rem(hot_y + dy, side)
                first = MAIN if x_first else MAIN + 2
                wanted.append((out, i, (served[peer, first], served[peer, first + 1])))
        copy_units(wanted, down, up, *scratch)


def gather_call(kernel, shapes, count, scalars, down, up):
    _, rank, width = down.shape
    lanes = up.shape[2]
    return pl.pallas_call(
        kernel,
        out_shape=[jax.ShapeDtypeStruct((n, 2 * rank + 16, width), down.dtype) for n in shapes],
        in_specs=[SMEM] * len(scalars) + [HBM, HBM],
        out_specs=[VMEM] * len(shapes),
        scratch_shapes=[
            pltpu.VMEM((2 * count, rank, lanes), up.dtype),
            pltpu.SemaphoreType.DMA((2 * count,)),
            pltpu.SemaphoreType.DMA((2 * count,)),
        ],
        compiler_params=pltpu.CompilerParams(vmem_limit_bytes=8 << 20),
        cost_estimate=pl.CostEstimate(
            flops=0, bytes_accessed=count * rank * (width + lanes) * 8, transcendentals=0
        ),
    )(*scalars, down, up)


def vmem_call(kernel, shapes, dtype, scalars, arrays, limit=10):
    return pl.pallas_call(
        kernel,
        out_shape=[jax.ShapeDtypeStruct(shape, dtype) for shape in shapes],
        in_specs=[SMEM] * len(scalars) + [VMEM] * len(arrays),
        out_specs=[VMEM] * len(shapes),
        compiler_params=pltpu.CompilerParams(vmem_limit_bytes=limit << 20),
        cost_estimate=pl.CostEstimate(
            flops=0,
            bytes_accessed=sum(math.prod(shape) for shape in shapes) * 4,
            transcendentals=0,
        ),
    )(*scalars, *arrays)


def move(dst, src):
    rows = src.shape[0]

    def body(i, carry):
        at = pl.ds(pl.multiple_of(i * 16, 16), 16)
        dst[at, :] = src[at, :]
        return carry

    lax.fori_loop(0, rows // 16, body, 0, unroll=3)


def relay_kernel(offsets, *refs):
    fresh, near, outs = refs[:4], refs[4:8], refs[8:]
    for i in range(4):
        at = offsets[i // 2]
        close = 1 if i % 2 == 0 else 3
        for source, when in ((near[i], at != close), (fresh[i], at == close)):

            @pl.when(when)
            def _(source=source, out=outs[i]):
                for u in range(2):
                    move(out.at[u], source.at[u])


def line_kernel(offsets, *refs):
    outs = refs[10:]
    for h in range(2):
        own, plus_a, minus_a, plus_b, minus_b = refs[5 * h : 5 * h + 5]
        out = outs[4 * h : 4 * h + 4]
        at = offsets[h]
        low, high = own.at[pl.ds(0, 2)], own.at[pl.ds(2, 2)]
        plus_b, minus_b = plus_b.at[pl.ds(2, 2)], minus_b.at[pl.ds(2, 2)]
        picks = ((low, high), (plus_a, plus_b), (plus_a, minus_a), (minus_a, minus_b))
        for offset, (first, second) in enumerate(picks):

            @pl.when(at == offset)
            def _(first=first, second=second, out=out):
                for u in range(2):
                    move(out[u], first.at[u])
                    move(out[2 + u], second.at[u])


def pick_kernel(offsets, *refs):
    for h in range(2):
        at = offsets[1 - h]
        for offset, source in enumerate(refs[4 * h : 4 * h + 4]):

            @pl.when(at == offset)
            def _(source=source, out=refs[8 + h]):
                move(out, source)


def paired(hidden, mine, i, pairs, cap, first, second):
    spots = [pl.multiple_of(mine[ORDER, j] * cap, cap) for j in (i, i + pairs)]
    rows = jnp.concatenate([hidden[pl.ds(spot, cap), :] for spot in spots], axis=0)
    product = lax.dot_general(
        rows,
        jnp.concatenate([first, second], axis=0),
        (((1,), (1,)), ((), ())),
        preferred_element_type=jnp.float32,
    )
    lane = lax.broadcasted_iota(jnp.int32, (cap, product.shape[1]), 1)
    return jnp.where(lane < first.shape[0], product[:cap], product[cap:])


def low_main_kernel(cap, mine, hidden, main, out):
    rank = out.shape[1] // 2
    pairs = out.shape[0] // cap

    def weights(j):
        place = mine[PLACE, j]
        unit = lax.div(place, 2)
        return main[unit, pl.ds(pl.multiple_of((place - 2 * unit) * rank, rank), rank), :]

    def body(i, carry):
        at = pl.ds(pl.multiple_of(i * cap, cap), cap)
        out[at, :] = paired(hidden, mine, i, pairs, cap, weights(i), weights(i + pairs))
        return carry

    lax.fori_loop(0, pairs, body, 0, unroll=2)


def low_extra_kernel(first, cap, mine, hidden, *refs):
    extras, out = refs[:-1], refs[-1]
    rank = out.shape[1] // 2
    for i in range(2):
        spots = [pl.multiple_of(mine[ORDER, first + 2 * u + i] * cap, cap) for u in range(2)]
        rows = jnp.concatenate([hidden[pl.ds(spot, cap), :] for spot in spots], axis=0)
        part = slice(i * rank, (i + 1) * rank)
        product = lax.dot_general(
            rows,
            jnp.concatenate([extras[0][part, :], extras[1][part, :]], axis=0),
            (((1,), (1,)), ((), ())),
            preferred_element_type=jnp.float32,
        )
        lane = lax.broadcasted_iota(jnp.int32, (cap, 2 * rank), 1)
        out[i * cap : (i + 1) * cap, :] = jnp.where(lane < rank, product[:cap], product[cap:])


def low_partial(kernel, pairs, cap, rank, mine, hidden, weights):
    return pl.pallas_call(
        kernel,
        out_shape=jax.ShapeDtypeStruct((pairs * cap, 2 * rank), jnp.float32),
        in_specs=[SMEM] + [VMEM] * (1 + len(weights)),
        out_specs=VMEM,
        compiler_params=pltpu.CompilerParams(vmem_limit_bytes=10 << 20),
        cost_estimate=pl.CostEstimate(
            flops=pairs * cap * rank * 4 * hidden.shape[1],
            bytes_accessed=sum(w.size for w in weights) * 2,
            transcendentals=0,
        ),
    )(mine, hidden, *weights)


def low_rank_rounds(partial):
    tp_count = lax.axis_size("tp")
    chips = tp_count // 2
    t = lax.axis_index("tp")
    z, core = t // 2, t % 2
    half = partial.shape[0] // 2
    piece = half // chips
    swap = [(i, i ^ 1) for i in range(tp_count)]
    turn = lambda d: [(i, (i + 2 * d) % tp_count) for i in range(tp_count)]
    cut = lambda array, start, size: lax.dynamic_slice_in_dim(array, start, size, 0)
    total = cut(partial, core * half, half) + lax.ppermute(
        cut(partial, (1 - core) * half, half), "tp", swap
    )
    pieces = [
        lax.ppermute(cut(total, (z + d) % chips * piece, piece), "tp", turn(d))
        for d in range(1, chips)
    ]
    summed = (cut(total, z * piece, piece) + sum(pieces)).astype(jnp.bfloat16)
    own = jnp.stack([summed] + [lax.ppermute(summed, "tp", turn(d)) for d in range(1, chips)])
    return own, lax.ppermute(own, "tp", swap)


def low_rank_doubling(partial):
    tp_count = lax.axis_size("tp")
    last = tp_count // 2 - 1
    z_of = lambda i: i // 2
    for partner in (
        lambda i: i ^ 1,
        lambda i: (z_of(i) ^ 1) * 2 + i % 2,
        lambda i: (last - z_of(i)) * 2 + i % 2,
    ):
        partial += lax.ppermute(partial, "tp", [(i, partner(i)) for i in range(tp_count)])
    return partial


def blend(base, out, counts, mine, j, both, ups, cap):
    rank = both.shape[1] // 2
    lane = lax.broadcasted_iota(jnp.int32, both.shape, 1)
    none = jnp.zeros_like(both)
    left = jnp.concatenate(
        [jnp.where(lane < rank, both, none), jnp.where(lane < rank, none, both)], axis=0
    )
    delta = jnp.dot(left, jnp.concatenate(ups, axis=0), preferred_element_type=jnp.float32)
    rows = lax.broadcasted_iota(jnp.int32, (cap, base.shape[1]), 0)
    for n in range(2):
        g = mine[ORDER, j[n]]
        here = pl.ds(pl.multiple_of(g * cap, cap), cap)
        merged = base[here, :] + ADAPTER_SCALE * delta[n * cap : (n + 1) * cap]
        out(n, here, jnp.where(rows < counts[g], merged, 0.0).astype(jnp.bfloat16))


def out_main_kernel(where, mine, counts, base, own, other, main, out, low):
    groups = counts.shape[0]
    cap = base.shape[0] // groups
    chips, piece, rank = own.shape[0], own.shape[1], own.shape[2] // 2
    lanes = base.shape[1]
    z, core = where[0], where[1]
    steps = rank // 16
    pairs = low.shape[0] // cap
    for d in range(chips):
        quarter = lax.rem(z - d + chips, chips)
        for ref, half in ((own, core), (other, 1 - core)):
            at = pl.multiple_of((half * chips + quarter) * piece, 16)
            low[pl.ds(at, piece), :] = ref[d]

    def up(j):
        place = mine[PLACE, j]
        unit = lax.div(place, 2)
        at = (place - 2 * unit) * steps * lanes
        return [
            main[unit, :, pl.ds(pl.multiple_of(at + part * lanes, lanes), lanes)]
            for part in range(steps)
        ]

    def store(n, here, value):
        out[here, :] = value

    def body(i, carry):
        both = low[pl.ds(pl.multiple_of(i * cap, cap), cap), :]
        spots = (i, i + pairs)
        blend(base, store, counts, mine, spots, both, up(i) + up(i + pairs), cap)
        return carry

    lax.fori_loop(0, pairs, body, 0, unroll=2)


def out_extra_kernel(mine, counts, base, low, first_pack, second_pack, _, out, blocks, sems):
    groups = counts.shape[0]
    cap = base.shape[0] // groups
    rank = low.shape[1] // 2
    lanes = base.shape[1]
    steps = rank // 16
    first = groups - EXTRA
    copies = []
    for i in range(2):
        both = low[i * cap : (i + 1) * cap, :].astype(jnp.bfloat16)
        ups = [
            pack[:, (i * steps + part) * lanes : (i * steps + part + 1) * lanes]
            for pack in (first_pack, second_pack)
            for part in range(steps)
        ]

        def store(n, here, value, i=i):
            blocks[2 * i + n] = value
            copy = pltpu.make_async_copy(
                blocks.at[2 * i + n], out.at[here, :], sems.at[2 * i + n]
            )
            copy.start()
            copies.append(copy)

        blend(base, store, counts, mine, (first + i, first + 2 + i), both, ups, cap)
    for copy in copies:
        copy.wait()


def whole(array):
    return pl.BlockSpec(array.shape, lambda i: (0,) * array.ndim)


def combine_main(where, mine, counts, base, own, other, main, rank):
    packs = pl.BlockSpec((main.shape[0], 16, main.shape[2]), lambda i: (0, rank // 8, 0))
    return pl.pallas_call(
        out_main_kernel,
        grid=(1,),
        out_shape=jax.ShapeDtypeStruct(base.shape, jnp.bfloat16),
        in_specs=[SMEM, SMEM, SMEM, whole(base), whole(own), whole(other), packs],
        out_specs=whole(base),
        scratch_shapes=[
            pltpu.VMEM((2 * own.shape[0] * own.shape[1], own.shape[2]), jnp.bfloat16)
        ],
        compiler_params=pltpu.CompilerParams(vmem_limit_bytes=6 << 20),
        cost_estimate=pl.CostEstimate(
            flops=base.size * rank * 2, bytes_accessed=base.size * 8, transcendentals=0
        ),
    )(where, mine, counts, base, own, other, main)


def combine_extra(mine, counts, base, low, extras, out, rank):
    pack = pl.BlockSpec((16, extras[0].shape[1]), lambda i: (rank // 8, 0))
    cap = base.shape[0] // counts.shape[0]
    return pl.pallas_call(
        out_extra_kernel,
        grid=(1,),
        out_shape=jax.ShapeDtypeStruct(out.shape, out.dtype),
        in_specs=[SMEM, SMEM, whole(base), whole(low), pack, pack, HBM],
        out_specs=HBM,
        input_output_aliases={6: 0},
        scratch_shapes=[
            pltpu.VMEM((EXTRA, cap, base.shape[1]), jnp.bfloat16),
            pltpu.SemaphoreType.DMA((EXTRA,)),
        ],
        compiler_params=pltpu.CompilerParams(vmem_limit_bytes=4 << 20),
        cost_estimate=pl.CostEstimate(
            flops=base.size * rank // 4, bytes_accessed=base.size * 4, transcendentals=0
        ),
    )(mine, counts, base, low, *extras, out)


def on_device(
    hidden,
    value_weight,
    down_weights,
    up_weights,
    group_adapter_id,
    adapter_storage_row,
    group_live_count,
):
    dp_count = lax.axis_size("dp")
    me = lax.axis_index("dp")
    owned, rank, width = down_weights.shape
    groups = group_adapter_id.shape[0] // dp_count
    cap = hidden.shape[0] // groups
    me_row = me.astype(jnp.int32).reshape(1)
    served, mine = index_tables(me_row, group_adapter_id, adapter_storage_row, dp_count)
    counts = lax.dynamic_slice_in_dim(group_live_count, me * groups, groups)

    def wide(hidden, value_weight, down_weights, up_weights):
        stored = adapter_storage_row[group_adapter_id]
        owners = (stored // owned).reshape(dp_count, groups)
        slots = (stored % owned).reshape(dp_count, groups)
        same = owners[:, :, None] == owners[:, None, :]
        earlier = jnp.arange(groups)[None, None, :] < jnp.arange(groups)[None, :, None]
        ranking = jnp.sum(same & earlier, axis=2)
        hits = (owners == me)[:, :, None] & (ranking[:, :, None] == jnp.arange(MOST))
        rows = jnp.sum(jnp.where(hits, slots[:, :, None], 0), axis=1).reshape(-1)
        my_owners = lax.dynamic_index_in_dim(owners, me, 0, keepdims=False)
        my_ranking = lax.dynamic_index_in_dim(ranking, me, 0, keepdims=False)
        base_terms = jnp.dot(hidden, value_weight, preferred_element_type=jnp.float32)
        base = lax.psum_scatter(base_terms, "tp", scatter_dimension=1, tiled=True)
        downs = lax.all_to_all(down_weights[rows], "dp", 0, 0, tiled=True)
        ups = lax.all_to_all(up_weights[rows], "dp", 0, 0, tiled=True)
        picked = my_owners * MOST + my_ranking
        partial = jnp.einsum(
            "gcd,grd->gcr",
            hidden.reshape(groups, cap, width),
            downs[picked],
            preferred_element_type=jnp.float32,
        )
        low = low_rank_sum(partial.reshape(groups * cap, rank))
        return finish(base, low, ups[picked], counts)

    def narrow(hidden, value_weight, down_weights, up_weights):
        side = math.isqrt(dp_count)
        hot = mine[FLAGS, HOT]
        a = (me // side - hot // side) % side
        b = (me % side - hot % side) % side
        offsets = jnp.stack([a, b]).astype(jnp.int32)
        trees = (True, False)
        soon = [
            (tree, ((2, part[0]), (2, part[1]), (near, 2), (near, 3)))
            for tree in trees
            for near, part in ((1, (0, 1)), (3, (2, 3)))
        ]
        late = [(tree, ((near, 0), (near, 1))) for tree in trees for near in (1, 3)]
        late += [(tree, ((0, 0), (0, 1), (0, 2), (0, 3))) for tree in trees]
        moves = ((1, 0), (-1, 0), (0, 1), (0, -1))
        turned = ((0, 1), (0, 2), (0, -1), (1, 0), (2, 0), (-1, 0))
        send = lambda values, ways: [shift(v, *way) for v, way in zip(values, ways)]
        barrier = lax.optimization_barrier
        (main_sent,) = gather_call(
            main_kernel, (dp_count,), dp_count, (served,), down_weights, up_weights
        )
        main = lax.all_to_all(main_sent, "dp", 0, 0, tiled=True)
        unit = main_sent.shape[1:]
        dtype = main_sent.dtype
        soon_served, _ = barrier((served, main_sent))
        gathered = gather_call(
            functools.partial(extra_kernel, soon),
            (4,) * 4,
            16,
            (me_row, soon_served, mine),
            down_weights,
            up_weights,
        )
        fresh = send(gathered, moves)
        later_served, _ = barrier((soon_served, gathered))
        later = gather_call(
            functools.partial(extra_kernel, late),
            (2,) * 4 + (4,) * 2,
            16,
            (me_row, later_served, mine),
            down_weights,
            up_weights,
        )
        base_hidden, _ = barrier((hidden, later))
        base_terms = jnp.dot(base_hidden, value_weight, preferred_element_type=jnp.float32)
        base = lax.psum_scatter(base_terms, "tp", scatter_dimension=1, tiled=True)
        main, _ = barrier((main, base_terms))
        pairs = (groups - EXTRA) // 2
        partial = low_partial(
            functools.partial(low_main_kernel, cap), pairs, cap, rank, mine, hidden, (main,)
        )
        own, other = low_rank_rounds(partial)
        t = lax.axis_index("tp")
        where = jnp.stack([t // 2, t % 2]).astype(jnp.int32)
        out = combine_main(where, mine, counts, base, own, other, main, rank)
        fresh, near, _ = barrier((fresh, later[:4], partial))
        relayed = vmem_call(
            relay_kernel, ((2,) + unit,) * 4, dtype, (offsets,), (*fresh, *near)
        )
        near_a = barrier(send(relayed, moves))
        tree_arrays = [
            (later[4 + h], near_a[2 * h], near_a[2 * h + 1], fresh[2 * h], fresh[2 * h + 1])
            for h in range(2)
        ]
        lines = vmem_call(
            line_kernel, (unit,) * 8, dtype, (offsets,), tree_arrays[0] + tree_arrays[1]
        )
        got = send(lines[1:4] + lines[5:8], turned)
        got, out = barrier((got, out))
        extras = vmem_call(
            pick_kernel,
            (unit,) * 2,
            dtype,
            (offsets,),
            (lines[0], *got[:3], lines[4], *got[3:]),
        )
        extra_partial = low_partial(
            functools.partial(low_extra_kernel, groups - EXTRA, cap),
            EXTRA // 2,
            cap,
            rank,
            mine,
            hidden,
            extras,
        )
        extra_low = low_rank_doubling(extra_partial)
        return combine_extra(mine, counts, base, extra_low, extras, out, rank)

    return lax.cond(
        mine[FLAGS, FITS] == 1, narrow, wide, hidden, value_weight, down_weights, up_weights
    )


def solution(mesh):
    return jax.shard_map(
        on_device,
        mesh=mesh,
        in_specs=(
            P("dp", "tp"),
            P("tp", None),
            P("dp", None, "tp"),
            P("dp", None, "tp"),
            P(),
            P(),
            P(),
        ),
        out_specs=P("dp", "tp"),
        check_vma=False,
    )
```

```python
import functools
import math

import jax
import jax.numpy as jnp
from jax import lax
from jax.experimental import pallas as pl
from jax.experimental.pallas import tpu as pltpu
from jax.sharding import PartitionSpec as P

ADAPTER_SCALE = 0.5
MAIN = 2
MOST = 6
EXTRA = MOST - MAIN


def low_rank_sum(partial):
    rows, rank = partial.shape
    tp_count = lax.axis_size("tp")
    pieces = lax.all_to_all(partial, "tp", split_axis=0, concat_axis=0, tiled=True)
    mine = jnp.sum(pieces.reshape(tp_count, rows // tp_count, rank), axis=0).astype(jnp.bfloat16)
    return lax.all_gather(mine, "tp", axis=0, tiled=True)


def finish(base, low, ups, counts):
    groups = counts.shape[0]
    cap = base.shape[0] // groups
    delta = jnp.einsum(
        "gcr,grv->gcv", low.reshape(groups, cap, -1), ups, preferred_element_type=jnp.float32
    )
    merged = base.reshape(groups, cap, -1) + ADAPTER_SCALE * delta
    active = jnp.arange(cap)[None, :, None] < counts[:, None, None]
    out = jnp.where(active, merged, jnp.float32(0.0)).astype(jnp.bfloat16)
    return out.reshape(base.shape)


SMEM = pl.BlockSpec(memory_space=pltpu.SMEM)
VMEM = pl.BlockSpec(memory_space=pltpu.VMEM)
HBM = pl.BlockSpec(memory_space=pltpu.HBM)
LANES = 128
ORDER, PLACE, FLAGS = 0, 1, 2
HOT, FITS = 0, 1


def shift(value, dx, dy):
    side = math.isqrt(lax.axis_size("dp"))
    pairs = [
        (x * side + y, (x + dx) % side * side + (y + dy) % side)
        for x in range(side)
        for y in range(side)
    ]
    return lax.ppermute(value, "dp", pairs)


def index_kernel(me_ref, ids_ref, table_ref, served_ref, mine_ref, owner_ref, rank_ref):
    total = ids_ref.shape[0]
    dp_count = served_ref.shape[0]
    groups = total // dp_count
    chunks = table_ref.shape[0]
    owned = chunks * LANES // dp_count
    me = me_ref[0]
    f32, bf16 = jnp.float32, jnp.bfloat16
    ids = ids_ref[...]
    lane = lax.broadcasted_iota(jnp.int32, (total, LANES), 1)
    found = jnp.zeros((total, LANES), jnp.int32)
    for c in range(chunks):
        found += jnp.where(ids == lane + c * LANES, table_ref[c : c + 1, :], 0)
    stored = jnp.sum(found, axis=1, keepdims=True)
    owner = lax.div(stored, owned)
    slot = stored - owner * owned
    holds = jnp.where(owner == lane, 1.0, 0.0)
    low = lax.broadcasted_iota(jnp.int32, (groups, groups), 0)
    low = jnp.where(low > lax.broadcasted_iota(jnp.int32, (groups, groups), 1), 1.0, 0.0)
    low = low.astype(bf16)
    holds16 = holds.astype(bf16)
    before = jnp.concatenate(
        [
            jnp.dot(low, holds16[r * groups : (r + 1) * groups], preferred_element_type=f32)
            for r in range(dp_count)
        ],
        axis=0,
    )
    ranking = jnp.sum(before * holds, axis=1, keepdims=True).astype(jnp.int32)
    owner_ref[...] = jnp.broadcast_to(owner, (total, LANES))
    rank_ref[...] = jnp.broadcast_to(ranking, (total, LANES))
    block_of = lax.div(lax.broadcasted_iota(jnp.int32, (dp_count, total), 1), groups)
    block = block_of == lax.broadcasted_iota(jnp.int32, (dp_count, total), 0)
    block = jnp.where(block, 1.0, 0.0).astype(bf16)
    loads = jnp.dot(block, holds16, preferred_element_type=f32)
    kept = jnp.where((owner == me) & (ranking == lane), slot, 0).astype(f32).astype(bf16)
    served_ref[...] = jnp.dot(block, kept, preferred_element_type=f32).astype(jnp.int32)
    least = jnp.min(loads, axis=0, keepdims=True)
    row_lane = lax.broadcasted_iota(jnp.int32, (1, LANES), 1)
    hot = jnp.min(jnp.where(least >= MOST, row_lane, LANES), axis=1, keepdims=True)
    spare = jnp.where(row_lane == hot, 0.0, loads)
    most = jnp.max(jnp.max(spare, axis=0, keepdims=True), axis=1, keepdims=True)
    fits = jnp.where(most <= MAIN, 1, 0)
    at = pl.ds(pl.multiple_of(me * groups, groups), groups)
    my_owner = owner_ref[at, :]
    my_rank = rank_ref[at, :]
    late = (my_owner == hot) & (my_rank >= MAIN)
    place = jnp.where(late, dp_count * MAIN + my_rank - MAIN, my_owner * MAIN + my_rank)
    early = jnp.where(late, 0.0, 1.0).astype(bf16)
    ahead = jnp.dot(low, early, preferred_element_type=f32).astype(jnp.int32)
    turn = jnp.where(late, groups - EXTRA + my_rank - MAIN, ahead)
    group_lane = lax.broadcasted_iota(jnp.int32, (groups, LANES), 1)
    group = lax.broadcasted_iota(jnp.int32, (groups, LANES), 0)
    here = turn == group_lane
    mine_ref[...] = jnp.zeros(mine_ref.shape, jnp.int32)
    mine_ref[ORDER : ORDER + 1, :] = jnp.sum(jnp.where(here, group, 0), axis=0, keepdims=True)
    mine_ref[PLACE : PLACE + 1, :] = jnp.sum(jnp.where(here, place, 0), axis=0, keepdims=True)
    mine_ref[FLAGS : FLAGS + 1, :] = jnp.where(
        row_lane == HOT, hot, jnp.where(row_lane == FITS, fits, 0)
    )


def index_tables(me, ids, table, dp_count):
    total = ids.shape[0]
    return pl.pallas_call(
        index_kernel,
        out_shape=(
            jax.ShapeDtypeStruct((dp_count, LANES), jnp.int32),
            jax.ShapeDtypeStruct((8, LANES), jnp.int32),
        ),
        in_specs=[SMEM, VMEM, VMEM],
        out_specs=(VMEM, VMEM),
        scratch_shapes=[pltpu.VMEM((total, LANES), jnp.int32)] * 2,
        compiler_params=pltpu.CompilerParams(vmem_limit_bytes=8 << 20),
    )(me, ids.reshape(total, 1), table.reshape(-1, LANES))


def copy_units(wanted, down, up, up_in, down_sem, up_sem):
    rank = down.shape[1]
    lanes = up.shape[2]
    steps = rank // 16
    downs, ups = [], []
    for i, (dest, index, rows) in enumerate(wanted):
        for half in range(2):
            n = 2 * i + half
            ups.append(pltpu.make_async_copy(up.at[rows[half]], up_in.at[n], up_sem.at[n]))
            ups[-1].start()
            downs.append(
                pltpu.make_async_copy(
                    down.at[rows[half]], dest.at[index, pl.ds(half * rank, rank)], down_sem.at[n]
                )
            )
            downs[-1].start()
    for i, (dest, index, rows) in enumerate(wanted):
        for half in range(2):
            n = 2 * i + half
            ups[n].wait()
            for part in range(steps):
                at = (half * steps + part) * lanes
                dest[index, 2 * rank : 2 * rank + 16, at : at + lanes] = up_in[
                    n, part * 16 : part * 16 + 16, :
                ]
    for copy in downs:
        copy.wait()


def main_kernel(served, down, up, out, *scratch):
    wanted = [(out, p, (served[p, 0], served[p, 1])) for p in range(out.shape[0])]
    copy_units(wanted, down, up, *scratch)


def extra_kernel(lines, me, served, mine, down, up, *refs):
    outs, scratch = refs[: len(lines)], refs[len(lines) :]
    dp_count = served.shape[0]
    side = math.isqrt(dp_count)
    hot = mine[FLAGS, HOT]

    @pl.when(hot == me[0])
    def _():
        hot_x, hot_y = lax.div(hot, side), lax.rem(hot, side)
        wanted = []
        for out, (x_first, units) in zip(outs, lines):
            for i, (a, b) in enumerate(units):
                dx, dy = (a, b) if x_first else (b, a)
                peer = lax.rem(hot_x + dx, side) * side + lax.rem(hot_y + dy, side)
                first = MAIN if x_first else MAIN + 2
                wanted.append((out, i, (served[peer, first], served[peer, first + 1])))
        copy_units(wanted, down, up, *scratch)


def gather_call(kernel, shapes, count, scalars, down, up, limit=8):
    _, rank, width = down.shape
    lanes = up.shape[2]
    return pl.pallas_call(
        kernel,
        out_shape=[jax.ShapeDtypeStruct((n, 2 * rank + 16, width), down.dtype) for n in shapes],
        in_specs=[SMEM] * len(scalars) + [HBM, HBM],
        out_specs=[VMEM] * len(shapes),
        scratch_shapes=[
            pltpu.VMEM((2 * count, rank, lanes), up.dtype),
            pltpu.SemaphoreType.DMA((2 * count,)),
            pltpu.SemaphoreType.DMA((2 * count,)),
        ],
        compiler_params=pltpu.CompilerParams(vmem_limit_bytes=limit << 20),
        cost_estimate=pl.CostEstimate(
            flops=0, bytes_accessed=count * rank * (width + lanes) * 8, transcendentals=0
        ),
    )(*scalars, down, up)


def vmem_call(kernel, shapes, dtype, scalars, arrays, limit=10):
    return pl.pallas_call(
        kernel,
        out_shape=[jax.ShapeDtypeStruct(shape, dtype) for shape in shapes],
        in_specs=[SMEM] * len(scalars) + [VMEM] * len(arrays),
        out_specs=[VMEM] * len(shapes),
        compiler_params=pltpu.CompilerParams(vmem_limit_bytes=limit << 20),
        cost_estimate=pl.CostEstimate(
            flops=0,
            bytes_accessed=sum(math.prod(shape) for shape in shapes) * 4,
            transcendentals=0,
        ),
    )(*scalars, *arrays)


def move(dst, src):
    rows = src.shape[0]

    def body(i, carry):
        at = pl.ds(pl.multiple_of(i * 16, 16), 16)
        dst[at, :] = src[at, :]
        return carry

    lax.fori_loop(0, rows // 16, body, 0, unroll=3)


def relay_kernel(offsets, *refs):
    fresh, near, outs = refs[:4], refs[4:8], refs[8:]
    for i in range(4):
        at = offsets[i // 2]
        close = 1 if i % 2 == 0 else 3
        for source, when in ((near[i], at != close), (fresh[i], at == close)):

            @pl.when(when)
            def _(source=source, out=outs[i]):
                for u in range(2):
                    move(out.at[u], source.at[u])


def line_kernel(offsets, *refs):
    outs = refs[10:]
    for h in range(2):
        own, plus_a, minus_a, plus_b, minus_b = refs[5 * h : 5 * h + 5]
        out = outs[4 * h : 4 * h + 4]
        at = offsets[h]
        low, high = own.at[pl.ds(0, 2)], own.at[pl.ds(2, 2)]
        plus_b, minus_b = plus_b.at[pl.ds(2, 2)], minus_b.at[pl.ds(2, 2)]
        picks = ((low, high), (plus_a, plus_b), (plus_a, minus_a), (minus_a, minus_b))
        for offset, (first, second) in enumerate(picks):

            @pl.when(at == offset)
            def _(first=first, second=second, out=out):
                for u in range(2):
                    move(out[u], first.at[u])
                    move(out[2 + u], second.at[u])


def pick_kernel(offsets, *refs):
    for h in range(2):
        at = offsets[1 - h]
        for offset, source in enumerate(refs[4 * h : 4 * h + 4]):

            @pl.when(at == offset)
            def _(source=source, out=refs[8 + h]):
                move(out, source)


def paired(hidden, mine, i, pairs, cap, first, second):
    spots = [pl.multiple_of(mine[ORDER, j] * cap, cap) for j in (i, i + pairs)]
    rows = jnp.concatenate([hidden[pl.ds(spot, cap), :] for spot in spots], axis=0)
    product = lax.dot_general(
        rows,
        jnp.concatenate([first, second], axis=0),
        (((1,), (1,)), ((), ())),
        preferred_element_type=jnp.float32,
    )
    lane = lax.broadcasted_iota(jnp.int32, (cap, product.shape[1]), 1)
    return jnp.where(lane < first.shape[0], product[:cap], product[cap:])


def low_main_kernel(cap, mine, hidden, main, out):
    rank = out.shape[1] // 2
    pairs = out.shape[0] // cap

    def weights(j):
        place = mine[PLACE, j]
        unit = lax.div(place, 2)
        return main[unit, pl.ds(pl.multiple_of((place - 2 * unit) * rank, rank), rank), :]

    def body(i, carry):
        at = pl.ds(pl.multiple_of(i * cap, cap), cap)
        out[at, :] = paired(hidden, mine, i, pairs, cap, weights(i), weights(i + pairs))
        return carry

    lax.fori_loop(0, pairs, body, 0, unroll=2)


def low_extra_kernel(first, cap, mine, hidden, *refs):
    extras, out = refs[:-1], refs[-1]
    rank = out.shape[1] // 2
    for i in range(2):
        spots = [pl.multiple_of(mine[ORDER, first + 2 * u + i] * cap, cap) for u in range(2)]
        rows = jnp.concatenate([hidden[pl.ds(spot, cap), :] for spot in spots], axis=0)
        part = slice(i * rank, (i + 1) * rank)
        product = lax.dot_general(
            rows,
            jnp.concatenate([extras[0][part, :], extras[1][part, :]], axis=0),
            (((1,), (1,)), ((), ())),
            preferred_element_type=jnp.float32,
        )
        lane = lax.broadcasted_iota(jnp.int32, (cap, 2 * rank), 1)
        out[i * cap : (i + 1) * cap, :] = jnp.where(lane < rank, product[:cap], product[cap:])


def low_partial(kernel, pairs, cap, rank, mine, hidden, weights):
    return pl.pallas_call(
        kernel,
        out_shape=jax.ShapeDtypeStruct((pairs * cap, 2 * rank), jnp.float32),
        in_specs=[SMEM] + [VMEM] * (1 + len(weights)),
        out_specs=VMEM,
        compiler_params=pltpu.CompilerParams(vmem_limit_bytes=10 << 20),
        cost_estimate=pl.CostEstimate(
            flops=pairs * cap * rank * 4 * hidden.shape[1],
            bytes_accessed=sum(w.size for w in weights) * 2,
            transcendentals=0,
        ),
    )(mine, hidden, *weights)


def low_rank_rounds(partial):
    tp_count = lax.axis_size("tp")
    chips = tp_count // 2
    t = lax.axis_index("tp")
    z, core = t // 2, t % 2
    half = partial.shape[0] // 2
    piece = half // chips
    swap = [(i, i ^ 1) for i in range(tp_count)]
    turn = lambda d: [(i, (i + 2 * d) % tp_count) for i in range(tp_count)]
    cut = lambda array, start, size: lax.dynamic_slice_in_dim(array, start, size, 0)
    total = cut(partial, core * half, half) + lax.ppermute(
        cut(partial, (1 - core) * half, half), "tp", swap
    )
    pieces = [
        lax.ppermute(cut(total, (z + d) % chips * piece, piece), "tp", turn(d))
        for d in range(1, chips)
    ]
    summed = (cut(total, z * piece, piece) + sum(pieces)).astype(jnp.bfloat16)
    own = jnp.stack([summed] + [lax.ppermute(summed, "tp", turn(d)) for d in range(1, chips)])
    return own, lax.ppermute(own, "tp", swap)


def low_rank_doubling(partial):
    tp_count = lax.axis_size("tp")
    last = tp_count // 2 - 1
    z_of = lambda i: i // 2
    for partner in (
        lambda i: i ^ 1,
        lambda i: (z_of(i) ^ 1) * 2 + i % 2,
        lambda i: (last - z_of(i)) * 2 + i % 2,
    ):
        partial += lax.ppermute(partial, "tp", [(i, partner(i)) for i in range(tp_count)])
    return partial


def blend(base, out, counts, mine, j, both, ups, cap):
    rank = both.shape[1] // 2
    lane = lax.broadcasted_iota(jnp.int32, both.shape, 1)
    none = jnp.zeros_like(both)
    left = jnp.concatenate(
        [jnp.where(lane < rank, both, none), jnp.where(lane < rank, none, both)], axis=0
    )
    delta = jnp.dot(left, jnp.concatenate(ups, axis=0), preferred_element_type=jnp.float32)
    rows = lax.broadcasted_iota(jnp.int32, (cap, base.shape[1]), 0)
    for n in range(2):
        g = mine[ORDER, j[n]]
        here = pl.ds(pl.multiple_of(g * cap, cap), cap)
        merged = base[here, :] + ADAPTER_SCALE * delta[n * cap : (n + 1) * cap]
        out(n, here, jnp.where(rows < counts[g], merged, 0.0).astype(jnp.bfloat16))


def out_main_kernel(where, mine, counts, base, own, other, main, out, low):
    groups = counts.shape[0]
    cap = base.shape[0] // groups
    chips, piece, rank = own.shape[0], own.shape[1], own.shape[2] // 2
    lanes = base.shape[1]
    z, core = where[0], where[1]
    steps = rank // 16
    pairs = low.shape[0] // cap
    for d in range(chips):
        quarter = lax.rem(z - d + chips, chips)
        for ref, half in ((own, core), (other, 1 - core)):
            at = pl.multiple_of((half * chips + quarter) * piece, 16)
            low[pl.ds(at, piece), :] = ref[d]

    def up(j):
        place = mine[PLACE, j]
        unit = lax.div(place, 2)
        at = (place - 2 * unit) * steps * lanes
        return [
            main[unit, :, pl.ds(pl.multiple_of(at + part * lanes, lanes), lanes)]
            for part in range(steps)
        ]

    def store(n, here, value):
        out[here, :] = value

    def body(i, carry):
        both = low[pl.ds(pl.multiple_of(i * cap, cap), cap), :]
        spots = (i, i + pairs)
        blend(base, store, counts, mine, spots, both, up(i) + up(i + pairs), cap)
        return carry

    lax.fori_loop(0, pairs, body, 0, unroll=2)


def out_extra_kernel(mine, counts, base, low, first_pack, second_pack, _, out, blocks, sems):
    groups = counts.shape[0]
    cap = base.shape[0] // groups
    rank = low.shape[1] // 2
    lanes = base.shape[1]
    steps = rank // 16
    first = groups - EXTRA
    copies = []
    for i in range(2):
        both = low[i * cap : (i + 1) * cap, :].astype(jnp.bfloat16)
        ups = [
            pack[:, (i * steps + part) * lanes : (i * steps + part + 1) * lanes]
            for pack in (first_pack, second_pack)
            for part in range(steps)
        ]

        def store(n, here, value, i=i):
            blocks[2 * i + n] = value
            copy = pltpu.make_async_copy(
                blocks.at[2 * i + n], out.at[here, :], sems.at[2 * i + n]
            )
            copy.start()
            copies.append(copy)

        blend(base, store, counts, mine, (first + i, first + 2 + i), both, ups, cap)
    for copy in copies:
        copy.wait()


def whole(array):
    return pl.BlockSpec(array.shape, lambda i: (0,) * array.ndim)


def combine_main(where, mine, counts, base, own, other, main, rank):
    packs = pl.BlockSpec((main.shape[0], 16, main.shape[2]), lambda i: (0, rank // 8, 0))
    return pl.pallas_call(
        out_main_kernel,
        grid=(1,),
        out_shape=jax.ShapeDtypeStruct(base.shape, jnp.bfloat16),
        in_specs=[SMEM, SMEM, SMEM, whole(base), whole(own), whole(other), packs],
        out_specs=whole(base),
        scratch_shapes=[
            pltpu.VMEM((2 * own.shape[0] * own.shape[1], own.shape[2]), jnp.bfloat16)
        ],
        compiler_params=pltpu.CompilerParams(vmem_limit_bytes=6 << 20),
        cost_estimate=pl.CostEstimate(
            flops=base.size * rank * 2, bytes_accessed=base.size * 8, transcendentals=0
        ),
    )(where, mine, counts, base, own, other, main)


def combine_extra(mine, counts, base, low, extras, out, rank):
    pack = pl.BlockSpec((16, extras[0].shape[1]), lambda i: (rank // 8, 0))
    cap = base.shape[0] // counts.shape[0]
    return pl.pallas_call(
        out_extra_kernel,
        grid=(1,),
        out_shape=jax.ShapeDtypeStruct(out.shape, out.dtype),
        in_specs=[SMEM, SMEM, whole(base), whole(low), pack, pack, HBM],
        out_specs=HBM,
        input_output_aliases={6: 0},
        scratch_shapes=[
            pltpu.VMEM((EXTRA, cap, base.shape[1]), jnp.bfloat16),
            pltpu.SemaphoreType.DMA((EXTRA,)),
        ],
        compiler_params=pltpu.CompilerParams(vmem_limit_bytes=4 << 20),
        cost_estimate=pl.CostEstimate(
            flops=base.size * rank // 4, bytes_accessed=base.size * 4, transcendentals=0
        ),
    )(mine, counts, base, low, *extras, out)


def on_device(
    hidden,
    value_weight,
    down_weights,
    up_weights,
    group_adapter_id,
    adapter_storage_row,
    group_live_count,
):
    dp_count = lax.axis_size("dp")
    me = lax.axis_index("dp")
    owned, rank, width = down_weights.shape
    groups = group_adapter_id.shape[0] // dp_count
    cap = hidden.shape[0] // groups
    me_row = me.astype(jnp.int32).reshape(1)
    served, mine = index_tables(me_row, group_adapter_id, adapter_storage_row, dp_count)
    counts = lax.dynamic_slice_in_dim(group_live_count, me * groups, groups)

    def wide(hidden, value_weight, down_weights, up_weights):
        stored = adapter_storage_row[group_adapter_id]
        owners = (stored // owned).reshape(dp_count, groups)
        slots = (stored % owned).reshape(dp_count, groups)
        same = owners[:, :, None] == owners[:, None, :]
        earlier = jnp.arange(groups)[None, None, :] < jnp.arange(groups)[None, :, None]
        ranking = jnp.sum(same & earlier, axis=2)
        hits = (owners == me)[:, :, None] & (ranking[:, :, None] == jnp.arange(MOST))
        rows = jnp.sum(jnp.where(hits, slots[:, :, None], 0), axis=1).reshape(-1)
        my_owners = lax.dynamic_index_in_dim(owners, me, 0, keepdims=False)
        my_ranking = lax.dynamic_index_in_dim(ranking, me, 0, keepdims=False)
        base_terms = jnp.dot(hidden, value_weight, preferred_element_type=jnp.float32)
        base = lax.psum_scatter(base_terms, "tp", scatter_dimension=1, tiled=True)
        downs = lax.all_to_all(down_weights[rows], "dp", 0, 0, tiled=True)
        ups = lax.all_to_all(up_weights[rows], "dp", 0, 0, tiled=True)
        picked = my_owners * MOST + my_ranking
        partial = jnp.einsum(
            "gcd,grd->gcr",
            hidden.reshape(groups, cap, width),
            downs[picked],
            preferred_element_type=jnp.float32,
        )
        low = low_rank_sum(partial.reshape(groups * cap, rank))
        return finish(base, low, ups[picked], counts)

    def narrow(hidden, value_weight, down_weights, up_weights):
        side = math.isqrt(dp_count)
        hot = mine[FLAGS, HOT]
        a = (me // side - hot // side) % side
        b = (me % side - hot % side) % side
        offsets = jnp.stack([a, b]).astype(jnp.int32)
        trees = (True, False)
        soon = [
            (tree, ((2, part[0]), (2, part[1]), (near, 2), (near, 3)))
            for tree in trees
            for near, part in ((1, (0, 1)), (3, (2, 3)))
        ]
        late = [(tree, ((near, 0), (near, 1))) for tree in trees for near in (1, 3)]
        late += [(tree, ((0, 0), (0, 1), (0, 2), (0, 3))) for tree in trees]
        moves = ((1, 0), (-1, 0), (0, 1), (0, -1))
        turned = ((0, 1), (0, 2), (0, -1), (1, 0), (2, 0), (-1, 0))
        send = lambda values, ways: [shift(v, *way) for v, way in zip(values, ways)]
        barrier = lax.optimization_barrier
        (main_sent,) = gather_call(
            main_kernel, (dp_count,), dp_count, (served,), down_weights, up_weights
        )
        main = lax.all_to_all(main_sent, "dp", 0, 0, tiled=True)
        unit = main_sent.shape[1:]
        dtype = main_sent.dtype
        gathered = gather_call(
            functools.partial(extra_kernel, soon),
            (4,) * 4,
            16,
            (me_row, served, mine),
            down_weights,
            up_weights,
            40,
        )
        later_served, _ = barrier((served, gathered))
        later = gather_call(
            functools.partial(extra_kernel, late),
            (2,) * 4 + (4,) * 2,
            16,
            (me_row, later_served, mine),
            down_weights,
            up_weights,
            40,
        )
        base_terms = jnp.dot(hidden, value_weight, preferred_element_type=jnp.float32)
        main, gathered, later, base_terms = barrier((main, gathered, later, base_terms))
        fresh = send(gathered, moves)
        base = lax.psum_scatter(base_terms, "tp", scatter_dimension=1, tiled=True)
        pairs = (groups - EXTRA) // 2
        partial = low_partial(
            functools.partial(low_main_kernel, cap), pairs, cap, rank, mine, hidden, (main,)
        )
        own, other = low_rank_rounds(partial)
        t = lax.axis_index("tp")
        where = jnp.stack([t // 2, t % 2]).astype(jnp.int32)
        out = combine_main(where, mine, counts, base, own, other, main, rank)
        fresh, near, _ = barrier((fresh, later[:4], partial))
        relayed = vmem_call(
            relay_kernel, ((2,) + unit,) * 4, dtype, (offsets,), (*fresh, *near)
        )
        near_a = barrier(send(relayed, moves))
        tree_arrays = [
            (later[4 + h], near_a[2 * h], near_a[2 * h + 1], fresh[2 * h], fresh[2 * h + 1])
            for h in range(2)
        ]
        lines = vmem_call(
            line_kernel, (unit,) * 8, dtype, (offsets,), tree_arrays[0] + tree_arrays[1]
        )
        got = send(lines[1:4] + lines[5:8], turned)
        got, out = barrier((got, out))
        extras = vmem_call(
            pick_kernel,
            (unit,) * 2,
            dtype,
            (offsets,),
            (lines[0], *got[:3], lines[4], *got[3:]),
        )
        extra_partial = low_partial(
            functools.partial(low_extra_kernel, groups - EXTRA, cap),
            EXTRA // 2,
            cap,
            rank,
            mine,
            hidden,
            extras,
        )
        extra_low = low_rank_doubling(extra_partial)
        return combine_extra(mine, counts, base, extra_low, extras, out, rank)

    return lax.cond(
        mine[FLAGS, FITS] == 1, narrow, wide, hidden, value_weight, down_weights, up_weights
    )


def solution(mesh):
    return jax.shard_map(
        on_device,
        mesh=mesh,
        in_specs=(
            P("dp", "tp"),
            P("tp", None),
            P("dp", None, "tp"),
            P("dp", None, "tp"),
            P(),
            P(),
            P(),
        ),
        out_specs=P("dp", "tp"),
        check_vma=False,
    )
```

```python
import functools
import math

import jax
import jax.numpy as jnp
from jax import lax
from jax.experimental import pallas as pl
from jax.experimental.pallas import tpu as pltpu
from jax.sharding import PartitionSpec as P

ADAPTER_SCALE = 0.5
MAIN = 2
MOST = 6
EXTRA = MOST - MAIN


def low_rank_sum(partial):
    rows, rank = partial.shape
    tp_count = lax.axis_size("tp")
    pieces = lax.all_to_all(partial, "tp", split_axis=0, concat_axis=0, tiled=True)
    mine = jnp.sum(pieces.reshape(tp_count, rows // tp_count, rank), axis=0).astype(jnp.bfloat16)
    return lax.all_gather(mine, "tp", axis=0, tiled=True)


def finish(base, low, ups, counts):
    groups = counts.shape[0]
    cap = base.shape[0] // groups
    delta = jnp.einsum(
        "gcr,grv->gcv", low.reshape(groups, cap, -1), ups, preferred_element_type=jnp.float32
    )
    merged = base.reshape(groups, cap, -1) + ADAPTER_SCALE * delta
    active = jnp.arange(cap)[None, :, None] < counts[:, None, None]
    out = jnp.where(active, merged, jnp.float32(0.0)).astype(jnp.bfloat16)
    return out.reshape(base.shape)


SMEM = pl.BlockSpec(memory_space=pltpu.SMEM)
VMEM = pl.BlockSpec(memory_space=pltpu.VMEM)
HBM = pl.BlockSpec(memory_space=pltpu.HBM)
LANES = 128
ORDER, PLACE, FLAGS = 0, 1, 2
HOT, FITS = 0, 1


def shift(value, dx, dy):
    side = math.isqrt(lax.axis_size("dp"))
    pairs = [
        (x * side + y, (x + dx) % side * side + (y + dy) % side)
        for x in range(side)
        for y in range(side)
    ]
    return lax.ppermute(value, "dp", pairs)


def index_kernel(me_ref, ids_ref, table_ref, served_ref, mine_ref, owner_ref, rank_ref):
    total = ids_ref.shape[0]
    dp_count = served_ref.shape[0]
    groups = total // dp_count
    chunks = table_ref.shape[0]
    owned = chunks * LANES // dp_count
    me = me_ref[0]
    f32, bf16 = jnp.float32, jnp.bfloat16
    ids = ids_ref[...]
    lane = lax.broadcasted_iota(jnp.int32, (total, LANES), 1)
    found = jnp.zeros((total, LANES), jnp.int32)
    for c in range(chunks):
        found += jnp.where(ids == lane + c * LANES, table_ref[c : c + 1, :], 0)
    stored = jnp.sum(found, axis=1, keepdims=True)
    owner = lax.div(stored, owned)
    slot = stored - owner * owned
    holds = jnp.where(owner == lane, 1.0, 0.0)
    low = lax.broadcasted_iota(jnp.int32, (groups, groups), 0)
    low = jnp.where(low > lax.broadcasted_iota(jnp.int32, (groups, groups), 1), 1.0, 0.0)
    low = low.astype(bf16)
    holds16 = holds.astype(bf16)
    before = jnp.concatenate(
        [
            jnp.dot(low, holds16[r * groups : (r + 1) * groups], preferred_element_type=f32)
            for r in range(dp_count)
        ],
        axis=0,
    )
    ranking = jnp.sum(before * holds, axis=1, keepdims=True).astype(jnp.int32)
    owner_ref[...] = jnp.broadcast_to(owner, (total, LANES))
    rank_ref[...] = jnp.broadcast_to(ranking, (total, LANES))
    block_of = lax.div(lax.broadcasted_iota(jnp.int32, (dp_count, total), 1), groups)
    block = block_of == lax.broadcasted_iota(jnp.int32, (dp_count, total), 0)
    block = jnp.where(block, 1.0, 0.0).astype(bf16)
    loads = jnp.dot(block, holds16, preferred_element_type=f32)
    kept = jnp.where((owner == me) & (ranking == lane), slot, 0).astype(f32).astype(bf16)
    served_ref[...] = jnp.dot(block, kept, preferred_element_type=f32).astype(jnp.int32)
    least = jnp.min(loads, axis=0, keepdims=True)
    row_lane = lax.broadcasted_iota(jnp.int32, (1, LANES), 1)
    hot = jnp.min(jnp.where(least >= MOST, row_lane, LANES), axis=1, keepdims=True)
    spare = jnp.where(row_lane == hot, 0.0, loads)
    most = jnp.max(jnp.max(spare, axis=0, keepdims=True), axis=1, keepdims=True)
    fits = jnp.where(most <= MAIN, 1, 0)
    at = pl.ds(pl.multiple_of(me * groups, groups), groups)
    my_owner = owner_ref[at, :]
    my_rank = rank_ref[at, :]
    late = (my_owner == hot) & (my_rank >= MAIN)
    place = jnp.where(late, dp_count * MAIN + my_rank - MAIN, my_owner * MAIN + my_rank)
    early = jnp.where(late, 0.0, 1.0).astype(bf16)
    ahead = jnp.dot(low, early, preferred_element_type=f32).astype(jnp.int32)
    turn = jnp.where(late, groups - EXTRA + my_rank - MAIN, ahead)
    group_lane = lax.broadcasted_iota(jnp.int32, (groups, LANES), 1)
    group = lax.broadcasted_iota(jnp.int32, (groups, LANES), 0)
    here = turn == group_lane
    mine_ref[...] = jnp.zeros(mine_ref.shape, jnp.int32)
    mine_ref[ORDER : ORDER + 1, :] = jnp.sum(jnp.where(here, group, 0), axis=0, keepdims=True)
    mine_ref[PLACE : PLACE + 1, :] = jnp.sum(jnp.where(here, place, 0), axis=0, keepdims=True)
    mine_ref[FLAGS : FLAGS + 1, :] = jnp.where(
        row_lane == HOT, hot, jnp.where(row_lane == FITS, fits, 0)
    )


def index_tables(me, ids, table, dp_count):
    total = ids.shape[0]
    return pl.pallas_call(
        index_kernel,
        out_shape=(
            jax.ShapeDtypeStruct((dp_count, LANES), jnp.int32),
            jax.ShapeDtypeStruct((8, LANES), jnp.int32),
        ),
        in_specs=[SMEM, VMEM, VMEM],
        out_specs=(VMEM, VMEM),
        scratch_shapes=[pltpu.VMEM((total, LANES), jnp.int32)] * 2,
        compiler_params=pltpu.CompilerParams(vmem_limit_bytes=8 << 20),
    )(me, ids.reshape(total, 1), table.reshape(-1, LANES))


def copy_units(wanted, down, up, up_in, down_sem, up_sem):
    rank = down.shape[1]
    lanes = up.shape[2]
    steps = rank // 16
    downs, ups = [], []
    for i, (dest, index, rows) in enumerate(wanted):
        for half in range(2):
            n = 2 * i + half
            ups.append(pltpu.make_async_copy(up.at[rows[half]], up_in.at[n], up_sem.at[n]))
            ups[-1].start()
            downs.append(
                pltpu.make_async_copy(
                    down.at[rows[half]], dest.at[index, pl.ds(half * rank, rank)], down_sem.at[n]
                )
            )
            downs[-1].start()
    for i, (dest, index, rows) in enumerate(wanted):
        for half in range(2):
            n = 2 * i + half
            ups[n].wait()
            for part in range(steps):
                at = (half * steps + part) * lanes
                dest[index, 2 * rank : 2 * rank + 16, at : at + lanes] = up_in[
                    n, part * 16 : part * 16 + 16, :
                ]
    for copy in downs:
        copy.wait()


def main_kernel(served, down, up, out, *scratch):
    wanted = [(out, p, (served[p, 0], served[p, 1])) for p in range(out.shape[0])]
    copy_units(wanted, down, up, *scratch)


def extra_kernel(lines, me, served, mine, down, up, *refs):
    outs, scratch = refs[: len(lines)], refs[len(lines) :]
    dp_count = served.shape[0]
    side = math.isqrt(dp_count)
    hot = mine[FLAGS, HOT]

    @pl.when(hot == me[0])
    def _():
        hot_x, hot_y = lax.div(hot, side), lax.rem(hot, side)
        wanted = []
        for out, (x_first, units) in zip(outs, lines):
            for i, (a, b) in enumerate(units):
                dx, dy = (a, b) if x_first else (b, a)
                peer = lax.rem(hot_x + dx, side) * side + lax.rem(hot_y + dy, side)
                first = MAIN if x_first else MAIN + 2
                wanted.append((out, i, (served[peer, first], served[peer, first + 1])))
        copy_units(wanted, down, up, *scratch)


def gather_call(kernel, shapes, count, scalars, down, up, limit=8):
    _, rank, width = down.shape
    lanes = up.shape[2]
    return pl.pallas_call(
        kernel,
        out_shape=[jax.ShapeDtypeStruct((n, 2 * rank + 16, width), down.dtype) for n in shapes],
        in_specs=[SMEM] * len(scalars) + [HBM, HBM],
        out_specs=[VMEM] * len(shapes),
        scratch_shapes=[
            pltpu.VMEM((2 * count, rank, lanes), up.dtype),
            pltpu.SemaphoreType.DMA((2 * count,)),
            pltpu.SemaphoreType.DMA((2 * count,)),
        ],
        compiler_params=pltpu.CompilerParams(vmem_limit_bytes=limit << 20),
        cost_estimate=pl.CostEstimate(
            flops=0, bytes_accessed=count * rank * (width + lanes) * 8, transcendentals=0
        ),
    )(*scalars, down, up)


def vmem_call(kernel, shapes, dtype, scalars, arrays, limit=10):
    return pl.pallas_call(
        kernel,
        out_shape=[jax.ShapeDtypeStruct(shape, dtype) for shape in shapes],
        in_specs=[SMEM] * len(scalars) + [VMEM] * len(arrays),
        out_specs=[VMEM] * len(shapes),
        compiler_params=pltpu.CompilerParams(vmem_limit_bytes=limit << 20),
        cost_estimate=pl.CostEstimate(
            flops=0,
            bytes_accessed=sum(math.prod(shape) for shape in shapes) * 4,
            transcendentals=0,
        ),
    )(*scalars, *arrays)


def move(dst, src):
    rows = src.shape[0]

    def body(i, carry):
        at = pl.ds(pl.multiple_of(i * 16, 16), 16)
        dst[at, :] = src[at, :]
        return carry

    lax.fori_loop(0, rows // 16, body, 0, unroll=3)


def relay_kernel(offsets, *refs):
    fresh, near, outs = refs[:4], refs[4:8], refs[8:]
    for i in range(4):
        at = offsets[i // 2]
        close = 1 if i % 2 == 0 else 3
        for source, when in ((near[i], at != close), (fresh[i], at == close)):

            @pl.when(when)
            def _(source=source, out=outs[i]):
                for u in range(2):
                    move(out.at[u], source.at[u])


def line_kernel(offsets, *refs):
    outs = refs[10:]
    for h in range(2):
        own, plus_a, minus_a, plus_b, minus_b = refs[5 * h : 5 * h + 5]
        out = outs[4 * h : 4 * h + 4]
        at = offsets[h]
        low, high = own.at[pl.ds(0, 2)], own.at[pl.ds(2, 2)]
        plus_b, minus_b = plus_b.at[pl.ds(2, 2)], minus_b.at[pl.ds(2, 2)]
        picks = ((low, high), (plus_a, plus_b), (plus_a, minus_a), (minus_a, minus_b))
        for offset, (first, second) in enumerate(picks):

            @pl.when(at == offset)
            def _(first=first, second=second, out=out):
                for u in range(2):
                    move(out[u], first.at[u])
                    move(out[2 + u], second.at[u])


def pick_kernel(offsets, *refs):
    for h in range(2):
        at = offsets[1 - h]
        for offset, source in enumerate(refs[4 * h : 4 * h + 4]):

            @pl.when(at == offset)
            def _(source=source, out=refs[8 + h]):
                move(out, source)


def paired(hidden, mine, i, pairs, cap, first, second):
    spots = [pl.multiple_of(mine[ORDER, j] * cap, cap) for j in (i, i + pairs)]
    rows = jnp.concatenate([hidden[pl.ds(spot, cap), :] for spot in spots], axis=0)
    product = lax.dot_general(
        rows,
        jnp.concatenate([first, second], axis=0),
        (((1,), (1,)), ((), ())),
        preferred_element_type=jnp.float32,
    )
    lane = lax.broadcasted_iota(jnp.int32, (cap, product.shape[1]), 1)
    return jnp.where(lane < first.shape[0], product[:cap], product[cap:])


def low_main_kernel(cap, mine, hidden, main, out):
    rank = out.shape[1] // 2
    pairs = out.shape[0] // cap

    def weights(j):
        place = mine[PLACE, j]
        unit = lax.div(place, 2)
        return main[unit, pl.ds(pl.multiple_of((place - 2 * unit) * rank, rank), rank), :]

    def body(i, carry):
        at = pl.ds(pl.multiple_of(i * cap, cap), cap)
        out[at, :] = paired(hidden, mine, i, pairs, cap, weights(i), weights(i + pairs))
        return carry

    lax.fori_loop(0, pairs, body, 0, unroll=2)


def low_extra_kernel(first, cap, mine, hidden, *refs):
    extras, out = refs[:-1], refs[-1]
    rank = out.shape[1] // 2
    for i in range(2):
        spots = [pl.multiple_of(mine[ORDER, first + 2 * u + i] * cap, cap) for u in range(2)]
        rows = jnp.concatenate([hidden[pl.ds(spot, cap), :] for spot in spots], axis=0)
        part = slice(i * rank, (i + 1) * rank)
        product = lax.dot_general(
            rows,
            jnp.concatenate([extras[0][part, :], extras[1][part, :]], axis=0),
            (((1,), (1,)), ((), ())),
            preferred_element_type=jnp.float32,
        )
        lane = lax.broadcasted_iota(jnp.int32, (cap, 2 * rank), 1)
        out[i * cap : (i + 1) * cap, :] = jnp.where(lane < rank, product[:cap], product[cap:])


def low_partial(kernel, pairs, cap, rank, mine, hidden, weights):
    return pl.pallas_call(
        kernel,
        out_shape=jax.ShapeDtypeStruct((pairs * cap, 2 * rank), jnp.float32),
        in_specs=[SMEM] + [VMEM] * (1 + len(weights)),
        out_specs=VMEM,
        compiler_params=pltpu.CompilerParams(vmem_limit_bytes=10 << 20),
        cost_estimate=pl.CostEstimate(
            flops=pairs * cap * rank * 4 * hidden.shape[1],
            bytes_accessed=sum(w.size for w in weights) * 2,
            transcendentals=0,
        ),
    )(mine, hidden, *weights)


def turn(step):
    tp_count = lax.axis_size("tp")
    return [(i, (i + 2 * step) % tp_count) for i in range(tp_count)]


def swap():
    return [(i, i ^ 1) for i in range(lax.axis_size("tp"))]


def low_rank_down(partial):
    chips = lax.axis_size("tp") // 2
    t = lax.axis_index("tp")
    z, core = t // 2, t % 2
    half = partial.shape[0] // 2
    piece = half // chips
    cut = lambda array, start, size: lax.dynamic_slice_in_dim(array, start, size, 0)
    total = cut(partial, core * half, half) + lax.ppermute(
        cut(partial, (1 - core) * half, half), "tp", swap()
    )
    pieces = [
        lax.ppermute(cut(total, (z + d) % chips * piece, piece), "tp", turn(d))
        for d in range(1, chips)
    ]
    return (cut(total, z * piece, piece) + sum(pieces)).astype(jnp.bfloat16)


def low_rank_up(summed):
    chips = lax.axis_size("tp") // 2
    own = jnp.stack([summed] + [lax.ppermute(summed, "tp", turn(d)) for d in range(1, chips)])
    return own, lax.ppermute(own, "tp", swap())


def low_rank_doubling(partial):
    tp_count = lax.axis_size("tp")
    last = tp_count // 2 - 1
    z_of = lambda i: i // 2
    for partner in (
        lambda i: i ^ 1,
        lambda i: (z_of(i) ^ 1) * 2 + i % 2,
        lambda i: (last - z_of(i)) * 2 + i % 2,
    ):
        partial += lax.ppermute(partial, "tp", [(i, partner(i)) for i in range(tp_count)])
    return partial


def blend(base, out, counts, mine, j, both, ups, cap):
    rank = both.shape[1] // 2
    lane = lax.broadcasted_iota(jnp.int32, both.shape, 1)
    none = jnp.zeros_like(both)
    left = jnp.concatenate(
        [jnp.where(lane < rank, both, none), jnp.where(lane < rank, none, both)], axis=0
    )
    delta = jnp.dot(left, jnp.concatenate(ups, axis=0), preferred_element_type=jnp.float32)
    rows = lax.broadcasted_iota(jnp.int32, (cap, base.shape[1]), 0)
    for n in range(2):
        g = mine[ORDER, j[n]]
        here = pl.ds(pl.multiple_of(g * cap, cap), cap)
        merged = base[here, :] + ADAPTER_SCALE * delta[n * cap : (n + 1) * cap]
        out(n, here, jnp.where(rows < counts[g], merged, 0.0).astype(jnp.bfloat16))


def out_main_kernel(where, mine, counts, base, own, other, main, out, low):
    groups = counts.shape[0]
    cap = base.shape[0] // groups
    chips, piece, rank = own.shape[0], own.shape[1], own.shape[2] // 2
    lanes = base.shape[1]
    z, core = where[0], where[1]
    steps = rank // 16
    pairs = low.shape[0] // cap
    for d in range(chips):
        quarter = lax.rem(z - d + chips, chips)
        for ref, half in ((own, core), (other, 1 - core)):
            at = pl.multiple_of((half * chips + quarter) * piece, 16)
            low[pl.ds(at, piece), :] = ref[d]

    def up(j):
        place = mine[PLACE, j]
        unit = lax.div(place, 2)
        at = (place - 2 * unit) * steps * lanes
        return [
            main[unit, :, pl.ds(pl.multiple_of(at + part * lanes, lanes), lanes)]
            for part in range(steps)
        ]

    def store(n, here, value):
        out[here, :] = value

    def body(i, carry):
        both = low[pl.ds(pl.multiple_of(i * cap, cap), cap), :]
        spots = (i, i + pairs)
        blend(base, store, counts, mine, spots, both, up(i) + up(i + pairs), cap)
        return carry

    lax.fori_loop(0, pairs, body, 0, unroll=2)


def out_extra_kernel(mine, counts, base, low, first_pack, second_pack, _, out, blocks, sems):
    groups = counts.shape[0]
    cap = base.shape[0] // groups
    rank = low.shape[1] // 2
    lanes = base.shape[1]
    steps = rank // 16
    first = groups - EXTRA
    copies = []
    for i in range(2):
        both = low[i * cap : (i + 1) * cap, :].astype(jnp.bfloat16)
        ups = [
            pack[:, (i * steps + part) * lanes : (i * steps + part + 1) * lanes]
            for pack in (first_pack, second_pack)
            for part in range(steps)
        ]

        def store(n, here, value, i=i):
            blocks[2 * i + n] = value
            copy = pltpu.make_async_copy(
                blocks.at[2 * i + n], out.at[here, :], sems.at[2 * i + n]
            )
            copy.start()
            copies.append(copy)

        blend(base, store, counts, mine, (first + i, first + 2 + i), both, ups, cap)
    for copy in copies:
        copy.wait()


def whole(array):
    return pl.BlockSpec(array.shape, lambda i: (0,) * array.ndim)


def combine_main(where, mine, counts, base, own, other, main, rank):
    packs = pl.BlockSpec((main.shape[0], 16, main.shape[2]), lambda i: (0, rank // 8, 0))
    return pl.pallas_call(
        out_main_kernel,
        grid=(1,),
        out_shape=jax.ShapeDtypeStruct(base.shape, jnp.bfloat16),
        in_specs=[SMEM, SMEM, SMEM, whole(base), whole(own), whole(other), packs],
        out_specs=whole(base),
        scratch_shapes=[
            pltpu.VMEM((2 * own.shape[0] * own.shape[1], own.shape[2]), jnp.bfloat16)
        ],
        compiler_params=pltpu.CompilerParams(vmem_limit_bytes=6 << 20),
        cost_estimate=pl.CostEstimate(
            flops=base.size * rank * 2, bytes_accessed=base.size * 8, transcendentals=0
        ),
    )(where, mine, counts, base, own, other, main)


def combine_extra(mine, counts, base, low, extras, out, rank):
    pack = pl.BlockSpec((16, extras[0].shape[1]), lambda i: (rank // 8, 0))
    cap = base.shape[0] // counts.shape[0]
    return pl.pallas_call(
        out_extra_kernel,
        grid=(1,),
        out_shape=jax.ShapeDtypeStruct(out.shape, out.dtype),
        in_specs=[SMEM, SMEM, whole(base), whole(low), pack, pack, HBM],
        out_specs=HBM,
        input_output_aliases={6: 0},
        scratch_shapes=[
            pltpu.VMEM((EXTRA, cap, base.shape[1]), jnp.bfloat16),
            pltpu.SemaphoreType.DMA((EXTRA,)),
        ],
        compiler_params=pltpu.CompilerParams(vmem_limit_bytes=4 << 20),
        cost_estimate=pl.CostEstimate(
            flops=base.size * rank // 4, bytes_accessed=base.size * 4, transcendentals=0
        ),
    )(mine, counts, base, low, *extras, out)


def on_device(
    hidden,
    value_weight,
    down_weights,
    up_weights,
    group_adapter_id,
    adapter_storage_row,
    group_live_count,
):
    dp_count = lax.axis_size("dp")
    me = lax.axis_index("dp")
    owned, rank, width = down_weights.shape
    groups = group_adapter_id.shape[0] // dp_count
    cap = hidden.shape[0] // groups
    me_row = me.astype(jnp.int32).reshape(1)
    served, mine = index_tables(me_row, group_adapter_id, adapter_storage_row, dp_count)
    counts = lax.dynamic_slice_in_dim(group_live_count, me * groups, groups)

    def wide(hidden, value_weight, down_weights, up_weights):
        stored = adapter_storage_row[group_adapter_id]
        owners = (stored // owned).reshape(dp_count, groups)
        slots = (stored % owned).reshape(dp_count, groups)
        same = owners[:, :, None] == owners[:, None, :]
        earlier = jnp.arange(groups)[None, None, :] < jnp.arange(groups)[None, :, None]
        ranking = jnp.sum(same & earlier, axis=2)
        hits = (owners == me)[:, :, None] & (ranking[:, :, None] == jnp.arange(MOST))
        rows = jnp.sum(jnp.where(hits, slots[:, :, None], 0), axis=1).reshape(-1)
        my_owners = lax.dynamic_index_in_dim(owners, me, 0, keepdims=False)
        my_ranking = lax.dynamic_index_in_dim(ranking, me, 0, keepdims=False)
        base_terms = jnp.dot(hidden, value_weight, preferred_element_type=jnp.float32)
        base = lax.psum_scatter(base_terms, "tp", scatter_dimension=1, tiled=True)
        downs = lax.all_to_all(down_weights[rows], "dp", 0, 0, tiled=True)
        ups = lax.all_to_all(up_weights[rows], "dp", 0, 0, tiled=True)
        picked = my_owners * MOST + my_ranking
        partial = jnp.einsum(
            "gcd,grd->gcr",
            hidden.reshape(groups, cap, width),
            downs[picked],
            preferred_element_type=jnp.float32,
        )
        low = low_rank_sum(partial.reshape(groups * cap, rank))
        return finish(base, low, ups[picked], counts)

    def narrow(hidden, value_weight, down_weights, up_weights):
        side = math.isqrt(dp_count)
        hot = mine[FLAGS, HOT]
        a = (me // side - hot // side) % side
        b = (me % side - hot % side) % side
        offsets = jnp.stack([a, b]).astype(jnp.int32)
        trees = (True, False)
        soon = [
            (tree, ((2, part[0]), (2, part[1]), (near, 2), (near, 3)))
            for tree in trees
            for near, part in ((1, (0, 1)), (3, (2, 3)))
        ]
        late = [(tree, ((near, 0), (near, 1))) for tree in trees for near in (1, 3)]
        late += [(tree, ((0, 0), (0, 1), (0, 2), (0, 3))) for tree in trees]
        moves = ((1, 0), (-1, 0), (0, 1), (0, -1))
        turned = ((0, 1), (0, 2), (0, -1), (1, 0), (2, 0), (-1, 0))
        send = lambda values, ways: [shift(v, *way) for v, way in zip(values, ways)]
        barrier = lax.optimization_barrier
        (main_sent,) = gather_call(
            main_kernel, (dp_count,), dp_count, (served,), down_weights, up_weights
        )
        main = lax.all_to_all(main_sent, "dp", 0, 0, tiled=True)
        unit = main_sent.shape[1:]
        dtype = main_sent.dtype
        gathered = gather_call(
            functools.partial(extra_kernel, soon),
            (4,) * 4,
            16,
            (me_row, served, mine),
            down_weights,
            up_weights,
            50,
        )
        later_served, _ = barrier((served, gathered))
        later = gather_call(
            functools.partial(extra_kernel, late),
            (2,) * 4 + (4,) * 2,
            16,
            (me_row, later_served, mine),
            down_weights,
            up_weights,
            50,
        )
        base_terms = jnp.dot(hidden, value_weight, preferred_element_type=jnp.float32)
        main, gathered, later, base_terms = barrier((main, gathered, later, base_terms))
        fresh = send(gathered, moves)
        base = lax.psum_scatter(base_terms, "tp", scatter_dimension=1, tiled=True)
        pairs = (groups - EXTRA) // 2
        partial = low_partial(
            functools.partial(low_main_kernel, cap), pairs, cap, rank, mine, hidden, (main,)
        )
        fresh, near, summed = barrier((fresh, later[:4], low_rank_down(partial)))
        relayed = vmem_call(
            relay_kernel, ((2,) + unit,) * 4, dtype, (offsets,), (*fresh, *near)
        )
        near_a, (own, other) = barrier((send(relayed, moves), low_rank_up(summed)))
        tree_arrays = [
            (later[4 + h], near_a[2 * h], near_a[2 * h + 1], fresh[2 * h], fresh[2 * h + 1])
            for h in range(2)
        ]
        lines = vmem_call(
            line_kernel, (unit,) * 8, dtype, (offsets,), tree_arrays[0] + tree_arrays[1]
        )
        got = send(lines[1:4] + lines[5:8], turned)
        t = lax.axis_index("tp")
        where = jnp.stack([t // 2, t % 2]).astype(jnp.int32)
        own, _ = barrier((own, lines))
        out = combine_main(where, mine, counts, base, own, other, main, rank)
        got, out = barrier((got, out))
        extras = vmem_call(
            pick_kernel,
            (unit,) * 2,
            dtype,
            (offsets,),
            (lines[0], *got[:3], lines[4], *got[3:]),
        )
        extra_partial = low_partial(
            functools.partial(low_extra_kernel, groups - EXTRA, cap),
            EXTRA // 2,
            cap,
            rank,
            mine,
            hidden,
            extras,
        )
        extra_low = low_rank_doubling(extra_partial)
        return combine_extra(mine, counts, base, extra_low, extras, out, rank)

    return lax.cond(
        mine[FLAGS, FITS] == 1, narrow, wide, hidden, value_weight, down_weights, up_weights
    )


def solution(mesh):
    return jax.shard_map(
        on_device,
        mesh=mesh,
        in_specs=(
            P("dp", "tp"),
            P("tp", None),
            P("dp", None, "tp"),
            P("dp", None, "tp"),
            P(),
            P(),
            P(),
        ),
        out_specs=P("dp", "tp"),
        check_vma=False,
    )
```

```python
import functools
import math

import jax
import jax.numpy as jnp
from jax import lax
from jax.experimental import pallas as pl
from jax.experimental.pallas import tpu as pltpu
from jax.sharding import PartitionSpec as P

ADAPTER_SCALE = 0.5
MAIN = 2
MOST = 6
EXTRA = MOST - MAIN


def low_rank_sum(partial):
    rows, rank = partial.shape
    tp_count = lax.axis_size("tp")
    pieces = lax.all_to_all(partial, "tp", split_axis=0, concat_axis=0, tiled=True)
    mine = jnp.sum(pieces.reshape(tp_count, rows // tp_count, rank), axis=0).astype(jnp.bfloat16)
    return lax.all_gather(mine, "tp", axis=0, tiled=True)


def finish(base, low, ups, counts):
    groups = counts.shape[0]
    cap = base.shape[0] // groups
    delta = jnp.einsum(
        "gcr,grv->gcv", low.reshape(groups, cap, -1), ups, preferred_element_type=jnp.float32
    )
    merged = base.reshape(groups, cap, -1) + ADAPTER_SCALE * delta
    active = jnp.arange(cap)[None, :, None] < counts[:, None, None]
    out = jnp.where(active, merged, jnp.float32(0.0)).astype(jnp.bfloat16)
    return out.reshape(base.shape)


SMEM = pl.BlockSpec(memory_space=pltpu.SMEM)
VMEM = pl.BlockSpec(memory_space=pltpu.VMEM)
HBM = pl.BlockSpec(memory_space=pltpu.HBM)
LANES = 128
ORDER, PLACE, FLAGS = 0, 1, 2
HOT, FITS = 0, 1


def shift(value, dx, dy):
    side = math.isqrt(lax.axis_size("dp"))
    pairs = [
        (x * side + y, (x + dx) % side * side + (y + dy) % side)
        for x in range(side)
        for y in range(side)
    ]
    return lax.ppermute(value, "dp", pairs)


def index_kernel(me_ref, ids_ref, table_ref, served_ref, mine_ref, owner_ref, rank_ref):
    total = ids_ref.shape[0]
    dp_count = served_ref.shape[0]
    groups = total // dp_count
    chunks = table_ref.shape[0]
    owned = chunks * LANES // dp_count
    me = me_ref[0]
    f32, bf16 = jnp.float32, jnp.bfloat16
    ids = ids_ref[...]
    lane = lax.broadcasted_iota(jnp.int32, (total, LANES), 1)
    found = jnp.zeros((total, LANES), jnp.int32)
    for c in range(chunks):
        found += jnp.where(ids == lane + c * LANES, table_ref[c : c + 1, :], 0)
    stored = jnp.sum(found, axis=1, keepdims=True)
    owner = lax.div(stored, owned)
    slot = stored - owner * owned
    holds = jnp.where(owner == lane, 1.0, 0.0)
    low = lax.broadcasted_iota(jnp.int32, (groups, groups), 0)
    low = jnp.where(low > lax.broadcasted_iota(jnp.int32, (groups, groups), 1), 1.0, 0.0)
    low = low.astype(bf16)
    holds16 = holds.astype(bf16)
    before = jnp.concatenate(
        [
            jnp.dot(low, holds16[r * groups : (r + 1) * groups], preferred_element_type=f32)
            for r in range(dp_count)
        ],
        axis=0,
    )
    ranking = jnp.sum(before * holds, axis=1, keepdims=True).astype(jnp.int32)
    owner_ref[...] = jnp.broadcast_to(owner, (total, LANES))
    rank_ref[...] = jnp.broadcast_to(ranking, (total, LANES))
    block_of = lax.div(lax.broadcasted_iota(jnp.int32, (dp_count, total), 1), groups)
    block = block_of == lax.broadcasted_iota(jnp.int32, (dp_count, total), 0)
    block = jnp.where(block, 1.0, 0.0).astype(bf16)
    loads = jnp.dot(block, holds16, preferred_element_type=f32)
    kept = jnp.where((owner == me) & (ranking == lane), slot, 0).astype(f32).astype(bf16)
    served_ref[...] = jnp.dot(block, kept, preferred_element_type=f32).astype(jnp.int32)
    least = jnp.min(loads, axis=0, keepdims=True)
    row_lane = lax.broadcasted_iota(jnp.int32, (1, LANES), 1)
    hot = jnp.min(jnp.where(least >= MOST, row_lane, LANES), axis=1, keepdims=True)
    spare = jnp.where(row_lane == hot, 0.0, loads)
    most = jnp.max(jnp.max(spare, axis=0, keepdims=True), axis=1, keepdims=True)
    fits = jnp.where(most <= MAIN, 1, 0)
    at = pl.ds(pl.multiple_of(me * groups, groups), groups)
    my_owner = owner_ref[at, :]
    my_rank = rank_ref[at, :]
    late = (my_owner == hot) & (my_rank >= MAIN)
    place = jnp.where(late, dp_count * MAIN + my_rank - MAIN, my_owner * MAIN + my_rank)
    early = jnp.where(late, 0.0, 1.0).astype(bf16)
    ahead = jnp.dot(low, early, preferred_element_type=f32).astype(jnp.int32)
    turn = jnp.where(late, groups - EXTRA + my_rank - MAIN, ahead)
    group_lane = lax.broadcasted_iota(jnp.int32, (groups, LANES), 1)
    group = lax.broadcasted_iota(jnp.int32, (groups, LANES), 0)
    here = turn == group_lane
    mine_ref[...] = jnp.zeros(mine_ref.shape, jnp.int32)
    mine_ref[ORDER : ORDER + 1, :] = jnp.sum(jnp.where(here, group, 0), axis=0, keepdims=True)
    mine_ref[PLACE : PLACE + 1, :] = jnp.sum(jnp.where(here, place, 0), axis=0, keepdims=True)
    mine_ref[FLAGS : FLAGS + 1, :] = jnp.where(
        row_lane == HOT, hot, jnp.where(row_lane == FITS, fits, 0)
    )


def index_tables(me, ids, table, dp_count):
    total = ids.shape[0]
    return pl.pallas_call(
        index_kernel,
        out_shape=(
            jax.ShapeDtypeStruct((dp_count, LANES), jnp.int32),
            jax.ShapeDtypeStruct((8, LANES), jnp.int32),
        ),
        in_specs=[SMEM, VMEM, VMEM],
        out_specs=(VMEM, VMEM),
        scratch_shapes=[pltpu.VMEM((total, LANES), jnp.int32)] * 2,
        compiler_params=pltpu.CompilerParams(vmem_limit_bytes=8 << 20),
    )(me, ids.reshape(total, 1), table.reshape(-1, LANES))


def copy_units(wanted, down, up, up_in, down_sem, up_sem):
    rank = down.shape[1]
    lanes = up.shape[2]
    steps = rank // 16
    downs, ups = [], []
    for i, (dest, index, rows) in enumerate(wanted):
        for half in range(2):
            n = 2 * i + half
            ups.append(pltpu.make_async_copy(up.at[rows[half]], up_in.at[n], up_sem.at[n]))
            ups[-1].start()
            downs.append(
                pltpu.make_async_copy(
                    down.at[rows[half]], dest.at[index, pl.ds(half * rank, rank)], down_sem.at[n]
                )
            )
            downs[-1].start()
    for i, (dest, index, rows) in enumerate(wanted):
        for half in range(2):
            n = 2 * i + half
            ups[n].wait()
            for part in range(steps):
                at = (half * steps + part) * lanes
                dest[index, 2 * rank : 2 * rank + 16, at : at + lanes] = up_in[
                    n, part * 16 : part * 16 + 16, :
                ]
    for copy in downs:
        copy.wait()


def main_kernel(served, down, up, out, *scratch):
    wanted = [(out, p, (served[p, 0], served[p, 1])) for p in range(out.shape[0])]
    copy_units(wanted, down, up, *scratch)


def extra_kernel(lines, me, served, mine, down, up, *refs):
    outs, scratch = refs[: len(lines)], refs[len(lines) :]
    dp_count = served.shape[0]
    side = math.isqrt(dp_count)
    hot = mine[FLAGS, HOT]

    @pl.when(hot == me[0])
    def _():
        hot_x, hot_y = lax.div(hot, side), lax.rem(hot, side)
        wanted = []
        for out, (x_first, units) in zip(outs, lines):
            for i, (a, b) in enumerate(units):
                dx, dy = (a, b) if x_first else (b, a)
                peer = lax.rem(hot_x + dx, side) * side + lax.rem(hot_y + dy, side)
                first = MAIN if x_first else MAIN + 2
                wanted.append((out, i, (served[peer, first], served[peer, first + 1])))
        copy_units(wanted, down, up, *scratch)


def gather_call(kernel, shapes, count, scalars, down, up, limit=8):
    _, rank, width = down.shape
    lanes = up.shape[2]
    return pl.pallas_call(
        kernel,
        out_shape=[jax.ShapeDtypeStruct((n, 2 * rank + 16, width), down.dtype) for n in shapes],
        in_specs=[SMEM] * len(scalars) + [HBM, HBM],
        out_specs=[VMEM] * len(shapes),
        scratch_shapes=[
            pltpu.VMEM((2 * count, rank, lanes), up.dtype),
            pltpu.SemaphoreType.DMA((2 * count,)),
            pltpu.SemaphoreType.DMA((2 * count,)),
        ],
        compiler_params=pltpu.CompilerParams(vmem_limit_bytes=limit << 20),
        cost_estimate=pl.CostEstimate(
            flops=0, bytes_accessed=count * rank * (width + lanes) * 8, transcendentals=0
        ),
    )(*scalars, down, up)


def vmem_call(kernel, shapes, dtype, scalars, arrays, limit=10):
    return pl.pallas_call(
        kernel,
        out_shape=[jax.ShapeDtypeStruct(shape, dtype) for shape in shapes],
        in_specs=[SMEM] * len(scalars) + [VMEM] * len(arrays),
        out_specs=[VMEM] * len(shapes),
        compiler_params=pltpu.CompilerParams(vmem_limit_bytes=limit << 20),
        cost_estimate=pl.CostEstimate(
            flops=0,
            bytes_accessed=sum(math.prod(shape) for shape in shapes) * 4,
            transcendentals=0,
        ),
    )(*scalars, *arrays)


def move(dst, src):
    rows = src.shape[0]

    def body(i, carry):
        at = pl.ds(pl.multiple_of(i * 16, 16), 16)
        dst[at, :] = src[at, :]
        return carry

    lax.fori_loop(0, rows // 16, body, 0, unroll=3)


def relay_kernel(offsets, *refs):
    fresh, near, outs = refs[:4], refs[4:8], refs[8:]
    for i in range(4):
        at = offsets[i // 2]
        close = 1 if i % 2 == 0 else 3
        for source, when in ((near[i], at != close), (fresh[i], at == close)):

            @pl.when(when)
            def _(source=source, out=outs[i]):
                for u in range(2):
                    move(out.at[u], source.at[u])


def line_kernel(offsets, *refs):
    outs = refs[10:]
    for h in range(2):
        own, plus_a, minus_a, plus_b, minus_b = refs[5 * h : 5 * h + 5]
        out = outs[4 * h : 4 * h + 4]
        at = offsets[h]
        low, high = own.at[pl.ds(0, 2)], own.at[pl.ds(2, 2)]
        plus_b, minus_b = plus_b.at[pl.ds(2, 2)], minus_b.at[pl.ds(2, 2)]
        picks = ((low, high), (plus_a, plus_b), (plus_a, minus_a), (minus_a, minus_b))
        for offset, (first, second) in enumerate(picks):

            @pl.when(at == offset)
            def _(first=first, second=second, out=out):
                for u in range(2):
                    move(out[u], first.at[u])
                    move(out[2 + u], second.at[u])


def pick_kernel(offsets, *refs):
    for h in range(2):
        at = offsets[1 - h]
        for offset, source in enumerate(refs[4 * h : 4 * h + 4]):

            @pl.when(at == offset)
            def _(source=source, out=refs[8 + h]):
                move(out, source)


def base_kernel(hidden, weight, out):
    out[...] = jnp.dot(hidden[...], weight[...], preferred_element_type=jnp.float32)


def base_product(hidden, weight, block=256):
    rows, width = hidden.shape
    columns = weight.shape[1]
    return pl.pallas_call(
        base_kernel,
        grid=(rows // block,),
        out_shape=jax.ShapeDtypeStruct((rows, columns), jnp.float32),
        in_specs=[
            pl.BlockSpec((block, width), lambda i: (i, 0)),
            pl.BlockSpec((width, columns), lambda i: (0, 0)),
        ],
        out_specs=pl.BlockSpec((block, columns), lambda i: (i, 0)),
        compiler_params=pltpu.CompilerParams(vmem_limit_bytes=14 << 20),
        cost_estimate=pl.CostEstimate(
            flops=2 * rows * width * columns,
            bytes_accessed=hidden.size * 2 + weight.size * 2 + rows * columns * 4,
            transcendentals=0,
        ),
    )(hidden, weight)


def paired(hidden, mine, i, pairs, cap, first, second):
    spots = [pl.multiple_of(mine[ORDER, j] * cap, cap) for j in (i, i + pairs)]
    rows = jnp.concatenate([hidden[pl.ds(spot, cap), :] for spot in spots], axis=0)
    product = lax.dot_general(
        rows,
        jnp.concatenate([first, second], axis=0),
        (((1,), (1,)), ((), ())),
        preferred_element_type=jnp.float32,
    )
    lane = lax.broadcasted_iota(jnp.int32, (cap, product.shape[1]), 1)
    return jnp.where(lane < first.shape[0], product[:cap], product[cap:])


def low_kernel(cap, mine, hidden, main, *refs):
    extras, out = refs[:-1], refs[-1]
    rank = out.shape[1] // 2
    pairs = out.shape[0] // cap
    full = pairs - EXTRA

    def weights(j):
        place = mine[PLACE, j]
        unit = lax.div(place, 2)
        return main[unit, pl.ds(pl.multiple_of((place - 2 * unit) * rank, rank), rank), :]

    def body(i, carry):
        at = pl.ds(pl.multiple_of(i * cap, cap), cap)
        out[at, :] = paired(hidden, mine, i, pairs, cap, weights(i), weights(i + pairs))
        return carry

    lax.fori_loop(0, full, body, 0, unroll=2)
    for e in range(EXTRA):
        i = full + e
        late = extras[e // 2][e % 2 * rank : (e % 2 + 1) * rank, :]
        out[i * cap : (i + 1) * cap, :] = paired(hidden, mine, i, pairs, cap, weights(i), late)


def low_partial(mine, hidden, main, extras, cap, rank):
    pairs = hidden.shape[0] // cap // 2
    return pl.pallas_call(
        functools.partial(low_kernel, cap),
        out_shape=jax.ShapeDtypeStruct((pairs * cap, 2 * rank), jnp.float32),
        in_specs=[SMEM] + [VMEM] * (2 + len(extras)),
        out_specs=VMEM,
        compiler_params=pltpu.CompilerParams(vmem_limit_bytes=12 << 20),
        cost_estimate=pl.CostEstimate(
            flops=pairs * cap * rank * 4 * hidden.shape[1],
            bytes_accessed=(hidden.size + main.size) * 2,
            transcendentals=0,
        ),
    )(mine, hidden, main, *extras)


def turn(step):
    tp_count = lax.axis_size("tp")
    return [(i, (i + 2 * step) % tp_count) for i in range(tp_count)]


def swap():
    return [(i, i ^ 1) for i in range(lax.axis_size("tp"))]


def low_rank_down(partial):
    chips = lax.axis_size("tp") // 2
    t = lax.axis_index("tp")
    z, core = t // 2, t % 2
    half = partial.shape[0] // 2
    piece = half // chips
    cut = lambda array, start, size: lax.dynamic_slice_in_dim(array, start, size, 0)
    total = cut(partial, core * half, half) + lax.ppermute(
        cut(partial, (1 - core) * half, half), "tp", swap()
    )
    pieces = [
        lax.ppermute(cut(total, (z + d) % chips * piece, piece), "tp", turn(d))
        for d in range(1, chips)
    ]
    return (cut(total, z * piece, piece) + sum(pieces)).astype(jnp.bfloat16)


def low_rank_up(summed):
    chips = lax.axis_size("tp") // 2
    own = jnp.stack([summed] + [lax.ppermute(summed, "tp", turn(d)) for d in range(1, chips)])
    return own, lax.ppermute(own, "tp", swap())


def blend(base, out, counts, mine, j, both, ups, cap):
    rank = both.shape[1] // 2
    lane = lax.broadcasted_iota(jnp.int32, both.shape, 1)
    none = jnp.zeros_like(both)
    left = jnp.concatenate(
        [jnp.where(lane < rank, both, none), jnp.where(lane < rank, none, both)], axis=0
    )
    delta = jnp.dot(left, jnp.concatenate(ups, axis=0), preferred_element_type=jnp.float32)
    rows = lax.broadcasted_iota(jnp.int32, (cap, base.shape[1]), 0)
    for n in range(2):
        g = mine[ORDER, j[n]]
        here = pl.ds(pl.multiple_of(g * cap, cap), cap)
        merged = base[here, :] + ADAPTER_SCALE * delta[n * cap : (n + 1) * cap]
        out[here, :] = jnp.where(rows < counts[g], merged, 0.0).astype(out.dtype)


def out_kernel(where, mine, counts, base, own, other, main, *refs):
    extras, out, low = refs[:2], refs[2], refs[3]
    groups = counts.shape[0]
    cap = base.shape[0] // groups
    chips, piece, rank = own.shape[0], own.shape[1], own.shape[2] // 2
    lanes = base.shape[1]
    z, core = where[0], where[1]
    steps = rank // 16
    pairs = groups // 2
    full = pairs - EXTRA
    for d in range(chips):
        quarter = lax.rem(z - d + chips, chips)
        for ref, half in ((own, core), (other, 1 - core)):
            at = pl.multiple_of((half * chips + quarter) * piece, piece)
            low[pl.ds(at, piece), :] = ref[d]

    def up(j):
        place = mine[PLACE, j]
        unit = lax.div(place, 2)
        at = (place - 2 * unit) * steps * lanes
        return [
            main[unit, :, pl.ds(pl.multiple_of(at + part * lanes, lanes), lanes)]
            for part in range(steps)
        ]

    def body(i, carry):
        both = low[pl.ds(pl.multiple_of(i * cap, cap), cap), :]
        blend(base, out, counts, mine, (i, i + pairs), both, up(i) + up(i + pairs), cap)
        return carry

    lax.fori_loop(0, full, body, 0, unroll=2)
    for e in range(EXTRA):
        i = full + e
        pack = extras[e // 2]
        late = [
            pack[:, (e % 2 * steps + part) * lanes : (e % 2 * steps + part + 1) * lanes]
            for part in range(steps)
        ]
        both = low[i * cap : (i + 1) * cap, :]
        blend(base, out, counts, mine, (i, i + pairs), both, up(i) + late, cap)


def whole(array):
    return pl.BlockSpec(array.shape, lambda i: (0,) * array.ndim)


def combine(where, mine, counts, base, own, other, main, extras, rank):
    packs = pl.BlockSpec((main.shape[0], 16, main.shape[2]), lambda i: (0, rank // 8, 0))
    pack = pl.BlockSpec((16, main.shape[2]), lambda i: (rank // 8, 0))
    return pl.pallas_call(
        out_kernel,
        grid=(1,),
        out_shape=jax.ShapeDtypeStruct(base.shape, jnp.bfloat16),
        in_specs=[SMEM, SMEM, SMEM, whole(base), whole(own), whole(other), packs, pack, pack],
        out_specs=whole(base),
        scratch_shapes=[
            pltpu.VMEM((2 * own.shape[0] * own.shape[1], own.shape[2]), jnp.bfloat16)
        ],
        compiler_params=pltpu.CompilerParams(vmem_limit_bytes=8 << 20),
        cost_estimate=pl.CostEstimate(
            flops=base.size * rank * 2, bytes_accessed=base.size * 8, transcendentals=0
        ),
    )(where, mine, counts, base, own, other, main, *extras)


def on_device(
    hidden,
    value_weight,
    down_weights,
    up_weights,
    group_adapter_id,
    adapter_storage_row,
    group_live_count,
):
    dp_count = lax.axis_size("dp")
    me = lax.axis_index("dp")
    owned, rank, width = down_weights.shape
    groups = group_adapter_id.shape[0] // dp_count
    cap = hidden.shape[0] // groups
    me_row = me.astype(jnp.int32).reshape(1)
    served, mine = index_tables(me_row, group_adapter_id, adapter_storage_row, dp_count)
    counts = lax.dynamic_slice_in_dim(group_live_count, me * groups, groups)

    def wide(hidden, value_weight, down_weights, up_weights):
        stored = adapter_storage_row[group_adapter_id]
        owners = (stored // owned).reshape(dp_count, groups)
        slots = (stored % owned).reshape(dp_count, groups)
        same = owners[:, :, None] == owners[:, None, :]
        earlier = jnp.arange(groups)[None, None, :] < jnp.arange(groups)[None, :, None]
        ranking = jnp.sum(same & earlier, axis=2)
        hits = (owners == me)[:, :, None] & (ranking[:, :, None] == jnp.arange(MOST))
        rows = jnp.sum(jnp.where(hits, slots[:, :, None], 0), axis=1).reshape(-1)
        my_owners = lax.dynamic_index_in_dim(owners, me, 0, keepdims=False)
        my_ranking = lax.dynamic_index_in_dim(ranking, me, 0, keepdims=False)
        base_terms = jnp.dot(hidden, value_weight, preferred_element_type=jnp.float32)
        base = lax.psum_scatter(base_terms, "tp", scatter_dimension=1, tiled=True)
        downs = lax.all_to_all(down_weights[rows], "dp", 0, 0, tiled=True)
        ups = lax.all_to_all(up_weights[rows], "dp", 0, 0, tiled=True)
        picked = my_owners * MOST + my_ranking
        partial = jnp.einsum(
            "gcd,grd->gcr",
            hidden.reshape(groups, cap, width),
            downs[picked],
            preferred_element_type=jnp.float32,
        )
        low = low_rank_sum(partial.reshape(groups * cap, rank))
        return finish(base, low, ups[picked], counts)

    def narrow(hidden, value_weight, down_weights, up_weights):
        side = math.isqrt(dp_count)
        hot = mine[FLAGS, HOT]
        a = (me // side - hot // side) % side
        b = (me % side - hot % side) % side
        offsets = jnp.stack([a, b]).astype(jnp.int32)
        trees = (True, False)
        soon = [
            (tree, ((2, part[0]), (2, part[1]), (near, 2), (near, 3)))
            for tree in trees
            for near, part in ((1, (0, 1)), (3, (2, 3)))
        ]
        late = [(tree, ((near, 0), (near, 1))) for tree in trees for near in (1, 3)]
        late += [(tree, ((0, 0), (0, 1), (0, 2), (0, 3))) for tree in trees]
        moves = ((1, 0), (-1, 0), (0, 1), (0, -1))
        turned = ((0, 1), (0, 2), (0, -1), (1, 0), (2, 0), (-1, 0))
        send = lambda values, ways: [shift(v, *way) for v, way in zip(values, ways)]
        barrier = lax.optimization_barrier
        scalars = (me_row, served, mine)
        gathered = gather_call(
            functools.partial(extra_kernel, soon), (4,) * 4, 16, scalars, down_weights, up_weights
        )
        fresh = send(gathered, moves)
        later_served, _ = barrier((served, gathered))
        later = gather_call(
            functools.partial(extra_kernel, late),
            (2,) * 4 + (4,) * 2,
            16,
            (me_row, later_served, mine),
            down_weights,
            up_weights,
        )
        main_served, _ = barrier((served, later))
        (main_sent,) = gather_call(
            main_kernel, (dp_count,), dp_count, (main_served,), down_weights, up_weights
        )
        base_hidden, _ = barrier((hidden, main_sent))
        base_terms = base_product(base_hidden, value_weight)
        base = lax.psum_scatter(base_terms, "tp", scatter_dimension=1, tiled=True)
        unit = main_sent.shape[1:]
        dtype = main_sent.dtype
        fresh, near, main_sent, _ = barrier((fresh, later[:4], main_sent, base_terms))
        relayed = vmem_call(
            relay_kernel, ((2,) + unit,) * 4, dtype, (offsets,), (*fresh, *near)
        )
        near_a, main_sent = barrier((send(relayed, moves), main_sent))
        main = lax.all_to_all(main_sent, "dp", 0, 0, tiled=True)
        tree_arrays = [
            (later[4 + h], near_a[2 * h], near_a[2 * h + 1], fresh[2 * h], fresh[2 * h + 1])
            for h in range(2)
        ]
        lines = vmem_call(
            line_kernel, (unit,) * 8, dtype, (offsets,), tree_arrays[0] + tree_arrays[1]
        )
        got = send(lines[1:4] + lines[5:8], turned)
        extras = vmem_call(
            pick_kernel,
            (unit,) * 2,
            dtype,
            (offsets,),
            (lines[0], *got[:3], lines[4], *got[3:]),
        )
        partial = low_partial(mine, hidden, main, extras, cap, rank)
        own, other = low_rank_up(low_rank_down(partial))
        t = lax.axis_index("tp")
        where = jnp.stack([t // 2, t % 2]).astype(jnp.int32)
        return combine(where, mine, counts, base, own, other, main, extras, rank)

    return lax.cond(
        mine[FLAGS, FITS] == 1, narrow, wide, hidden, value_weight, down_weights, up_weights
    )


def solution(mesh):
    return jax.shard_map(
        on_device,
        mesh=mesh,
        in_specs=(
            P("dp", "tp"),
            P("tp", None),
            P("dp", None, "tp"),
            P("dp", None, "tp"),
            P(),
            P(),
            P(),
        ),
        out_specs=P("dp", "tp"),
        check_vma=False,
    )
```

```python
import functools
import math

import jax
import jax.numpy as jnp
from jax import lax
from jax.experimental import pallas as pl
from jax.experimental.pallas import tpu as pltpu
from jax.sharding import PartitionSpec as P

ADAPTER_SCALE = 0.5
MAIN = 2
MOST = 6
EXTRA = MOST - MAIN


def low_rank_sum(partial):
    rows, rank = partial.shape
    tp_count = lax.axis_size("tp")
    pieces = lax.all_to_all(partial, "tp", split_axis=0, concat_axis=0, tiled=True)
    mine = jnp.sum(pieces.reshape(tp_count, rows // tp_count, rank), axis=0).astype(jnp.bfloat16)
    return lax.all_gather(mine, "tp", axis=0, tiled=True)


def finish(base, low, ups, counts):
    groups = counts.shape[0]
    cap = base.shape[0] // groups
    delta = jnp.einsum(
        "gcr,grv->gcv", low.reshape(groups, cap, -1), ups, preferred_element_type=jnp.float32
    )
    merged = base.reshape(groups, cap, -1) + ADAPTER_SCALE * delta
    active = jnp.arange(cap)[None, :, None] < counts[:, None, None]
    out = jnp.where(active, merged, jnp.float32(0.0)).astype(jnp.bfloat16)
    return out.reshape(base.shape)


SMEM = pl.BlockSpec(memory_space=pltpu.SMEM)
VMEM = pl.BlockSpec(memory_space=pltpu.VMEM)
HBM = pl.BlockSpec(memory_space=pltpu.HBM)
LANES = 128
ORDER, PLACE, FLAGS = 0, 1, 2
HOT, FITS, AT, CHIP, CORE = 0, 1, 2, 4, 5


def shift(value, dx, dy):
    side = math.isqrt(lax.axis_size("dp"))
    pairs = [
        (x * side + y, (x + dx) % side * side + (y + dy) % side)
        for x in range(side)
        for y in range(side)
    ]
    return lax.ppermute(value, "dp", pairs)


def index_kernel(spot_ref, ids_ref, table_ref, served_ref, mine_ref, owner_ref, rank_ref):
    total = ids_ref.shape[0]
    dp_count = served_ref.shape[0]
    groups = total // dp_count
    chunks = table_ref.shape[0]
    owned = chunks * LANES // dp_count
    me = spot_ref[0]
    f32, bf16 = jnp.float32, jnp.bfloat16
    ids = ids_ref[...]
    lane = lax.broadcasted_iota(jnp.int32, (total, LANES), 1)
    found = jnp.zeros((total, LANES), jnp.int32)
    for c in range(chunks):
        found += jnp.where(ids == lane + c * LANES, table_ref[c : c + 1, :], 0)
    stored = jnp.sum(found, axis=1, keepdims=True)
    owner = lax.div(stored, owned)
    slot = stored - owner * owned
    holds = jnp.where(owner == lane, 1.0, 0.0)
    low = lax.broadcasted_iota(jnp.int32, (groups, groups), 0)
    low = jnp.where(low > lax.broadcasted_iota(jnp.int32, (groups, groups), 1), 1.0, 0.0)
    low = low.astype(bf16)
    holds16 = holds.astype(bf16)
    before = jnp.concatenate(
        [
            jnp.dot(low, holds16[r * groups : (r + 1) * groups], preferred_element_type=f32)
            for r in range(dp_count)
        ],
        axis=0,
    )
    ranking = jnp.sum(before * holds, axis=1, keepdims=True).astype(jnp.int32)
    owner_ref[...] = jnp.broadcast_to(owner, (total, LANES))
    rank_ref[...] = jnp.broadcast_to(ranking, (total, LANES))
    block_of = lax.div(lax.broadcasted_iota(jnp.int32, (dp_count, total), 1), groups)
    block = block_of == lax.broadcasted_iota(jnp.int32, (dp_count, total), 0)
    block = jnp.where(block, 1.0, 0.0).astype(bf16)
    loads = jnp.dot(block, holds16, preferred_element_type=f32)
    kept = jnp.where((owner == me) & (ranking == lane), slot, 0).astype(f32).astype(bf16)
    served_ref[...] = jnp.dot(block, kept, preferred_element_type=f32).astype(jnp.int32)
    least = jnp.min(loads, axis=0, keepdims=True)
    row_lane = lax.broadcasted_iota(jnp.int32, (1, LANES), 1)
    hot = jnp.min(jnp.where(least >= MOST, row_lane, LANES), axis=1, keepdims=True)
    spare = jnp.where(row_lane == hot, 0.0, loads)
    most = jnp.max(jnp.max(spare, axis=0, keepdims=True), axis=1, keepdims=True)
    fits = jnp.where(most <= MAIN, 1, 0)
    at = pl.ds(pl.multiple_of(me * groups, groups), groups)
    my_owner = owner_ref[at, :]
    my_rank = rank_ref[at, :]
    late = (my_owner == hot) & (my_rank >= MAIN)
    place = jnp.where(late, dp_count * MAIN + my_rank - MAIN, my_owner * MAIN + my_rank)
    early = jnp.where(late, 0.0, 1.0).astype(bf16)
    ahead = jnp.dot(low, early, preferred_element_type=f32).astype(jnp.int32)
    turn = jnp.where(late, groups - EXTRA + my_rank - MAIN, ahead)
    group_lane = lax.broadcasted_iota(jnp.int32, (groups, LANES), 1)
    group = lax.broadcasted_iota(jnp.int32, (groups, LANES), 0)
    here = turn == group_lane
    mine_ref[...] = jnp.zeros(mine_ref.shape, jnp.int32)
    mine_ref[ORDER : ORDER + 1, :] = jnp.sum(jnp.where(here, group, 0), axis=0, keepdims=True)
    mine_ref[PLACE : PLACE + 1, :] = jnp.sum(jnp.where(here, place, 0), axis=0, keepdims=True)
    side = math.isqrt(dp_count)
    x, y = lax.div(me, side), lax.rem(me, side)
    flags = (
        (HOT, hot),
        (FITS, fits),
        (AT, lax.rem(x - lax.div(hot, side) + side, side)),
        (AT + 1, lax.rem(y - lax.rem(hot, side) + side, side)),
        (CHIP, lax.div(spot_ref[1], 2)),
        (CORE, lax.rem(spot_ref[1], 2)),
    )
    row = jnp.zeros((1, LANES), jnp.int32)
    for at, value in flags:
        row = jnp.where(row_lane == at, value, row)
    mine_ref[FLAGS : FLAGS + 1, :] = row


def index_tables(spot, ids, table, dp_count):
    total = ids.shape[0]
    return pl.pallas_call(
        index_kernel,
        out_shape=(
            jax.ShapeDtypeStruct((dp_count, LANES), jnp.int32),
            jax.ShapeDtypeStruct((8, LANES), jnp.int32),
        ),
        in_specs=[SMEM, VMEM, VMEM],
        out_specs=(VMEM, VMEM),
        scratch_shapes=[pltpu.VMEM((total, LANES), jnp.int32)] * 2,
        compiler_params=pltpu.CompilerParams(vmem_limit_bytes=8 << 20),
    )(spot, ids.reshape(total, 1), table.reshape(-1, LANES))


def copy_units(wanted, down, up, up_in, down_sem, up_sem):
    rank = down.shape[1]
    lanes = up.shape[2]
    steps = rank // 16
    downs, ups = [], []
    for i, (dest, index, rows) in enumerate(wanted):
        for half in range(2):
            n = 2 * i + half
            ups.append(pltpu.make_async_copy(up.at[rows[half]], up_in.at[n], up_sem.at[n]))
            ups[-1].start()
            downs.append(
                pltpu.make_async_copy(
                    down.at[rows[half]], dest.at[index, pl.ds(half * rank, rank)], down_sem.at[n]
                )
            )
            downs[-1].start()
    for i, (dest, index, rows) in enumerate(wanted):
        for half in range(2):
            n = 2 * i + half
            ups[n].wait()
            for part in range(steps):
                at = (half * steps + part) * lanes
                dest[index, 2 * rank : 2 * rank + 16, at : at + lanes] = up_in[
                    n, part * 16 : part * 16 + 16, :
                ]
    for copy in downs:
        copy.wait()


def gather_kernel(lines, served, mine, down, up, *refs):
    main, outs, scratch = refs[0], refs[1 : 1 + len(lines)], refs[1 + len(lines) :]
    dp_count = served.shape[0]
    side = math.isqrt(dp_count)
    hot = mine[FLAGS, HOT]

    @pl.when((mine[FLAGS, AT] == 0) & (mine[FLAGS, AT + 1] == 0))
    def _():
        hot_x, hot_y = lax.div(hot, side), lax.rem(hot, side)
        wanted = []
        for out, (x_first, units) in zip(outs, lines):
            for i, (a, b) in enumerate(units):
                dx, dy = (a, b) if x_first else (b, a)
                peer = lax.rem(hot_x + dx, side) * side + lax.rem(hot_y + dy, side)
                first = MAIN if x_first else MAIN + 2
                wanted.append((out, i, (served[peer, first], served[peer, first + 1])))
        copy_units(wanted, down, up, *scratch)

    copy_units(
        [(main, p, (served[p, 0], served[p, 1])) for p in range(dp_count)], down, up, *scratch
    )


def gather_units(lines, served, mine, down, up):
    _, rank, width = down.shape
    lanes = up.shape[2]
    dp_count = served.shape[0]
    shapes = [dp_count] + [len(units) for _, units in lines]
    count = max(dp_count, sum(shapes[1:]))
    return pl.pallas_call(
        functools.partial(gather_kernel, lines),
        out_shape=[jax.ShapeDtypeStruct((n, 2 * rank + 16, width), down.dtype) for n in shapes],
        in_specs=[SMEM, SMEM, HBM, HBM],
        out_specs=[VMEM] * len(shapes),
        scratch_shapes=[
            pltpu.VMEM((2 * count, rank, lanes), up.dtype),
            pltpu.SemaphoreType.DMA((2 * count,)),
            pltpu.SemaphoreType.DMA((2 * count,)),
        ],
        compiler_params=pltpu.CompilerParams(vmem_limit_bytes=18 << 20),
        cost_estimate=pl.CostEstimate(
            flops=0, bytes_accessed=count * rank * (width + lanes) * 8, transcendentals=0
        ),
    )(served, mine, down, up)


def vmem_call(kernel, shapes, dtype, scalars, arrays, limit=10):
    return pl.pallas_call(
        kernel,
        out_shape=[jax.ShapeDtypeStruct(shape, dtype) for shape in shapes],
        in_specs=[SMEM] * len(scalars) + [VMEM] * len(arrays),
        out_specs=[VMEM] * len(shapes),
        compiler_params=pltpu.CompilerParams(vmem_limit_bytes=limit << 20),
        cost_estimate=pl.CostEstimate(
            flops=0,
            bytes_accessed=sum(math.prod(shape) for shape in shapes) * 4,
            transcendentals=0,
        ),
    )(*scalars, *arrays)


def move(dst, src):
    rows = src.shape[0]

    def body(i, carry):
        at = pl.ds(pl.multiple_of(i * 16, 16), 16)
        dst[at, :] = src[at, :]
        return carry

    lax.fori_loop(0, rows // 16, body, 0, unroll=3)


def relay_kernel(mine, *refs):
    fresh, near, outs = refs[:4], refs[4:8], refs[8:]
    for i in range(4):
        at = mine[FLAGS, AT + i // 2]
        close = 1 if i % 2 == 0 else 3
        for source, when in ((near[i], at != close), (fresh[i], at == close)):

            @pl.when(when)
            def _(source=source, out=outs[i]):
                for u in range(2):
                    move(out.at[u], source.at[u])


def line_kernel(mine, *refs):
    outs = refs[10:]
    for h in range(2):
        own, plus_a, minus_a, plus_b, minus_b = refs[5 * h : 5 * h + 5]
        out = outs[4 * h : 4 * h + 4]
        at = mine[FLAGS, AT + h]
        low, high = own.at[pl.ds(0, 2)], own.at[pl.ds(2, 2)]
        plus_b, minus_b = plus_b.at[pl.ds(2, 2)], minus_b.at[pl.ds(2, 2)]
        picks = ((low, high), (plus_a, plus_b), (plus_a, minus_a), (minus_a, minus_b))
        for offset, (first, second) in enumerate(picks):

            @pl.when(at == offset)
            def _(first=first, second=second, out=out):
                for u in range(2):
                    move(out[u], first.at[u])
                    move(out[2 + u], second.at[u])


def pick_kernel(mine, *refs):
    for h in range(2):
        at = mine[FLAGS, AT + 1 - h]
        for offset, source in enumerate(refs[4 * h : 4 * h + 4]):

            @pl.when(at == offset)
            def _(source=source, out=refs[8 + h]):
                move(out, source)


def base_kernel(hidden, weight, out):
    out[...] = jnp.dot(hidden[...], weight[...], preferred_element_type=jnp.float32)


def base_product(hidden, weight, block=256):
    rows, width = hidden.shape
    columns = weight.shape[1]
    return pl.pallas_call(
        base_kernel,
        grid=(rows // block,),
        out_shape=jax.ShapeDtypeStruct((rows, columns), jnp.float32),
        in_specs=[
            pl.BlockSpec((block, width), lambda i: (i, 0)),
            pl.BlockSpec((width, columns), lambda i: (0, 0)),
        ],
        out_specs=pl.BlockSpec((block, columns), lambda i: (i, 0)),
        compiler_params=pltpu.CompilerParams(vmem_limit_bytes=14 << 20),
        cost_estimate=pl.CostEstimate(
            flops=2 * rows * width * columns,
            bytes_accessed=hidden.size * 2 + weight.size * 2 + rows * columns * 4,
            transcendentals=0,
        ),
    )(hidden, weight)


def paired(hidden, mine, i, pairs, cap, first, second):
    spots = [pl.multiple_of(mine[ORDER, j] * cap, cap) for j in (i, i + pairs)]
    rows = jnp.concatenate([hidden[pl.ds(spot, cap), :] for spot in spots], axis=0)
    product = lax.dot_general(
        rows,
        jnp.concatenate([first, second], axis=0),
        (((1,), (1,)), ((), ())),
        preferred_element_type=jnp.float32,
    )
    lane = lax.broadcasted_iota(jnp.int32, (cap, product.shape[1]), 1)
    return jnp.where(lane < first.shape[0], product[:cap], product[cap:])


def low_kernel(cap, mine, hidden, main, *refs):
    extras, out = refs[:-1], refs[-1]
    rank = out.shape[1] // 2
    pairs = out.shape[0] // cap
    full = pairs - EXTRA

    def weights(j):
        place = mine[PLACE, j]
        unit = lax.div(place, 2)
        return main[unit, pl.ds(pl.multiple_of((place - 2 * unit) * rank, rank), rank), :]

    def body(i, carry):
        at = pl.ds(pl.multiple_of(i * cap, cap), cap)
        out[at, :] = paired(hidden, mine, i, pairs, cap, weights(i), weights(i + pairs))
        return carry

    lax.fori_loop(0, full, body, 0, unroll=2)
    for e in range(EXTRA):
        i = full + e
        late = extras[e // 2][e % 2 * rank : (e % 2 + 1) * rank, :]
        out[i * cap : (i + 1) * cap, :] = paired(hidden, mine, i, pairs, cap, weights(i), late)


def low_partial(mine, hidden, main, extras, cap, rank):
    pairs = hidden.shape[0] // cap // 2
    return pl.pallas_call(
        functools.partial(low_kernel, cap),
        out_shape=jax.ShapeDtypeStruct((pairs * cap, 2 * rank), jnp.float32),
        in_specs=[SMEM] + [VMEM] * (2 + len(extras)),
        out_specs=VMEM,
        compiler_params=pltpu.CompilerParams(vmem_limit_bytes=12 << 20),
        cost_estimate=pl.CostEstimate(
            flops=pairs * cap * rank * 4 * hidden.shape[1],
            bytes_accessed=(hidden.size + main.size) * 2,
            transcendentals=0,
        ),
    )(mine, hidden, main, *extras)


def turn(step):
    tp_count = lax.axis_size("tp")
    return [(i, (i + 2 * step) % tp_count) for i in range(tp_count)]


def swap():
    return [(i, i ^ 1) for i in range(lax.axis_size("tp"))]


def low_rank_down(partial):
    chips = lax.axis_size("tp") // 2
    t = lax.axis_index("tp")
    z, core = t // 2, t % 2
    half = partial.shape[0] // 2
    piece = half // chips
    cut = lambda array, start, size: lax.dynamic_slice_in_dim(array, start, size, 0)
    total = cut(partial, core * half, half) + lax.ppermute(
        cut(partial, (1 - core) * half, half), "tp", swap()
    )
    pieces = [
        lax.ppermute(cut(total, (z + d) % chips * piece, piece), "tp", turn(d))
        for d in range(1, chips)
    ]
    return (cut(total, z * piece, piece) + sum(pieces)).astype(jnp.bfloat16)


def low_rank_up(summed):
    chips = lax.axis_size("tp") // 2
    own = jnp.stack([summed] + [lax.ppermute(summed, "tp", turn(d)) for d in range(1, chips)])
    return own, lax.ppermute(own, "tp", swap())


def blend(base, out, counts, mine, j, both, ups, cap):
    rank = both.shape[1] // 2
    lane = lax.broadcasted_iota(jnp.int32, both.shape, 1)
    none = jnp.zeros_like(both)
    left = jnp.concatenate(
        [jnp.where(lane < rank, both, none), jnp.where(lane < rank, none, both)], axis=0
    )
    delta = jnp.dot(left, jnp.concatenate(ups, axis=0), preferred_element_type=jnp.float32)
    rows = lax.broadcasted_iota(jnp.int32, (cap, base.shape[1]), 0)
    for n in range(2):
        g = mine[ORDER, j[n]]
        here = pl.ds(pl.multiple_of(g * cap, cap), cap)
        merged = base[here, :] + ADAPTER_SCALE * delta[n * cap : (n + 1) * cap]
        out[here, :] = jnp.where(rows < counts[g], merged, 0.0).astype(out.dtype)


def out_kernel(mine, counts, base, own, other, main, *refs):
    extras, out, low = refs[:2], refs[2], refs[3]
    groups = counts.shape[0]
    cap = base.shape[0] // groups
    chips, piece, rank = own.shape[0], own.shape[1], own.shape[2] // 2
    lanes = base.shape[1]
    z, core = mine[FLAGS, CHIP], mine[FLAGS, CORE]
    steps = rank // 16
    pairs = groups // 2
    full = pairs - EXTRA
    for d in range(chips):
        quarter = lax.rem(z - d + chips, chips)
        for ref, half in ((own, core), (other, 1 - core)):
            at = pl.multiple_of((half * chips + quarter) * piece, piece)
            low[pl.ds(at, piece), :] = ref[d]

    def up(j):
        place = mine[PLACE, j]
        unit = lax.div(place, 2)
        at = (place - 2 * unit) * steps * lanes
        return [
            main[unit, :, pl.ds(pl.multiple_of(at + part * lanes, lanes), lanes)]
            for part in range(steps)
        ]

    def body(i, carry):
        both = low[pl.ds(pl.multiple_of(i * cap, cap), cap), :]
        blend(base, out, counts, mine, (i, i + pairs), both, up(i) + up(i + pairs), cap)
        return carry

    lax.fori_loop(0, full, body, 0, unroll=2)
    for e in range(EXTRA):
        i = full + e
        pack = extras[e // 2]
        late = [
            pack[:, (e % 2 * steps + part) * lanes : (e % 2 * steps + part + 1) * lanes]
            for part in range(steps)
        ]
        both = low[i * cap : (i + 1) * cap, :]
        blend(base, out, counts, mine, (i, i + pairs), both, up(i) + late, cap)


def whole(array):
    return pl.BlockSpec(array.shape, lambda i: (0,) * array.ndim)


def combine(mine, counts, base, own, other, main, extras, rank):
    packs = pl.BlockSpec((main.shape[0], 16, main.shape[2]), lambda i: (0, rank // 8, 0))
    pack = pl.BlockSpec((16, main.shape[2]), lambda i: (rank // 8, 0))
    return pl.pallas_call(
        out_kernel,
        grid=(1,),
        out_shape=jax.ShapeDtypeStruct(base.shape, jnp.bfloat16),
        in_specs=[SMEM, SMEM, whole(base), whole(own), whole(other), packs, pack, pack],
        out_specs=whole(base),
        scratch_shapes=[
            pltpu.VMEM((2 * own.shape[0] * own.shape[1], own.shape[2]), jnp.bfloat16)
        ],
        compiler_params=pltpu.CompilerParams(vmem_limit_bytes=8 << 20),
        cost_estimate=pl.CostEstimate(
            flops=base.size * rank * 2, bytes_accessed=base.size * 8, transcendentals=0
        ),
    )(mine, counts, base, own, other, main, *extras)


def on_device(
    hidden,
    value_weight,
    down_weights,
    up_weights,
    group_adapter_id,
    adapter_storage_row,
    group_live_count,
):
    dp_count = lax.axis_size("dp")
    me = lax.axis_index("dp")
    owned, rank, width = down_weights.shape
    groups = group_adapter_id.shape[0] // dp_count
    cap = hidden.shape[0] // groups
    spot = jnp.stack([me, lax.axis_index("tp")]).astype(jnp.int32)
    served, mine = index_tables(spot, group_adapter_id, adapter_storage_row, dp_count)
    counts = lax.dynamic_slice_in_dim(group_live_count, me * groups, groups)

    def wide(hidden, value_weight, down_weights, up_weights):
        stored = adapter_storage_row[group_adapter_id]
        owners = (stored // owned).reshape(dp_count, groups)
        slots = (stored % owned).reshape(dp_count, groups)
        same = owners[:, :, None] == owners[:, None, :]
        earlier = jnp.arange(groups)[None, None, :] < jnp.arange(groups)[None, :, None]
        ranking = jnp.sum(same & earlier, axis=2)
        hits = (owners == me)[:, :, None] & (ranking[:, :, None] == jnp.arange(MOST))
        rows = jnp.sum(jnp.where(hits, slots[:, :, None], 0), axis=1).reshape(-1)
        my_owners = lax.dynamic_index_in_dim(owners, me, 0, keepdims=False)
        my_ranking = lax.dynamic_index_in_dim(ranking, me, 0, keepdims=False)
        base_terms = jnp.dot(hidden, value_weight, preferred_element_type=jnp.float32)
        base = lax.psum_scatter(base_terms, "tp", scatter_dimension=1, tiled=True)
        downs = lax.all_to_all(down_weights[rows], "dp", 0, 0, tiled=True)
        ups = lax.all_to_all(up_weights[rows], "dp", 0, 0, tiled=True)
        picked = my_owners * MOST + my_ranking
        partial = jnp.einsum(
            "gcd,grd->gcr",
            hidden.reshape(groups, cap, width),
            downs[picked],
            preferred_element_type=jnp.float32,
        )
        low = low_rank_sum(partial.reshape(groups * cap, rank))
        return finish(base, low, ups[picked], counts)

    def narrow(hidden, value_weight, down_weights, up_weights):
        trees = (True, False)
        soon = [
            (tree, ((2, part[0]), (2, part[1]), (near, 2), (near, 3)))
            for tree in trees
            for near, part in ((1, (0, 1)), (3, (2, 3)))
        ]
        late = [(tree, ((near, 0), (near, 1))) for tree in trees for near in (1, 3)]
        late += [(tree, ((0, 0), (0, 1), (0, 2), (0, 3))) for tree in trees]
        moves = ((1, 0), (-1, 0), (0, 1), (0, -1))
        turned = ((0, 1), (0, 2), (0, -1), (1, 0), (2, 0), (-1, 0))
        send = lambda values, ways: [shift(v, *way) for v, way in zip(values, ways)]
        barrier = lax.optimization_barrier
        main_sent, *gathered = gather_units(soon + late, served, mine, down_weights, up_weights)
        unit, dtype = main_sent.shape[1:], main_sent.dtype
        near, homes = gathered[4:8], gathered[8:]
        fresh = barrier(send(gathered[:4], moves))
        relayed = vmem_call(
            relay_kernel, ((2,) + unit,) * 4, dtype, (mine,), (*fresh, *near)
        )
        base_hidden, _ = barrier((hidden, relayed))
        base_terms = base_product(base_hidden, value_weight)
        base = lax.psum_scatter(base_terms, "tp", scatter_dimension=1, tiled=True)
        near_a, main_sent = barrier((send(relayed, moves), main_sent))
        main = lax.all_to_all(main_sent, "dp", 0, 0, tiled=True)
        tree_arrays = [
            (homes[h], near_a[2 * h], near_a[2 * h + 1], fresh[2 * h], fresh[2 * h + 1])
            for h in range(2)
        ]
        lines = vmem_call(
            line_kernel, (unit,) * 8, dtype, (mine,), tree_arrays[0] + tree_arrays[1]
        )
        got = send(lines[1:4] + lines[5:8], turned)
        extras = vmem_call(
            pick_kernel, (unit,) * 2, dtype, (mine,), (lines[0], *got[:3], lines[4], *got[3:])
        )
        partial = low_partial(mine, hidden, main, extras, cap, rank)
        own, other = low_rank_up(low_rank_down(partial))
        return combine(mine, counts, base, own, other, main, extras, rank)

    return lax.cond(
        mine[FLAGS, FITS] == 1, narrow, wide, hidden, value_weight, down_weights, up_weights
    )


def solution(mesh):
    return jax.shard_map(
        on_device,
        mesh=mesh,
        in_specs=(
            P("dp", "tp"),
            P("tp", None),
            P("dp", None, "tp"),
            P("dp", None, "tp"),
            P(),
            P(),
            P(),
        ),
        out_specs=P("dp", "tp"),
        check_vma=False,
    )
```

```python
import functools
import math

import jax
import jax.numpy as jnp
from jax import lax
from jax.experimental import pallas as pl
from jax.experimental.pallas import tpu as pltpu
from jax.sharding import PartitionSpec as P

ADAPTER_SCALE = 0.5
MAIN = 2
MOST = 6
EXTRA = MOST - MAIN


def low_rank_sum(partial):
    rows, rank = partial.shape
    tp_count = lax.axis_size("tp")
    pieces = lax.all_to_all(partial, "tp", split_axis=0, concat_axis=0, tiled=True)
    mine = jnp.sum(pieces.reshape(tp_count, rows // tp_count, rank), axis=0).astype(jnp.bfloat16)
    return lax.all_gather(mine, "tp", axis=0, tiled=True)


def finish(base, low, ups, counts):
    groups = counts.shape[0]
    cap = base.shape[0] // groups
    delta = jnp.einsum(
        "gcr,grv->gcv", low.reshape(groups, cap, -1), ups, preferred_element_type=jnp.float32
    )
    merged = base.reshape(groups, cap, -1) + ADAPTER_SCALE * delta
    active = jnp.arange(cap)[None, :, None] < counts[:, None, None]
    out = jnp.where(active, merged, jnp.float32(0.0)).astype(jnp.bfloat16)
    return out.reshape(base.shape)


SMEM = pl.BlockSpec(memory_space=pltpu.SMEM)
VMEM = pl.BlockSpec(memory_space=pltpu.VMEM)
HBM = pl.BlockSpec(memory_space=pltpu.HBM)
LANES = 128
ORDER, PLACE, FLAGS = 0, 1, 2
HOT, FITS, AT, CHIP, CORE = 0, 1, 2, 4, 5


def shift(value, dx, dy):
    side = math.isqrt(lax.axis_size("dp"))
    pairs = [
        (x * side + y, (x + dx) % side * side + (y + dy) % side)
        for x in range(side)
        for y in range(side)
    ]
    return lax.ppermute(value, "dp", pairs)


def index_kernel(spot_ref, ids_ref, table_ref, served_ref, mine_ref, owner_ref, rank_ref):
    total = ids_ref.shape[0]
    dp_count = served_ref.shape[0]
    groups = total // dp_count
    chunks = table_ref.shape[0]
    owned = chunks * LANES // dp_count
    me = spot_ref[0]
    f32, bf16 = jnp.float32, jnp.bfloat16
    ids = ids_ref[...]
    lane = lax.broadcasted_iota(jnp.int32, (total, LANES), 1)
    found = jnp.zeros((total, LANES), jnp.int32)
    for c in range(chunks):
        found += jnp.where(ids == lane + c * LANES, table_ref[c : c + 1, :], 0)
    stored = jnp.sum(found, axis=1, keepdims=True)
    owner = lax.div(stored, owned)
    slot = stored - owner * owned
    holds = jnp.where(owner == lane, 1.0, 0.0)
    low = lax.broadcasted_iota(jnp.int32, (groups, groups), 0)
    low = jnp.where(low > lax.broadcasted_iota(jnp.int32, (groups, groups), 1), 1.0, 0.0)
    low = low.astype(bf16)
    holds16 = holds.astype(bf16)
    before = jnp.concatenate(
        [
            jnp.dot(low, holds16[r * groups : (r + 1) * groups], preferred_element_type=f32)
            for r in range(dp_count)
        ],
        axis=0,
    )
    ranking = jnp.sum(before * holds, axis=1, keepdims=True).astype(jnp.int32)
    owner_ref[...] = jnp.broadcast_to(owner, (total, LANES))
    rank_ref[...] = jnp.broadcast_to(ranking, (total, LANES))
    block_of = lax.div(lax.broadcasted_iota(jnp.int32, (dp_count, total), 1), groups)
    block = block_of == lax.broadcasted_iota(jnp.int32, (dp_count, total), 0)
    block = jnp.where(block, 1.0, 0.0).astype(bf16)
    loads = jnp.dot(block, holds16, preferred_element_type=f32)
    kept = jnp.where((owner == me) & (ranking == lane), slot, 0).astype(f32).astype(bf16)
    served_ref[...] = jnp.dot(block, kept, preferred_element_type=f32).astype(jnp.int32)
    least = jnp.min(loads, axis=0, keepdims=True)
    row_lane = lax.broadcasted_iota(jnp.int32, (1, LANES), 1)
    hot = jnp.min(jnp.where(least >= MOST, row_lane, LANES), axis=1, keepdims=True)
    spare = jnp.where(row_lane == hot, 0.0, loads)
    most = jnp.max(jnp.max(spare, axis=0, keepdims=True), axis=1, keepdims=True)
    fits = jnp.where(most <= MAIN, 1, 0)
    at = pl.ds(pl.multiple_of(me * groups, groups), groups)
    my_owner = owner_ref[at, :]
    my_rank = rank_ref[at, :]
    late = (my_owner == hot) & (my_rank >= MAIN)
    place = jnp.where(late, dp_count * MAIN + my_rank - MAIN, my_owner * MAIN + my_rank)
    early = jnp.where(late, 0.0, 1.0).astype(bf16)
    ahead = jnp.dot(low, early, preferred_element_type=f32).astype(jnp.int32)
    turn = jnp.where(late, groups - EXTRA + my_rank - MAIN, ahead)
    group_lane = lax.broadcasted_iota(jnp.int32, (groups, LANES), 1)
    group = lax.broadcasted_iota(jnp.int32, (groups, LANES), 0)
    here = turn == group_lane
    mine_ref[...] = jnp.zeros(mine_ref.shape, jnp.int32)
    mine_ref[ORDER : ORDER + 1, :] = jnp.sum(jnp.where(here, group, 0), axis=0, keepdims=True)
    mine_ref[PLACE : PLACE + 1, :] = jnp.sum(jnp.where(here, place, 0), axis=0, keepdims=True)
    side = math.isqrt(dp_count)
    x, y = lax.div(me, side), lax.rem(me, side)
    flags = (
        (HOT, hot),
        (FITS, fits),
        (AT, lax.rem(x - lax.div(hot, side) + side, side)),
        (AT + 1, lax.rem(y - lax.rem(hot, side) + side, side)),
        (CHIP, lax.div(spot_ref[1], 2)),
        (CORE, lax.rem(spot_ref[1], 2)),
    )
    row = jnp.zeros((1, LANES), jnp.int32)
    for at, value in flags:
        row = jnp.where(row_lane == at, value, row)
    mine_ref[FLAGS : FLAGS + 1, :] = row


def index_tables(spot, ids, table, dp_count):
    total = ids.shape[0]
    return pl.pallas_call(
        index_kernel,
        out_shape=(
            jax.ShapeDtypeStruct((dp_count, LANES), jnp.int32),
            jax.ShapeDtypeStruct((8, LANES), jnp.int32),
        ),
        in_specs=[SMEM, VMEM, VMEM],
        out_specs=(VMEM, VMEM),
        scratch_shapes=[pltpu.VMEM((total, LANES), jnp.int32)] * 2,
        compiler_params=pltpu.CompilerParams(vmem_limit_bytes=8 << 20),
    )(spot, ids.reshape(total, 1), table.reshape(-1, LANES))


def copy_units(wanted, down, up, up_in, down_sem, up_sem):
    rank = down.shape[1]
    lanes = up.shape[2]
    steps = rank // 16
    downs, ups = [], []
    for i, (dest, index, rows) in enumerate(wanted):
        for half in range(2):
            n = 2 * i + half
            ups.append(pltpu.make_async_copy(up.at[rows[half]], up_in.at[n], up_sem.at[n]))
            ups[-1].start()
            downs.append(
                pltpu.make_async_copy(
                    down.at[rows[half]], dest.at[index, pl.ds(half * rank, rank)], down_sem.at[n]
                )
            )
            downs[-1].start()
    for i, (dest, index, rows) in enumerate(wanted):
        for half in range(2):
            n = 2 * i + half
            ups[n].wait()
            for part in range(steps):
                at = (half * steps + part) * lanes
                dest[index, 2 * rank : 2 * rank + 16, at : at + lanes] = up_in[
                    n, part * 16 : part * 16 + 16, :
                ]
    for copy in downs:
        copy.wait()


def main_kernel(served, mine, down, up, out, *scratch):
    rows = [(served[p, 0], served[p, 1]) for p in range(out.shape[0])]
    copy_units([(out, p, pair) for p, pair in enumerate(rows)], down, up, *scratch)


def extra_kernel(lines, served, mine, down, up, *refs):
    outs, scratch = refs[: len(lines)], refs[len(lines) :]
    dp_count = served.shape[0]
    side = math.isqrt(dp_count)
    hot = mine[FLAGS, HOT]

    @pl.when((mine[FLAGS, AT] == 0) & (mine[FLAGS, AT + 1] == 0))
    def _():
        hot_x, hot_y = lax.div(hot, side), lax.rem(hot, side)
        wanted = []
        for out, (x_first, units) in zip(outs, lines):
            for i, (a, b) in enumerate(units):
                dx, dy = (a, b) if x_first else (b, a)
                peer = lax.rem(hot_x + dx, side) * side + lax.rem(hot_y + dy, side)
                first = MAIN if x_first else MAIN + 2
                wanted.append((out, i, (served[peer, first], served[peer, first + 1])))
        copy_units(wanted, down, up, *scratch)


def gather_units(kernel, shapes, served, mine, down, up):
    _, rank, width = down.shape
    lanes = up.shape[2]
    count = sum(shapes)
    return pl.pallas_call(
        kernel,
        out_shape=[jax.ShapeDtypeStruct((n, 2 * rank + 16, width), down.dtype) for n in shapes],
        in_specs=[SMEM, SMEM, HBM, HBM],
        out_specs=[VMEM] * len(shapes),
        scratch_shapes=[
            pltpu.VMEM((2 * count, rank, lanes), up.dtype),
            pltpu.SemaphoreType.DMA((2 * count,)),
            pltpu.SemaphoreType.DMA((2 * count,)),
        ],
        compiler_params=pltpu.CompilerParams(vmem_limit_bytes=(count // 2 << 20)),
        cost_estimate=pl.CostEstimate(
            flops=0, bytes_accessed=count * rank * (width + lanes) * 8, transcendentals=0
        ),
    )(served, mine, down, up)


def vmem_call(kernel, shapes, dtype, scalars, arrays, limit=10):
    return pl.pallas_call(
        kernel,
        out_shape=[jax.ShapeDtypeStruct(shape, dtype) for shape in shapes],
        in_specs=[SMEM] * len(scalars) + [VMEM] * len(arrays),
        out_specs=[VMEM] * len(shapes),
        compiler_params=pltpu.CompilerParams(vmem_limit_bytes=limit << 20),
        cost_estimate=pl.CostEstimate(
            flops=0,
            bytes_accessed=sum(math.prod(shape) for shape in shapes) * 4,
            transcendentals=0,
        ),
    )(*scalars, *arrays)


def move(dst, src):
    rows = src.shape[0]

    def body(i, carry):
        at = pl.ds(pl.multiple_of(i * 16, 16), 16)
        dst[at, :] = src[at, :]
        return carry

    lax.fori_loop(0, rows // 16, body, 0, unroll=3)


def relay_kernel(mine, *refs):
    fresh, near, outs = refs[:4], refs[4:8], refs[8:]
    for i in range(4):
        at = mine[FLAGS, AT + i // 2]
        close = 1 if i % 2 == 0 else 3
        for source, when in ((near[i], at != close), (fresh[i], at == close)):

            @pl.when(when)
            def _(source=source, out=outs[i]):
                for u in range(2):
                    move(out.at[u], source.at[u])


def line_kernel(mine, *refs):
    outs = refs[10:]
    for h in range(2):
        own, plus_a, minus_a, plus_b, minus_b = refs[5 * h : 5 * h + 5]
        out = outs[4 * h : 4 * h + 4]
        at = mine[FLAGS, AT + h]
        low, high = own.at[pl.ds(0, 2)], own.at[pl.ds(2, 2)]
        plus_b, minus_b = plus_b.at[pl.ds(2, 2)], minus_b.at[pl.ds(2, 2)]
        picks = ((low, high), (plus_a, plus_b), (plus_a, minus_a), (minus_a, minus_b))
        for offset, (first, second) in enumerate(picks):

            @pl.when(at == offset)
            def _(first=first, second=second, out=out):
                for u in range(2):
                    move(out[u], first.at[u])
                    move(out[2 + u], second.at[u])


def pick_kernel(mine, *refs):
    for h in range(2):
        at = mine[FLAGS, AT + 1 - h]
        for offset, source in enumerate(refs[4 * h : 4 * h + 4]):

            @pl.when(at == offset)
            def _(source=source, out=refs[8 + h]):
                move(out, source)


def base_kernel(hidden, weight, out):
    out[...] = jnp.dot(hidden[...], weight[...], preferred_element_type=jnp.float32)


def base_product(hidden, weight, block=256):
    rows, width = hidden.shape
    columns = weight.shape[1]
    return pl.pallas_call(
        base_kernel,
        grid=(rows // block,),
        out_shape=jax.ShapeDtypeStruct((rows, columns), jnp.float32),
        in_specs=[
            pl.BlockSpec((block, width), lambda i: (i, 0)),
            pl.BlockSpec((width, columns), lambda i: (0, 0)),
        ],
        out_specs=pl.BlockSpec((block, columns), lambda i: (i, 0)),
        compiler_params=pltpu.CompilerParams(vmem_limit_bytes=14 << 20),
        cost_estimate=pl.CostEstimate(
            flops=2 * rows * width * columns,
            bytes_accessed=hidden.size * 2 + weight.size * 2 + rows * columns * 4,
            transcendentals=0,
        ),
    )(hidden, weight)


def paired(hidden, mine, groups, cap, first, second):
    spots = [pl.multiple_of(mine[ORDER, j] * cap, cap) for j in groups]
    rows = jnp.concatenate([hidden[pl.ds(spot, cap), :] for spot in spots], axis=0)
    product = lax.dot_general(
        rows,
        jnp.concatenate([first, second], axis=0),
        (((1,), (1,)), ((), ())),
        preferred_element_type=jnp.float32,
    )
    lane = lax.broadcasted_iota(jnp.int32, (cap, product.shape[1]), 1)
    return jnp.where(lane < first.shape[0], product[:cap], product[cap:])


def low_main_kernel(cap, mine, hidden, main, out):
    rank = out.shape[1] // 2
    pairs = out.shape[0] // cap - EXTRA // 2

    def weights(j):
        place = mine[PLACE, j]
        unit = lax.div(place, 2)
        return main[unit, pl.ds(pl.multiple_of((place - 2 * unit) * rank, rank), rank), :]

    def body(i, carry):
        at = pl.ds(pl.multiple_of(i * cap, cap), cap)
        spots = (i, i + pairs)
        out[at, :] = paired(hidden, mine, spots, cap, weights(i), weights(i + pairs))
        return carry

    lax.fori_loop(0, pairs, body, 0, unroll=2)


def low_extra_kernel(cap, mine, hidden, first, second, _, out):
    rank = out.shape[1] // 2
    pairs = out.shape[0] // cap
    for e in range(EXTRA // 2):
        spots = (2 * pairs - EXTRA + e, 2 * pairs - EXTRA // 2 + e)
        at = (pairs - EXTRA // 2 + e) * cap
        part = slice(e * rank, (e + 1) * rank)
        out[at : at + cap, :] = paired(
            hidden, mine, spots, cap, first[part, :], second[part, :]
        )


def low_call(kernel, cap, rank, mine, hidden, arrays, aliases):
    pairs = hidden.shape[0] // cap // 2
    return pl.pallas_call(
        functools.partial(kernel, cap),
        out_shape=jax.ShapeDtypeStruct((pairs * cap, 2 * rank), jnp.float32),
        in_specs=[SMEM] + [VMEM] * (1 + len(arrays)),
        out_specs=VMEM,
        input_output_aliases=aliases,
        compiler_params=pltpu.CompilerParams(vmem_limit_bytes=12 << 20),
        cost_estimate=pl.CostEstimate(
            flops=pairs * cap * rank * 4 * hidden.shape[1],
            bytes_accessed=sum(array.size for array in arrays) * 2,
            transcendentals=0,
        ),
    )(mine, hidden, *arrays)


def turn(step):
    tp_count = lax.axis_size("tp")
    return [(i, (i + 2 * step) % tp_count) for i in range(tp_count)]


def swap():
    return [(i, i ^ 1) for i in range(lax.axis_size("tp"))]


def low_rank_down(partial):
    chips = lax.axis_size("tp") // 2
    t = lax.axis_index("tp")
    z, core = t // 2, t % 2
    half = partial.shape[0] // 2
    piece = half // chips
    cut = lambda array, start, size: lax.dynamic_slice_in_dim(array, start, size, 0)
    total = cut(partial, core * half, half) + lax.ppermute(
        cut(partial, (1 - core) * half, half), "tp", swap()
    )
    pieces = [
        lax.ppermute(cut(total, (z + d) % chips * piece, piece), "tp", turn(d))
        for d in range(1, chips)
    ]
    return (cut(total, z * piece, piece) + sum(pieces)).astype(jnp.bfloat16)


def low_rank_up(summed):
    chips = lax.axis_size("tp") // 2
    own = jnp.stack([summed] + [lax.ppermute(summed, "tp", turn(d)) for d in range(1, chips)])
    return own, lax.ppermute(own, "tp", swap())


def blend(base, out, counts, mine, j, both, ups, cap):
    rank = both.shape[1] // 2
    lane = lax.broadcasted_iota(jnp.int32, both.shape, 1)
    none = jnp.zeros_like(both)
    left = jnp.concatenate(
        [jnp.where(lane < rank, both, none), jnp.where(lane < rank, none, both)], axis=0
    )
    delta = jnp.dot(left, jnp.concatenate(ups, axis=0), preferred_element_type=jnp.float32)
    rows = lax.broadcasted_iota(jnp.int32, (cap, base.shape[1]), 0)
    for n in range(2):
        g = mine[ORDER, j[n]]
        here = pl.ds(pl.multiple_of(g * cap, cap), cap)
        merged = base[here, :] + ADAPTER_SCALE * delta[n * cap : (n + 1) * cap]
        out[here, :] = jnp.where(rows < counts[g], merged, 0.0).astype(out.dtype)


def out_kernel(mine, counts, base, own, other, main, *refs):
    extras, out, low = refs[:2], refs[2], refs[3]
    groups = counts.shape[0]
    cap = base.shape[0] // groups
    chips, piece, rank = own.shape[0], own.shape[1], own.shape[2] // 2
    lanes = base.shape[1]
    z, core = mine[FLAGS, CHIP], mine[FLAGS, CORE]
    steps = rank // 16
    pairs = (groups - EXTRA) // 2
    for d in range(chips):
        quarter = lax.rem(z - d + chips, chips)
        for ref, half in ((own, core), (other, 1 - core)):
            at = pl.multiple_of((half * chips + quarter) * piece, piece)
            low[pl.ds(at, piece), :] = ref[d]

    def up(j):
        place = mine[PLACE, j]
        unit = lax.div(place, 2)
        at = (place - 2 * unit) * steps * lanes
        return [
            main[unit, :, pl.ds(pl.multiple_of(at + part * lanes, lanes), lanes)]
            for part in range(steps)
        ]

    def body(i, carry):
        both = low[pl.ds(pl.multiple_of(i * cap, cap), cap), :]
        blend(base, out, counts, mine, (i, i + pairs), both, up(i) + up(i + pairs), cap)
        return carry

    lax.fori_loop(0, pairs, body, 0, unroll=2)
    for e in range(EXTRA // 2):
        ups = [
            pack[:, (e * steps + part) * lanes : (e * steps + part + 1) * lanes]
            for pack in extras
            for part in range(steps)
        ]
        both = low[(pairs + e) * cap : (pairs + e + 1) * cap, :]
        spots = (groups - EXTRA + e, groups - EXTRA // 2 + e)
        blend(base, out, counts, mine, spots, both, ups, cap)


def whole(array):
    return pl.BlockSpec(array.shape, lambda i: (0,) * array.ndim)


def combine(mine, counts, base, own, other, main, extras, rank):
    packs = pl.BlockSpec((main.shape[0], 16, main.shape[2]), lambda i: (0, rank // 8, 0))
    pack = pl.BlockSpec((16, main.shape[2]), lambda i: (rank // 8, 0))
    return pl.pallas_call(
        out_kernel,
        grid=(1,),
        out_shape=jax.ShapeDtypeStruct(base.shape, jnp.bfloat16),
        in_specs=[SMEM, SMEM, whole(base), whole(own), whole(other), packs, pack, pack],
        out_specs=whole(base),
        scratch_shapes=[
            pltpu.VMEM((2 * own.shape[0] * own.shape[1], own.shape[2]), jnp.bfloat16)
        ],
        compiler_params=pltpu.CompilerParams(vmem_limit_bytes=8 << 20),
        cost_estimate=pl.CostEstimate(
            flops=base.size * rank * 2, bytes_accessed=base.size * 8, transcendentals=0
        ),
    )(mine, counts, base, own, other, main, *extras)


def on_device(
    hidden,
    value_weight,
    down_weights,
    up_weights,
    group_adapter_id,
    adapter_storage_row,
    group_live_count,
):
    dp_count = lax.axis_size("dp")
    me = lax.axis_index("dp")
    owned, rank, width = down_weights.shape
    groups = group_adapter_id.shape[0] // dp_count
    cap = hidden.shape[0] // groups
    spot = jnp.stack([me, lax.axis_index("tp")]).astype(jnp.int32)
    served, mine = index_tables(spot, group_adapter_id, adapter_storage_row, dp_count)
    counts = lax.dynamic_slice_in_dim(group_live_count, me * groups, groups)

    def wide(hidden, value_weight, down_weights, up_weights):
        stored = adapter_storage_row[group_adapter_id]
        owners = (stored // owned).reshape(dp_count, groups)
        slots = (stored % owned).reshape(dp_count, groups)
        same = owners[:, :, None] == owners[:, None, :]
        earlier = jnp.arange(groups)[None, None, :] < jnp.arange(groups)[None, :, None]
        ranking = jnp.sum(same & earlier, axis=2)
        hits = (owners == me)[:, :, None] & (ranking[:, :, None] == jnp.arange(MOST))
        rows = jnp.sum(jnp.where(hits, slots[:, :, None], 0), axis=1).reshape(-1)
        my_owners = lax.dynamic_index_in_dim(owners, me, 0, keepdims=False)
        my_ranking = lax.dynamic_index_in_dim(ranking, me, 0, keepdims=False)
        base_terms = jnp.dot(hidden, value_weight, preferred_element_type=jnp.float32)
        base = lax.psum_scatter(base_terms, "tp", scatter_dimension=1, tiled=True)
        downs = lax.all_to_all(down_weights[rows], "dp", 0, 0, tiled=True)
        ups = lax.all_to_all(up_weights[rows], "dp", 0, 0, tiled=True)
        picked = my_owners * MOST + my_ranking
        partial = jnp.einsum(
            "gcd,grd->gcr",
            hidden.reshape(groups, cap, width),
            downs[picked],
            preferred_element_type=jnp.float32,
        )
        low = low_rank_sum(partial.reshape(groups * cap, rank))
        return finish(base, low, ups[picked], counts)

    def narrow(hidden, value_weight, down_weights, up_weights):
        trees = (True, False)
        soon = [
            (tree, ((2, part[0]), (2, part[1]), (near, 2), (near, 3)))
            for tree in trees
            for near, part in ((1, (0, 1)), (3, (2, 3)))
        ]
        late = [(tree, ((near, 0), (near, 1))) for tree in trees for near in (1, 3)]
        late += [(tree, ((0, 0), (0, 1), (0, 2), (0, 3))) for tree in trees]
        moves = ((1, 0), (-1, 0), (0, 1), (0, -1))
        turned = ((0, 1), (0, 2), (0, -1), (1, 0), (2, 0), (-1, 0))
        send = lambda values, ways: [shift(v, *way) for v, way in zip(values, ways)]
        barrier = lax.optimization_barrier
        (main_sent,) = gather_units(
            main_kernel, [dp_count], served, mine, down_weights, up_weights
        )
        main = lax.all_to_all(main_sent, "dp", 0, 0, tiled=True)
        unit, dtype = main_sent.shape[1:], main_sent.dtype
        later_served, _ = barrier((served, main_sent))
        wanted = soon + late
        gathered = gather_units(
            functools.partial(extra_kernel, wanted),
            [len(units) for _, units in wanted],
            later_served,
            mine,
            down_weights,
            up_weights,
        )
        near, homes = gathered[4:8], gathered[8:]
        fresh = send(gathered[:4], moves)
        base_hidden, _ = barrier((hidden, gathered))
        base_terms = base_product(base_hidden, value_weight)
        main, fresh, base_terms = barrier((main, fresh, base_terms))
        base = lax.psum_scatter(base_terms, "tp", scatter_dimension=1, tiled=True)
        partial = low_call(low_main_kernel, cap, rank, mine, hidden, (main,), {})
        relayed = vmem_call(
            relay_kernel, ((2,) + unit,) * 4, dtype, (mine,), (*fresh, *near)
        )
        near_a, partial = barrier((send(relayed, moves), partial))
        tree_arrays = [
            (homes[h], near_a[2 * h], near_a[2 * h + 1], fresh[2 * h], fresh[2 * h + 1])
            for h in range(2)
        ]
        lines = vmem_call(
            line_kernel, (unit,) * 8, dtype, (mine,), tree_arrays[0] + tree_arrays[1]
        )
        got = send(lines[1:4] + lines[5:8], turned)
        extras = vmem_call(
            pick_kernel, (unit,) * 2, dtype, (mine,), (lines[0], *got[:3], lines[4], *got[3:])
        )
        partial = low_call(
            low_extra_kernel, cap, rank, mine, hidden, (*extras, partial), {4: 0}
        )
        own, other = low_rank_up(low_rank_down(partial))
        return combine(mine, counts, base, own, other, main, extras, rank)

    return lax.cond(
        mine[FLAGS, FITS] == 1, narrow, wide, hidden, value_weight, down_weights, up_weights
    )


def solution(mesh):
    return jax.shard_map(
        on_device,
        mesh=mesh,
        in_specs=(
            P("dp", "tp"),
            P("tp", None),
            P("dp", None, "tp"),
            P("dp", None, "tp"),
            P(),
            P(),
            P(),
        ),
        out_specs=P("dp", "tp"),
        check_vma=False,
    )
```

```python
import functools
import math

import jax
import jax.numpy as jnp
from jax import lax
from jax.experimental import pallas as pl
from jax.experimental.pallas import tpu as pltpu
from jax.sharding import PartitionSpec as P

ADAPTER_SCALE = 0.5
MAIN = 2
MOST = 6
EXTRA = MOST - MAIN


def low_rank_sum(partial):
    rows, rank = partial.shape
    tp_count = lax.axis_size("tp")
    pieces = lax.all_to_all(partial, "tp", split_axis=0, concat_axis=0, tiled=True)
    mine = jnp.sum(pieces.reshape(tp_count, rows // tp_count, rank), axis=0).astype(jnp.bfloat16)
    return lax.all_gather(mine, "tp", axis=0, tiled=True)


def finish(base, low, ups, counts):
    groups = counts.shape[0]
    cap = base.shape[0] // groups
    delta = jnp.einsum(
        "gcr,grv->gcv", low.reshape(groups, cap, -1), ups, preferred_element_type=jnp.float32
    )
    merged = base.reshape(groups, cap, -1) + ADAPTER_SCALE * delta
    active = jnp.arange(cap)[None, :, None] < counts[:, None, None]
    out = jnp.where(active, merged, jnp.float32(0.0)).astype(jnp.bfloat16)
    return out.reshape(base.shape)


SMEM = pl.BlockSpec(memory_space=pltpu.SMEM)
VMEM = pl.BlockSpec(memory_space=pltpu.VMEM)
HBM = pl.BlockSpec(memory_space=pltpu.HBM)
LANES = 128
ORDER, PLACE, FLAGS = 0, 1, 2
HOT, FITS, AT, CHIP, CORE = 0, 1, 2, 4, 5


def shift(value, dx, dy):
    side = math.isqrt(lax.axis_size("dp"))
    pairs = [
        (x * side + y, (x + dx) % side * side + (y + dy) % side)
        for x in range(side)
        for y in range(side)
    ]
    return lax.ppermute(value, "dp", pairs)


def index_kernel(spot_ref, ids_ref, table_ref, served_ref, mine_ref, owner_ref, rank_ref):
    total = ids_ref.shape[0]
    dp_count = served_ref.shape[0]
    groups = total // dp_count
    chunks = table_ref.shape[0]
    owned = chunks * LANES // dp_count
    me = spot_ref[0]
    f32, bf16 = jnp.float32, jnp.bfloat16
    ids = ids_ref[...]
    lane = lax.broadcasted_iota(jnp.int32, (total, LANES), 1)
    found = jnp.zeros((total, LANES), jnp.int32)
    for c in range(chunks):
        found += jnp.where(ids == lane + c * LANES, table_ref[c : c + 1, :], 0)
    stored = jnp.sum(found, axis=1, keepdims=True)
    owner = lax.div(stored, owned)
    slot = stored - owner * owned
    holds = jnp.where(owner == lane, 1.0, 0.0)
    low = lax.broadcasted_iota(jnp.int32, (groups, groups), 0)
    low = jnp.where(low > lax.broadcasted_iota(jnp.int32, (groups, groups), 1), 1.0, 0.0)
    low = low.astype(bf16)
    holds16 = holds.astype(bf16)
    before = jnp.concatenate(
        [
            jnp.dot(low, holds16[r * groups : (r + 1) * groups], preferred_element_type=f32)
            for r in range(dp_count)
        ],
        axis=0,
    )
    ranking = jnp.sum(before * holds, axis=1, keepdims=True).astype(jnp.int32)
    owner_ref[...] = jnp.broadcast_to(owner, (total, LANES))
    rank_ref[...] = jnp.broadcast_to(ranking, (total, LANES))
    block_of = lax.div(lax.broadcasted_iota(jnp.int32, (dp_count, total), 1), groups)
    block = block_of == lax.broadcasted_iota(jnp.int32, (dp_count, total), 0)
    block = jnp.where(block, 1.0, 0.0).astype(bf16)
    loads = jnp.dot(block, holds16, preferred_element_type=f32)
    kept = jnp.where((owner == me) & (ranking == lane), slot, 0).astype(f32).astype(bf16)
    served_ref[...] = jnp.dot(block, kept, preferred_element_type=f32).astype(jnp.int32)
    least = jnp.min(loads, axis=0, keepdims=True)
    row_lane = lax.broadcasted_iota(jnp.int32, (1, LANES), 1)
    hot = jnp.min(jnp.where(least >= MOST, row_lane, LANES), axis=1, keepdims=True)
    spare = jnp.where(row_lane == hot, 0.0, loads)
    most = jnp.max(jnp.max(spare, axis=0, keepdims=True), axis=1, keepdims=True)
    fits = jnp.where(most <= MAIN, 1, 0)
    at = pl.ds(pl.multiple_of(me * groups, groups), groups)
    my_owner = owner_ref[at, :]
    my_rank = rank_ref[at, :]
    late = (my_owner == hot) & (my_rank >= MAIN)
    place = jnp.where(late, dp_count * MAIN + my_rank - MAIN, my_owner * MAIN + my_rank)
    early = jnp.where(late, 0.0, 1.0).astype(bf16)
    ahead = jnp.dot(low, early, preferred_element_type=f32).astype(jnp.int32)
    turn = jnp.where(late, groups - EXTRA + my_rank - MAIN, ahead)
    group_lane = lax.broadcasted_iota(jnp.int32, (groups, LANES), 1)
    group = lax.broadcasted_iota(jnp.int32, (groups, LANES), 0)
    here = turn == group_lane
    mine_ref[...] = jnp.zeros(mine_ref.shape, jnp.int32)
    mine_ref[ORDER : ORDER + 1, :] = jnp.sum(jnp.where(here, group, 0), axis=0, keepdims=True)
    mine_ref[PLACE : PLACE + 1, :] = jnp.sum(jnp.where(here, place, 0), axis=0, keepdims=True)
    side = math.isqrt(dp_count)
    x, y = lax.div(me, side), lax.rem(me, side)
    flags = (
        (HOT, hot),
        (FITS, fits),
        (AT, lax.rem(x - lax.div(hot, side) + side, side)),
        (AT + 1, lax.rem(y - lax.rem(hot, side) + side, side)),
        (CHIP, lax.div(spot_ref[1], 2)),
        (CORE, lax.rem(spot_ref[1], 2)),
    )
    row = jnp.zeros((1, LANES), jnp.int32)
    for at, value in flags:
        row = jnp.where(row_lane == at, value, row)
    mine_ref[FLAGS : FLAGS + 1, :] = row


def index_tables(spot, ids, table, dp_count):
    total = ids.shape[0]
    return pl.pallas_call(
        index_kernel,
        out_shape=(
            jax.ShapeDtypeStruct((dp_count, LANES), jnp.int32),
            jax.ShapeDtypeStruct((8, LANES), jnp.int32),
        ),
        in_specs=[SMEM, VMEM, VMEM],
        out_specs=(VMEM, VMEM),
        scratch_shapes=[pltpu.VMEM((total, LANES), jnp.int32)] * 2,
        compiler_params=pltpu.CompilerParams(vmem_limit_bytes=8 << 20),
    )(spot, ids.reshape(total, 1), table.reshape(-1, LANES))


def copy_units(wanted, down, up, up_in, down_sem, up_sem):
    rank = down.shape[1]
    lanes = up.shape[2]
    steps = rank // 16
    downs, ups = [], []
    for i, (dest, index, rows) in enumerate(wanted):
        for half in range(2):
            n = 2 * i + half
            ups.append(pltpu.make_async_copy(up.at[rows[half]], up_in.at[n], up_sem.at[n]))
            ups[-1].start()
            downs.append(
                pltpu.make_async_copy(
                    down.at[rows[half]], dest.at[index, pl.ds(half * rank, rank)], down_sem.at[n]
                )
            )
            downs[-1].start()
    for i, (dest, index, rows) in enumerate(wanted):
        for half in range(2):
            n = 2 * i + half
            ups[n].wait()
            for part in range(steps):
                at = (half * steps + part) * lanes
                dest[index, 2 * rank : 2 * rank + 16, at : at + lanes] = up_in[
                    n, part * 16 : part * 16 + 16, :
                ]
    for copy in downs:
        copy.wait()


def extra_rows(lines, outs, served, mine):
    side = math.isqrt(served.shape[0])
    hot = mine[FLAGS, HOT]
    hot_x, hot_y = lax.div(hot, side), lax.rem(hot, side)
    wanted = []
    for out, (x_first, units) in zip(outs, lines):
        for i, (a, b) in enumerate(units):
            dx, dy = (a, b) if x_first else (b, a)
            peer = lax.rem(hot_x + dx, side) * side + lax.rem(hot_y + dy, side)
            first = MAIN if x_first else MAIN + 2
            wanted.append((out, i, (served[peer, first], served[peer, first + 1])))
    return wanted


def extra_kernel(lines, served, mine, down, up, *refs):
    outs, scratch = refs[: len(lines)], refs[len(lines) :]

    @pl.when((mine[FLAGS, AT] == 0) & (mine[FLAGS, AT + 1] == 0))
    def _():
        copy_units(extra_rows(lines, outs, served, mine), down, up, *scratch)


def gather_kernel(lines, served, mine, down, up, main, *refs):
    extra_kernel(lines, served, mine, down, up, *refs)
    rows = [(served[p, 0], served[p, 1]) for p in range(main.shape[0])]
    wanted = [(main, p, pair) for p, pair in enumerate(rows)]
    copy_units(wanted, down, up, *refs[len(lines) :])


def gather_units(kernel, shapes, served, mine, down, up):
    _, rank, width = down.shape
    lanes = up.shape[2]
    count = 16
    return pl.pallas_call(
        kernel,
        out_shape=[jax.ShapeDtypeStruct((n, 2 * rank + 16, width), down.dtype) for n in shapes],
        in_specs=[SMEM, SMEM, HBM, HBM],
        out_specs=[VMEM] * len(shapes),
        scratch_shapes=[
            pltpu.VMEM((2 * count, rank, lanes), up.dtype),
            pltpu.SemaphoreType.DMA((2 * count,)),
            pltpu.SemaphoreType.DMA((2 * count,)),
        ],
        compiler_params=pltpu.CompilerParams(vmem_limit_bytes=14 << 20),
        cost_estimate=pl.CostEstimate(
            flops=0, bytes_accessed=count * rank * (width + lanes) * 8, transcendentals=0
        ),
    )(served, mine, down, up)


def vmem_call(kernel, shapes, dtype, scalars, arrays, limit=10):
    return pl.pallas_call(
        kernel,
        out_shape=[jax.ShapeDtypeStruct(shape, dtype) for shape in shapes],
        in_specs=[SMEM] * len(scalars) + [VMEM] * len(arrays),
        out_specs=[VMEM] * len(shapes),
        compiler_params=pltpu.CompilerParams(vmem_limit_bytes=limit << 20),
        cost_estimate=pl.CostEstimate(
            flops=0,
            bytes_accessed=sum(math.prod(shape) for shape in shapes) * 4,
            transcendentals=0,
        ),
    )(*scalars, *arrays)


def move(dst, src):
    rows = src.shape[0]

    def body(i, carry):
        at = pl.ds(pl.multiple_of(i * 16, 16), 16)
        dst[at, :] = src[at, :]
        return carry

    lax.fori_loop(0, rows // 16, body, 0, unroll=3)


def relay_kernel(mine, *refs):
    fresh, near, outs = refs[:4], refs[4:8], refs[8:]
    for i in range(4):
        at = mine[FLAGS, AT + i // 2]
        close = 1 if i % 2 == 0 else 3
        for source, when in ((near[i], at != close), (fresh[i], at == close)):

            @pl.when(when)
            def _(source=source, out=outs[i]):
                for u in range(2):
                    move(out.at[u], source.at[u])


def line_kernel(mine, *refs):
    outs = refs[10:]
    for h in range(2):
        own, plus_a, minus_a, plus_b, minus_b = refs[5 * h : 5 * h + 5]
        out = outs[4 * h : 4 * h + 4]
        at = mine[FLAGS, AT + h]
        low, high = own.at[pl.ds(0, 2)], own.at[pl.ds(2, 2)]
        plus_b, minus_b = plus_b.at[pl.ds(2, 2)], minus_b.at[pl.ds(2, 2)]
        picks = ((low, high), (plus_a, plus_b), (plus_a, minus_a), (minus_a, minus_b))
        for offset, (first, second) in enumerate(picks):

            @pl.when(at == offset)
            def _(first=first, second=second, out=out):
                for u in range(2):
                    move(out[u], first.at[u])
                    move(out[2 + u], second.at[u])


def pick_kernel(mine, *refs):
    for h in range(2):
        at = mine[FLAGS, AT + 1 - h]
        for offset, source in enumerate(refs[4 * h : 4 * h + 4]):

            @pl.when(at == offset)
            def _(source=source, out=refs[8 + h]):
                move(out, source)


def base_kernel(hidden, weight, out):
    out[...] = jnp.dot(hidden[...], weight[...], preferred_element_type=jnp.float32)


def base_product(hidden, weight, block=256):
    rows, width = hidden.shape
    columns = weight.shape[1]
    return pl.pallas_call(
        base_kernel,
        grid=(rows // block,),
        out_shape=jax.ShapeDtypeStruct((rows, columns), jnp.float32),
        in_specs=[
            pl.BlockSpec((block, width), lambda i: (i, 0)),
            pl.BlockSpec((width, columns), lambda i: (0, 0)),
        ],
        out_specs=pl.BlockSpec((block, columns), lambda i: (i, 0)),
        compiler_params=pltpu.CompilerParams(vmem_limit_bytes=14 << 20),
        cost_estimate=pl.CostEstimate(
            flops=2 * rows * width * columns,
            bytes_accessed=hidden.size * 2 + weight.size * 2 + rows * columns * 4,
            transcendentals=0,
        ),
    )(hidden, weight)


def paired(hidden, mine, groups, cap, first, second):
    spots = [pl.multiple_of(mine[ORDER, j] * cap, cap) for j in groups]
    rows = jnp.concatenate([hidden[pl.ds(spot, cap), :] for spot in spots], axis=0)
    product = lax.dot_general(
        rows,
        jnp.concatenate([first, second], axis=0),
        (((1,), (1,)), ((), ())),
        preferred_element_type=jnp.float32,
    )
    lane = lax.broadcasted_iota(jnp.int32, (cap, product.shape[1]), 1)
    return jnp.where(lane < first.shape[0], product[:cap], product[cap:])


def low_main_kernel(cap, mine, hidden, main, out):
    rank = out.shape[1] // 2
    pairs = out.shape[0] // cap - EXTRA // 2

    def weights(j):
        place = mine[PLACE, j]
        unit = lax.div(place, 2)
        return main[unit, pl.ds(pl.multiple_of((place - 2 * unit) * rank, rank), rank), :]

    def body(i, carry):
        at = pl.ds(pl.multiple_of(i * cap, cap), cap)
        spots = (i, i + pairs)
        out[at, :] = paired(hidden, mine, spots, cap, weights(i), weights(i + pairs))
        return carry

    lax.fori_loop(0, pairs, body, 0, unroll=2)


def low_extra_kernel(cap, mine, hidden, first, second, _, out):
    rank = out.shape[1] // 2
    pairs = out.shape[0] // cap
    for e in range(EXTRA // 2):
        spots = (2 * pairs - EXTRA + e, 2 * pairs - EXTRA // 2 + e)
        at = (pairs - EXTRA // 2 + e) * cap
        part = slice(e * rank, (e + 1) * rank)
        out[at : at + cap, :] = paired(
            hidden, mine, spots, cap, first[part, :], second[part, :]
        )


def low_call(kernel, cap, rank, mine, hidden, arrays, aliases):
    pairs = hidden.shape[0] // cap // 2
    return pl.pallas_call(
        functools.partial(kernel, cap),
        out_shape=jax.ShapeDtypeStruct((pairs * cap, 2 * rank), jnp.float32),
        in_specs=[SMEM] + [VMEM] * (1 + len(arrays)),
        out_specs=VMEM,
        input_output_aliases=aliases,
        compiler_params=pltpu.CompilerParams(vmem_limit_bytes=12 << 20),
        cost_estimate=pl.CostEstimate(
            flops=pairs * cap * rank * 4 * hidden.shape[1],
            bytes_accessed=sum(array.size for array in arrays) * 2,
            transcendentals=0,
        ),
    )(mine, hidden, *arrays)


def turn(step):
    tp_count = lax.axis_size("tp")
    return [(i, (i + 2 * step) % tp_count) for i in range(tp_count)]


def swap():
    return [(i, i ^ 1) for i in range(lax.axis_size("tp"))]


def low_rank_down(partial):
    chips = lax.axis_size("tp") // 2
    t = lax.axis_index("tp")
    z, core = t // 2, t % 2
    half = partial.shape[0] // 2
    piece = half // chips
    cut = lambda array, start, size: lax.dynamic_slice_in_dim(array, start, size, 0)
    total = cut(partial, core * half, half) + lax.ppermute(
        cut(partial, (1 - core) * half, half), "tp", swap()
    )
    pieces = [
        lax.ppermute(cut(total, (z + d) % chips * piece, piece), "tp", turn(d))
        for d in range(1, chips)
    ]
    return (cut(total, z * piece, piece) + sum(pieces)).astype(jnp.bfloat16)


def low_rank_up(summed):
    chips = lax.axis_size("tp") // 2
    own = jnp.stack([summed] + [lax.ppermute(summed, "tp", turn(d)) for d in range(1, chips)])
    return own, lax.ppermute(own, "tp", swap())


def blend(base, out, counts, mine, j, both, ups, cap):
    rank = both.shape[1] // 2
    lane = lax.broadcasted_iota(jnp.int32, both.shape, 1)
    none = jnp.zeros_like(both)
    left = jnp.concatenate(
        [jnp.where(lane < rank, both, none), jnp.where(lane < rank, none, both)], axis=0
    )
    delta = jnp.dot(left, jnp.concatenate(ups, axis=0), preferred_element_type=jnp.float32)
    rows = lax.broadcasted_iota(jnp.int32, (cap, base.shape[1]), 0)
    for n in range(2):
        g = mine[ORDER, j[n]]
        here = pl.ds(pl.multiple_of(g * cap, cap), cap)
        merged = base[here, :] + ADAPTER_SCALE * delta[n * cap : (n + 1) * cap]
        out[here, :] = jnp.where(rows < counts[g], merged, 0.0).astype(out.dtype)


def out_kernel(mine, counts, base, own, other, main, *refs):
    extras, out, low = refs[:2], refs[2], refs[3]
    groups = counts.shape[0]
    cap = base.shape[0] // groups
    chips, piece, rank = own.shape[0], own.shape[1], own.shape[2] // 2
    lanes = base.shape[1]
    z, core = mine[FLAGS, CHIP], mine[FLAGS, CORE]
    steps = rank // 16
    pairs = (groups - EXTRA) // 2
    for d in range(chips):
        quarter = lax.rem(z - d + chips, chips)
        for ref, half in ((own, core), (other, 1 - core)):
            at = pl.multiple_of((half * chips + quarter) * piece, piece)
            low[pl.ds(at, piece), :] = ref[d]

    def up(j):
        place = mine[PLACE, j]
        unit = lax.div(place, 2)
        at = (place - 2 * unit) * steps * lanes
        return [
            main[unit, :, pl.ds(pl.multiple_of(at + part * lanes, lanes), lanes)]
            for part in range(steps)
        ]

    def body(i, carry):
        both = low[pl.ds(pl.multiple_of(i * cap, cap), cap), :]
        blend(base, out, counts, mine, (i, i + pairs), both, up(i) + up(i + pairs), cap)
        return carry

    lax.fori_loop(0, pairs, body, 0, unroll=2)
    for e in range(EXTRA // 2):
        ups = [
            pack[:, (e * steps + part) * lanes : (e * steps + part + 1) * lanes]
            for pack in extras
            for part in range(steps)
        ]
        both = low[(pairs + e) * cap : (pairs + e + 1) * cap, :]
        spots = (groups - EXTRA + e, groups - EXTRA // 2 + e)
        blend(base, out, counts, mine, spots, both, ups, cap)


def whole(array):
    return pl.BlockSpec(array.shape, lambda i: (0,) * array.ndim)


def combine(mine, counts, base, own, other, main, extras, rank):
    packs = pl.BlockSpec((main.shape[0], 16, main.shape[2]), lambda i: (0, rank // 8, 0))
    pack = pl.BlockSpec((16, main.shape[2]), lambda i: (rank // 8, 0))
    return pl.pallas_call(
        out_kernel,
        grid=(1,),
        out_shape=jax.ShapeDtypeStruct(base.shape, jnp.bfloat16),
        in_specs=[SMEM, SMEM, whole(base), whole(own), whole(other), packs, pack, pack],
        out_specs=whole(base),
        scratch_shapes=[
            pltpu.VMEM((2 * own.shape[0] * own.shape[1], own.shape[2]), jnp.bfloat16)
        ],
        compiler_params=pltpu.CompilerParams(vmem_limit_bytes=8 << 20),
        cost_estimate=pl.CostEstimate(
            flops=base.size * rank * 2, bytes_accessed=base.size * 8, transcendentals=0
        ),
    )(mine, counts, base, own, other, main, *extras)


def on_device(
    hidden,
    value_weight,
    down_weights,
    up_weights,
    group_adapter_id,
    adapter_storage_row,
    group_live_count,
):
    dp_count = lax.axis_size("dp")
    me = lax.axis_index("dp")
    owned, rank, width = down_weights.shape
    groups = group_adapter_id.shape[0] // dp_count
    cap = hidden.shape[0] // groups
    spot = jnp.stack([me, lax.axis_index("tp")]).astype(jnp.int32)
    served, mine = index_tables(spot, group_adapter_id, adapter_storage_row, dp_count)
    counts = lax.dynamic_slice_in_dim(group_live_count, me * groups, groups)

    def wide(hidden, value_weight, down_weights, up_weights):
        stored = adapter_storage_row[group_adapter_id]
        owners = (stored // owned).reshape(dp_count, groups)
        slots = (stored % owned).reshape(dp_count, groups)
        same = owners[:, :, None] == owners[:, None, :]
        earlier = jnp.arange(groups)[None, None, :] < jnp.arange(groups)[None, :, None]
        ranking = jnp.sum(same & earlier, axis=2)
        hits = (owners == me)[:, :, None] & (ranking[:, :, None] == jnp.arange(MOST))
        rows = jnp.sum(jnp.where(hits, slots[:, :, None], 0), axis=1).reshape(-1)
        my_owners = lax.dynamic_index_in_dim(owners, me, 0, keepdims=False)
        my_ranking = lax.dynamic_index_in_dim(ranking, me, 0, keepdims=False)
        base_terms = jnp.dot(hidden, value_weight, preferred_element_type=jnp.float32)
        base = lax.psum_scatter(base_terms, "tp", scatter_dimension=1, tiled=True)
        downs = lax.all_to_all(down_weights[rows], "dp", 0, 0, tiled=True)
        ups = lax.all_to_all(up_weights[rows], "dp", 0, 0, tiled=True)
        picked = my_owners * MOST + my_ranking
        partial = jnp.einsum(
            "gcd,grd->gcr",
            hidden.reshape(groups, cap, width),
            downs[picked],
            preferred_element_type=jnp.float32,
        )
        low = low_rank_sum(partial.reshape(groups * cap, rank))
        return finish(base, low, ups[picked], counts)

    def narrow(hidden, value_weight, down_weights, up_weights):
        trees = (True, False)
        soon = [
            (tree, ((2, part[0]), (2, part[1]), (near, 2), (near, 3)))
            for tree in trees
            for near, part in ((1, (0, 1)), (3, (2, 3)))
        ]
        late = [(tree, ((near, 0), (near, 1))) for tree in trees for near in (1, 3)]
        late += [(tree, ((0, 0), (0, 1), (0, 2), (0, 3))) for tree in trees]
        moves = ((1, 0), (-1, 0), (0, 1), (0, -1))
        turned = ((0, 1), (0, 2), (0, -1), (1, 0), (2, 0), (-1, 0))
        send = lambda values, ways: [shift(v, *way) for v, way in zip(values, ways)]
        barrier = lax.optimization_barrier
        main_sent, *gathered = gather_units(
            functools.partial(gather_kernel, soon),
            [dp_count] + [len(units) for _, units in soon],
            served,
            mine,
            down_weights,
            up_weights,
        )
        unit, dtype = main_sent.shape[1:], main_sent.dtype
        fresh = send(gathered, moves)
        later_served, _ = barrier((served, gathered))
        later = gather_units(
            functools.partial(extra_kernel, late),
            [len(units) for _, units in late],
            later_served,
            mine,
            down_weights,
            up_weights,
        )
        near, homes = later[:4], later[4:]
        base_hidden, _ = barrier((hidden, gathered))
        base_terms = base_product(base_hidden, value_weight)
        fresh, near, base_terms = barrier((fresh, near, base_terms))
        relayed = vmem_call(
            relay_kernel, ((2,) + unit,) * 4, dtype, (mine,), (*fresh, *near)
        )
        near_a, main_sent, base_terms = barrier((send(relayed, moves), main_sent, base_terms))
        base = lax.psum_scatter(base_terms, "tp", scatter_dimension=1, tiled=True)
        main = lax.all_to_all(main_sent, "dp", 0, 0, tiled=True)
        tree_arrays = [
            (homes[h], near_a[2 * h], near_a[2 * h + 1], fresh[2 * h], fresh[2 * h + 1])
            for h in range(2)
        ]
        lines = vmem_call(
            line_kernel, (unit,) * 8, dtype, (mine,), tree_arrays[0] + tree_arrays[1]
        )
        got = send(lines[1:4] + lines[5:8], turned)
        partial = low_call(low_main_kernel, cap, rank, mine, hidden, (main,), {})
        got, partial = barrier((got, partial))
        extras = vmem_call(
            pick_kernel, (unit,) * 2, dtype, (mine,), (lines[0], *got[:3], lines[4], *got[3:])
        )
        partial = low_call(
            low_extra_kernel, cap, rank, mine, hidden, (*extras, partial), {4: 0}
        )
        own, other = low_rank_up(low_rank_down(partial))
        return combine(mine, counts, base, own, other, main, extras, rank)

    return lax.cond(
        mine[FLAGS, FITS] == 1, narrow, wide, hidden, value_weight, down_weights, up_weights
    )


def solution(mesh):
    return jax.shard_map(
        on_device,
        mesh=mesh,
        in_specs=(
            P("dp", "tp"),
            P("tp", None),
            P("dp", None, "tp"),
            P("dp", None, "tp"),
            P(),
            P(),
            P(),
        ),
        out_specs=P("dp", "tp"),
        check_vma=False,
    )
```

```python
import functools
import math

import jax
import jax.numpy as jnp
from jax import lax
from jax.experimental import pallas as pl
from jax.experimental.pallas import tpu as pltpu
from jax.sharding import PartitionSpec as P

ADAPTER_SCALE = 0.5
MAIN = 2
MOST = 6
EXTRA = MOST - MAIN


def low_rank_sum(partial):
    rows, rank = partial.shape
    tp_count = lax.axis_size("tp")
    pieces = lax.all_to_all(partial, "tp", split_axis=0, concat_axis=0, tiled=True)
    mine = jnp.sum(pieces.reshape(tp_count, rows // tp_count, rank), axis=0).astype(jnp.bfloat16)
    return lax.all_gather(mine, "tp", axis=0, tiled=True)


def finish(base, low, ups, counts):
    groups = counts.shape[0]
    cap = base.shape[0] // groups
    delta = jnp.einsum(
        "gcr,grv->gcv", low.reshape(groups, cap, -1), ups, preferred_element_type=jnp.float32
    )
    merged = base.reshape(groups, cap, -1) + ADAPTER_SCALE * delta
    active = jnp.arange(cap)[None, :, None] < counts[:, None, None]
    out = jnp.where(active, merged, jnp.float32(0.0)).astype(jnp.bfloat16)
    return out.reshape(base.shape)


SMEM = pl.BlockSpec(memory_space=pltpu.SMEM)
VMEM = pl.BlockSpec(memory_space=pltpu.VMEM)
HBM = pl.BlockSpec(memory_space=pltpu.HBM)
LANES = 128
ORDER, PLACE, FLAGS = 0, 1, 2
HOT, FITS, AT, CHIP, CORE = 0, 1, 2, 4, 5


def shift(value, dx, dy):
    side = math.isqrt(lax.axis_size("dp"))
    pairs = [
        (x * side + y, (x + dx) % side * side + (y + dy) % side)
        for x in range(side)
        for y in range(side)
    ]
    return lax.ppermute(value, "dp", pairs)


def index_kernel(spot_ref, ids_ref, table_ref, served_ref, mine_ref, owner_ref, rank_ref):
    total = ids_ref.shape[0]
    dp_count = served_ref.shape[0]
    groups = total // dp_count
    chunks = table_ref.shape[0]
    owned = chunks * LANES // dp_count
    me = spot_ref[0]
    f32, bf16 = jnp.float32, jnp.bfloat16
    ids = ids_ref[...]
    lane = lax.broadcasted_iota(jnp.int32, (total, LANES), 1)
    found = jnp.zeros((total, LANES), jnp.int32)
    for c in range(chunks):
        found += jnp.where(ids == lane + c * LANES, table_ref[c : c + 1, :], 0)
    stored = jnp.sum(found, axis=1, keepdims=True)
    owner = lax.div(stored, owned)
    slot = stored - owner * owned
    holds = jnp.where(owner == lane, 1.0, 0.0)
    low = lax.broadcasted_iota(jnp.int32, (groups, groups), 0)
    low = jnp.where(low > lax.broadcasted_iota(jnp.int32, (groups, groups), 1), 1.0, 0.0)
    low = low.astype(bf16)
    holds16 = holds.astype(bf16)
    before = jnp.concatenate(
        [
            jnp.dot(low, holds16[r * groups : (r + 1) * groups], preferred_element_type=f32)
            for r in range(dp_count)
        ],
        axis=0,
    )
    ranking = jnp.sum(before * holds, axis=1, keepdims=True).astype(jnp.int32)
    owner_ref[...] = jnp.broadcast_to(owner, (total, LANES))
    rank_ref[...] = jnp.broadcast_to(ranking, (total, LANES))
    block_of = lax.div(lax.broadcasted_iota(jnp.int32, (dp_count, total), 1), groups)
    block = block_of == lax.broadcasted_iota(jnp.int32, (dp_count, total), 0)
    block = jnp.where(block, 1.0, 0.0).astype(bf16)
    loads = jnp.dot(block, holds16, preferred_element_type=f32)
    kept = jnp.where((owner == me) & (ranking == lane), slot, 0).astype(f32).astype(bf16)
    served_ref[...] = jnp.dot(block, kept, preferred_element_type=f32).astype(jnp.int32)
    least = jnp.min(loads, axis=0, keepdims=True)
    row_lane = lax.broadcasted_iota(jnp.int32, (1, LANES), 1)
    hot = jnp.min(jnp.where(least >= MOST, row_lane, LANES), axis=1, keepdims=True)
    spare = jnp.where(row_lane == hot, 0.0, loads)
    most = jnp.max(jnp.max(spare, axis=0, keepdims=True), axis=1, keepdims=True)
    fits = jnp.where(most <= MAIN, 1, 0)
    at = pl.ds(pl.multiple_of(me * groups, groups), groups)
    my_owner = owner_ref[at, :]
    my_rank = rank_ref[at, :]
    late = (my_owner == hot) & (my_rank >= MAIN)
    place = jnp.where(late, dp_count * MAIN + my_rank - MAIN, my_owner * MAIN + my_rank)
    early = jnp.where(late, 0.0, 1.0).astype(bf16)
    ahead = jnp.dot(low, early, preferred_element_type=f32).astype(jnp.int32)
    turn = jnp.where(late, groups - EXTRA + my_rank - MAIN, ahead)
    group_lane = lax.broadcasted_iota(jnp.int32, (groups, LANES), 1)
    group = lax.broadcasted_iota(jnp.int32, (groups, LANES), 0)
    here = turn == group_lane
    mine_ref[...] = jnp.zeros(mine_ref.shape, jnp.int32)
    mine_ref[ORDER : ORDER + 1, :] = jnp.sum(jnp.where(here, group, 0), axis=0, keepdims=True)
    mine_ref[PLACE : PLACE + 1, :] = jnp.sum(jnp.where(here, place, 0), axis=0, keepdims=True)
    side = math.isqrt(dp_count)
    x, y = lax.div(me, side), lax.rem(me, side)
    flags = (
        (HOT, hot),
        (FITS, fits),
        (AT, lax.rem(x - lax.div(hot, side) + side, side)),
        (AT + 1, lax.rem(y - lax.rem(hot, side) + side, side)),
        (CHIP, lax.div(spot_ref[1], 2)),
        (CORE, lax.rem(spot_ref[1], 2)),
    )
    row = jnp.zeros((1, LANES), jnp.int32)
    for at, value in flags:
        row = jnp.where(row_lane == at, value, row)
    mine_ref[FLAGS : FLAGS + 1, :] = row


def index_tables(spot, ids, table, dp_count):
    total = ids.shape[0]
    return pl.pallas_call(
        index_kernel,
        out_shape=(
            jax.ShapeDtypeStruct((dp_count, LANES), jnp.int32),
            jax.ShapeDtypeStruct((8, LANES), jnp.int32),
        ),
        in_specs=[SMEM, VMEM, VMEM],
        out_specs=(VMEM, VMEM),
        scratch_shapes=[pltpu.VMEM((total, LANES), jnp.int32)] * 2,
        compiler_params=pltpu.CompilerParams(vmem_limit_bytes=8 << 20),
    )(spot, ids.reshape(total, 1), table.reshape(-1, LANES))


def copy_units(wanted, down, up, up_in, down_sem, up_sem):
    rank = down.shape[1]
    lanes = up.shape[2]
    steps = rank // 16
    downs, ups = [], []
    for i, (dest, index, rows) in enumerate(wanted):
        for half in range(2):
            n = 2 * i + half
            ups.append(pltpu.make_async_copy(up.at[rows[half]], up_in.at[n], up_sem.at[n]))
            ups[-1].start()
            downs.append(
                pltpu.make_async_copy(
                    down.at[rows[half]], dest.at[index, pl.ds(half * rank, rank)], down_sem.at[n]
                )
            )
            downs[-1].start()
    for i, (dest, index, rows) in enumerate(wanted):
        for half in range(2):
            n = 2 * i + half
            ups[n].wait()
            for part in range(steps):
                at = (half * steps + part) * lanes
                dest[index, 2 * rank : 2 * rank + 16, at : at + lanes] = up_in[
                    n, part * 16 : part * 16 + 16, :
                ]
    for copy in downs:
        copy.wait()


def extra_rows(lines, outs, served, mine):
    side = math.isqrt(served.shape[0])
    hot = mine[FLAGS, HOT]
    hot_x, hot_y = lax.div(hot, side), lax.rem(hot, side)
    wanted = []
    for out, (x_first, units) in zip(outs, lines):
        for i, (a, b) in enumerate(units):
            dx, dy = (a, b) if x_first else (b, a)
            peer = lax.rem(hot_x + dx, side) * side + lax.rem(hot_y + dy, side)
            first = MAIN if x_first else MAIN + 2
            wanted.append((out, i, (served[peer, first], served[peer, first + 1])))
    return wanted


def extra_kernel(lines, served, mine, down, up, *refs):
    outs, scratch = refs[: len(lines)], refs[len(lines) :]

    @pl.when((mine[FLAGS, AT] == 0) & (mine[FLAGS, AT + 1] == 0))
    def _():
        copy_units(extra_rows(lines, outs, served, mine), down, up, *scratch)


def gather_kernel(lines, served, mine, down, up, main, *refs):
    extra_kernel(lines, served, mine, down, up, *refs)
    rows = [(served[p, 0], served[p, 1]) for p in range(main.shape[0])]
    wanted = [(main, p, pair) for p, pair in enumerate(rows)]
    copy_units(wanted, down, up, *refs[len(lines) :])


def gather_units(kernel, shapes, served, mine, down, up):
    _, rank, width = down.shape
    lanes = up.shape[2]
    count = 16
    return pl.pallas_call(
        kernel,
        out_shape=[jax.ShapeDtypeStruct((n, 2 * rank + 16, width), down.dtype) for n in shapes],
        in_specs=[SMEM, SMEM, HBM, HBM],
        out_specs=[VMEM] * len(shapes),
        scratch_shapes=[
            pltpu.VMEM((2 * count, rank, lanes), up.dtype),
            pltpu.SemaphoreType.DMA((2 * count,)),
            pltpu.SemaphoreType.DMA((2 * count,)),
        ],
        compiler_params=pltpu.CompilerParams(vmem_limit_bytes=14 << 20),
        cost_estimate=pl.CostEstimate(
            flops=0, bytes_accessed=count * rank * (width + lanes) * 8, transcendentals=0
        ),
    )(served, mine, down, up)


def vmem_call(kernel, shapes, dtype, scalars, arrays, limit=10):
    return pl.pallas_call(
        kernel,
        out_shape=[jax.ShapeDtypeStruct(shape, dtype) for shape in shapes],
        in_specs=[SMEM] * len(scalars) + [VMEM] * len(arrays),
        out_specs=[VMEM] * len(shapes),
        compiler_params=pltpu.CompilerParams(vmem_limit_bytes=limit << 20),
        cost_estimate=pl.CostEstimate(
            flops=0,
            bytes_accessed=sum(math.prod(shape) for shape in shapes) * 4,
            transcendentals=0,
        ),
    )(*scalars, *arrays)


def move(dst, src):
    rows = src.shape[0]

    def body(i, carry):
        at = pl.ds(pl.multiple_of(i * 16, 16), 16)
        dst[at, :] = src[at, :]
        return carry

    lax.fori_loop(0, rows // 16, body, 0, unroll=3)


def relay_kernel(mine, *refs):
    fresh, near, outs = refs[:4], refs[4:8], refs[8:]
    for i in range(4):
        at = mine[FLAGS, AT + i // 2]
        close = 1 if i % 2 == 0 else 3
        for source, when in ((near[i], at != close), (fresh[i], at == close)):

            @pl.when(when)
            def _(source=source, out=outs[i]):
                for u in range(2):
                    move(out.at[u], source.at[u])


def line_kernel(mine, *refs):
    outs = refs[10:]
    for h in range(2):
        own, plus_a, minus_a, plus_b, minus_b = refs[5 * h : 5 * h + 5]
        out = outs[4 * h : 4 * h + 4]
        at = mine[FLAGS, AT + h]
        low, high = own.at[pl.ds(0, 2)], own.at[pl.ds(2, 2)]
        plus_b, minus_b = plus_b.at[pl.ds(2, 2)], minus_b.at[pl.ds(2, 2)]
        picks = ((low, high), (plus_a, plus_b), (plus_a, minus_a), (minus_a, minus_b))
        for offset, (first, second) in enumerate(picks):

            @pl.when(at == offset)
            def _(first=first, second=second, out=out):
                for u in range(2):
                    move(out[u], first.at[u])
                    move(out[2 + u], second.at[u])


def pick_kernel(mine, *refs):
    for h in range(2):
        at = mine[FLAGS, AT + 1 - h]
        for offset, source in enumerate(refs[4 * h : 4 * h + 4]):

            @pl.when(at == offset)
            def _(source=source, out=refs[8 + h]):
                move(out, source)


def base_kernel(hidden, weight, out):
    out[...] = jnp.dot(hidden[...], weight[...], preferred_element_type=jnp.float32)


def base_product(hidden, weight, block=256):
    rows, width = hidden.shape
    columns = weight.shape[1]
    return pl.pallas_call(
        base_kernel,
        grid=(rows // block,),
        out_shape=jax.ShapeDtypeStruct((rows, columns), jnp.float32),
        in_specs=[
            pl.BlockSpec((block, width), lambda i: (i, 0)),
            pl.BlockSpec((width, columns), lambda i: (0, 0)),
        ],
        out_specs=pl.BlockSpec((block, columns), lambda i: (i, 0)),
        compiler_params=pltpu.CompilerParams(vmem_limit_bytes=14 << 20),
        cost_estimate=pl.CostEstimate(
            flops=2 * rows * width * columns,
            bytes_accessed=hidden.size * 2 + weight.size * 2 + rows * columns * 4,
            transcendentals=0,
        ),
    )(hidden, weight)


def paired(hidden, mine, groups, cap, first, second):
    spots = [pl.multiple_of(mine[ORDER, j] * cap, cap) for j in groups]
    rows = jnp.concatenate([hidden[pl.ds(spot, cap), :] for spot in spots], axis=0)
    product = lax.dot_general(
        rows,
        jnp.concatenate([first, second], axis=0),
        (((1,), (1,)), ((), ())),
        preferred_element_type=jnp.float32,
    )
    lane = lax.broadcasted_iota(jnp.int32, (cap, product.shape[1]), 1)
    return jnp.where(lane < first.shape[0], product[:cap], product[cap:])


def low_main_kernel(cap, mine, hidden, main, out):
    rank = out.shape[1] // 2
    pairs = out.shape[0] // cap - EXTRA // 2

    def weights(j):
        place = mine[PLACE, j]
        unit = lax.div(place, 2)
        return main[unit, pl.ds(pl.multiple_of((place - 2 * unit) * rank, rank), rank), :]

    def body(i, carry):
        at = pl.ds(pl.multiple_of(i * cap, cap), cap)
        spots = (i, i + pairs)
        out[at, :] = paired(hidden, mine, spots, cap, weights(i), weights(i + pairs))
        return carry

    lax.fori_loop(0, pairs, body, 0, unroll=2)


def low_extra_kernel(cap, mine, hidden, first, second, _, out):
    rank = out.shape[1] // 2
    pairs = out.shape[0] // cap
    for e in range(EXTRA // 2):
        spots = (2 * pairs - EXTRA + e, 2 * pairs - EXTRA // 2 + e)
        at = (pairs - EXTRA // 2 + e) * cap
        part = slice(e * rank, (e + 1) * rank)
        out[at : at + cap, :] = paired(
            hidden, mine, spots, cap, first[part, :], second[part, :]
        )


def low_call(kernel, cap, rank, mine, hidden, arrays, aliases):
    pairs = hidden.shape[0] // cap // 2
    return pl.pallas_call(
        functools.partial(kernel, cap),
        out_shape=jax.ShapeDtypeStruct((pairs * cap, 2 * rank), jnp.float32),
        in_specs=[SMEM] + [VMEM] * (1 + len(arrays)),
        out_specs=VMEM,
        input_output_aliases=aliases,
        compiler_params=pltpu.CompilerParams(vmem_limit_bytes=12 << 20),
        cost_estimate=pl.CostEstimate(
            flops=pairs * cap * rank * 4 * hidden.shape[1],
            bytes_accessed=sum(array.size for array in arrays) * 2,
            transcendentals=0,
        ),
    )(mine, hidden, *arrays)


def turn(step):
    tp_count = lax.axis_size("tp")
    return [(i, (i + 2 * step) % tp_count) for i in range(tp_count)]


def swap():
    return [(i, i ^ 1) for i in range(lax.axis_size("tp"))]


def low_rank_down(partial):
    chips = lax.axis_size("tp") // 2
    t = lax.axis_index("tp")
    z, core = t // 2, t % 2
    half = partial.shape[0] // 2
    piece = half // chips
    cut = lambda array, start, size: lax.dynamic_slice_in_dim(array, start, size, 0)
    total = cut(partial, core * half, half) + lax.ppermute(
        cut(partial, (1 - core) * half, half), "tp", swap()
    )
    pieces = [
        lax.ppermute(cut(total, (z + d) % chips * piece, piece), "tp", turn(d))
        for d in range(1, chips)
    ]
    return (cut(total, z * piece, piece) + sum(pieces)).astype(jnp.bfloat16)


def low_rank_up(summed):
    chips = lax.axis_size("tp") // 2
    own = jnp.stack([summed] + [lax.ppermute(summed, "tp", turn(d)) for d in range(1, chips)])
    return own, lax.ppermute(own, "tp", swap())


def blend(base, out, counts, mine, j, both, ups, cap):
    rank = both.shape[1] // 2
    lane = lax.broadcasted_iota(jnp.int32, both.shape, 1)
    none = jnp.zeros_like(both)
    left = jnp.concatenate(
        [jnp.where(lane < rank, both, none), jnp.where(lane < rank, none, both)], axis=0
    )
    delta = jnp.dot(left, jnp.concatenate(ups, axis=0), preferred_element_type=jnp.float32)
    rows = lax.broadcasted_iota(jnp.int32, (cap, base.shape[1]), 0)
    for n in range(2):
        g = mine[ORDER, j[n]]
        here = pl.ds(pl.multiple_of(g * cap, cap), cap)
        merged = base[here, :] + ADAPTER_SCALE * delta[n * cap : (n + 1) * cap]
        out[here, :] = jnp.where(rows < counts[g], merged, 0.0).astype(out.dtype)


def out_kernel(mine, counts, base, own, other, main, *refs):
    extras, out, low = refs[:2], refs[2], refs[3]
    groups = counts.shape[0]
    cap = base.shape[0] // groups
    chips, piece, rank = own.shape[0], own.shape[1], own.shape[2] // 2
    lanes = base.shape[1]
    z, core = mine[FLAGS, CHIP], mine[FLAGS, CORE]
    steps = rank // 16
    pairs = (groups - EXTRA) // 2
    for d in range(chips):
        quarter = lax.rem(z - d + chips, chips)
        for ref, half in ((own, core), (other, 1 - core)):
            at = pl.multiple_of((half * chips + quarter) * piece, piece)
            low[pl.ds(at, piece), :] = ref[d]

    def up(j):
        place = mine[PLACE, j]
        unit = lax.div(place, 2)
        at = (place - 2 * unit) * steps * lanes
        return [
            main[unit, :, pl.ds(pl.multiple_of(at + part * lanes, lanes), lanes)]
            for part in range(steps)
        ]

    def body(i, carry):
        both = low[pl.ds(pl.multiple_of(i * cap, cap), cap), :]
        blend(base, out, counts, mine, (i, i + pairs), both, up(i) + up(i + pairs), cap)
        return carry

    lax.fori_loop(0, pairs, body, 0, unroll=2)
    for e in range(EXTRA // 2):
        ups = [
            pack[:, (e * steps + part) * lanes : (e * steps + part + 1) * lanes]
            for pack in extras
            for part in range(steps)
        ]
        both = low[(pairs + e) * cap : (pairs + e + 1) * cap, :]
        spots = (groups - EXTRA + e, groups - EXTRA // 2 + e)
        blend(base, out, counts, mine, spots, both, ups, cap)


def whole(array):
    return pl.BlockSpec(array.shape, lambda i: (0,) * array.ndim)


def combine(mine, counts, base, own, other, main, extras, rank):
    packs = pl.BlockSpec((main.shape[0], 16, main.shape[2]), lambda i: (0, rank // 8, 0))
    pack = pl.BlockSpec((16, main.shape[2]), lambda i: (rank // 8, 0))
    return pl.pallas_call(
        out_kernel,
        grid=(1,),
        out_shape=jax.ShapeDtypeStruct(base.shape, jnp.bfloat16),
        in_specs=[SMEM, SMEM, whole(base), whole(own), whole(other), packs, pack, pack],
        out_specs=whole(base),
        scratch_shapes=[
            pltpu.VMEM((2 * own.shape[0] * own.shape[1], own.shape[2]), jnp.bfloat16)
        ],
        compiler_params=pltpu.CompilerParams(vmem_limit_bytes=8 << 20),
        cost_estimate=pl.CostEstimate(
            flops=base.size * rank * 2, bytes_accessed=base.size * 8, transcendentals=0
        ),
    )(mine, counts, base, own, other, main, *extras)


def on_device(
    hidden,
    value_weight,
    down_weights,
    up_weights,
    group_adapter_id,
    adapter_storage_row,
    group_live_count,
):
    dp_count = lax.axis_size("dp")
    me = lax.axis_index("dp")
    owned, rank, width = down_weights.shape
    groups = group_adapter_id.shape[0] // dp_count
    cap = hidden.shape[0] // groups
    spot = jnp.stack([me, lax.axis_index("tp")]).astype(jnp.int32)
    served, mine = index_tables(spot, group_adapter_id, adapter_storage_row, dp_count)
    counts = lax.dynamic_slice_in_dim(group_live_count, me * groups, groups)

    def wide(hidden, value_weight, down_weights, up_weights):
        stored = adapter_storage_row[group_adapter_id]
        owners = (stored // owned).reshape(dp_count, groups)
        slots = (stored % owned).reshape(dp_count, groups)
        same = owners[:, :, None] == owners[:, None, :]
        earlier = jnp.arange(groups)[None, None, :] < jnp.arange(groups)[None, :, None]
        ranking = jnp.sum(same & earlier, axis=2)
        hits = (owners == me)[:, :, None] & (ranking[:, :, None] == jnp.arange(MOST))
        rows = jnp.sum(jnp.where(hits, slots[:, :, None], 0), axis=1).reshape(-1)
        my_owners = lax.dynamic_index_in_dim(owners, me, 0, keepdims=False)
        my_ranking = lax.dynamic_index_in_dim(ranking, me, 0, keepdims=False)
        base_terms = jnp.dot(hidden, value_weight, preferred_element_type=jnp.float32)
        base = lax.psum_scatter(base_terms, "tp", scatter_dimension=1, tiled=True)
        downs = lax.all_to_all(down_weights[rows], "dp", 0, 0, tiled=True)
        ups = lax.all_to_all(up_weights[rows], "dp", 0, 0, tiled=True)
        picked = my_owners * MOST + my_ranking
        partial = jnp.einsum(
            "gcd,grd->gcr",
            hidden.reshape(groups, cap, width),
            downs[picked],
            preferred_element_type=jnp.float32,
        )
        low = low_rank_sum(partial.reshape(groups * cap, rank))
        return finish(base, low, ups[picked], counts)

    def narrow(hidden, value_weight, down_weights, up_weights):
        trees = (True, False)
        soon = [
            (tree, ((2, part[0]), (2, part[1]), (near, 2), (near, 3)))
            for tree in trees
            for near, part in ((1, (0, 1)), (3, (2, 3)))
        ]
        late = [(tree, ((near, 0), (near, 1))) for tree in trees for near in (1, 3)]
        late += [(tree, ((0, 0), (0, 1), (0, 2), (0, 3))) for tree in trees]
        moves = ((1, 0), (-1, 0), (0, 1), (0, -1))
        turned = ((0, 1), (0, 2), (0, -1), (1, 0), (2, 0), (-1, 0))
        send = lambda values, ways: [shift(v, *way) for v, way in zip(values, ways)]
        barrier = lax.optimization_barrier
        gathered = gather_units(
            functools.partial(extra_kernel, soon),
            [len(units) for _, units in soon],
            served,
            mine,
            down_weights,
            up_weights,
        )
        unit, dtype = gathered[0].shape[1:], gathered[0].dtype
        fresh = send(gathered, moves)
        later_served, _ = barrier((served, gathered))
        main_sent, *later = gather_units(
            functools.partial(gather_kernel, late),
            [dp_count] + [len(units) for _, units in late],
            later_served,
            mine,
            down_weights,
            up_weights,
        )
        near, homes = later[:4], later[4:]
        fresh, near, main_sent = barrier((fresh, near, main_sent))
        relayed = vmem_call(
            relay_kernel, ((2,) + unit,) * 4, dtype, (mine,), (*fresh, *near)
        )
        base_hidden, relayed = barrier((hidden, relayed))
        base_terms = base_product(base_hidden, value_weight)
        near_a, main_sent, base_terms = barrier((send(relayed, moves), main_sent, base_terms))
        base = lax.psum_scatter(base_terms, "tp", scatter_dimension=1, tiled=True)
        main = lax.all_to_all(main_sent, "dp", 0, 0, tiled=True)
        tree_arrays = [
            (homes[h], near_a[2 * h], near_a[2 * h + 1], fresh[2 * h], fresh[2 * h + 1])
            for h in range(2)
        ]
        lines = vmem_call(
            line_kernel, (unit,) * 8, dtype, (mine,), tree_arrays[0] + tree_arrays[1]
        )
        got = send(lines[1:4] + lines[5:8], turned)
        partial = low_call(low_main_kernel, cap, rank, mine, hidden, (main,), {})
        got, partial = barrier((got, partial))
        extras = vmem_call(
            pick_kernel, (unit,) * 2, dtype, (mine,), (lines[0], *got[:3], lines[4], *got[3:])
        )
        partial = low_call(
            low_extra_kernel, cap, rank, mine, hidden, (*extras, partial), {4: 0}
        )
        own, other = low_rank_up(low_rank_down(partial))
        return combine(mine, counts, base, own, other, main, extras, rank)

    return lax.cond(
        mine[FLAGS, FITS] == 1, narrow, wide, hidden, value_weight, down_weights, up_weights
    )


def solution(mesh):
    return jax.shard_map(
        on_device,
        mesh=mesh,
        in_specs=(
            P("dp", "tp"),
            P("tp", None),
            P("dp", None, "tp"),
            P("dp", None, "tp"),
            P(),
            P(),
            P(),
        ),
        out_specs=P("dp", "tp"),
        check_vma=False,
    )
```

```python
import functools
import math

import jax
import jax.numpy as jnp
from jax import lax
from jax.experimental import pallas as pl
from jax.experimental.pallas import tpu as pltpu
from jax.sharding import PartitionSpec as P

ADAPTER_SCALE = 0.5
MAIN = 2
MOST = 6
EXTRA = MOST - MAIN


def low_rank_sum(partial):
    rows, rank = partial.shape
    tp_count = lax.axis_size("tp")
    pieces = lax.all_to_all(partial, "tp", split_axis=0, concat_axis=0, tiled=True)
    mine = jnp.sum(pieces.reshape(tp_count, rows // tp_count, rank), axis=0).astype(jnp.bfloat16)
    return lax.all_gather(mine, "tp", axis=0, tiled=True)


def finish(base, low, ups, counts):
    groups = counts.shape[0]
    cap = base.shape[0] // groups
    delta = jnp.einsum(
        "gcr,grv->gcv", low.reshape(groups, cap, -1), ups, preferred_element_type=jnp.float32
    )
    merged = base.reshape(groups, cap, -1) + ADAPTER_SCALE * delta
    active = jnp.arange(cap)[None, :, None] < counts[:, None, None]
    out = jnp.where(active, merged, jnp.float32(0.0)).astype(jnp.bfloat16)
    return out.reshape(base.shape)


SMEM = pl.BlockSpec(memory_space=pltpu.SMEM)
VMEM = pl.BlockSpec(memory_space=pltpu.VMEM)
HBM = pl.BlockSpec(memory_space=pltpu.HBM)
LANES = 128
ORDER, PLACE, FLAGS = 0, 1, 2
HOT, FITS, AT, CHIP, CORE, ME = 0, 1, 2, 4, 5, 6


def shift(value, dx, dy):
    side = math.isqrt(lax.axis_size("dp"))
    pairs = [
        (x * side + y, (x + dx) % side * side + (y + dy) % side)
        for x in range(side)
        for y in range(side)
    ]
    return lax.ppermute(value, "dp", pairs)


def index_kernel(spot_ref, ids_ref, table_ref, served_ref, mine_ref, owner_ref, rank_ref):
    total = ids_ref.shape[0]
    dp_count = served_ref.shape[0]
    groups = total // dp_count
    chunks = table_ref.shape[0]
    owned = chunks * LANES // dp_count
    me = spot_ref[0]
    f32, bf16 = jnp.float32, jnp.bfloat16
    ids = ids_ref[...]
    lane = lax.broadcasted_iota(jnp.int32, (total, LANES), 1)
    found = jnp.zeros((total, LANES), jnp.int32)
    for c in range(chunks):
        found += jnp.where(ids == lane + c * LANES, table_ref[c : c + 1, :], 0)
    stored = jnp.sum(found, axis=1, keepdims=True)
    owner = lax.div(stored, owned)
    slot = stored - owner * owned
    holds = jnp.where(owner == lane, 1.0, 0.0)
    low = lax.broadcasted_iota(jnp.int32, (groups, groups), 0)
    low = jnp.where(low > lax.broadcasted_iota(jnp.int32, (groups, groups), 1), 1.0, 0.0)
    low = low.astype(bf16)
    holds16 = holds.astype(bf16)
    before = jnp.concatenate(
        [
            jnp.dot(low, holds16[r * groups : (r + 1) * groups], preferred_element_type=f32)
            for r in range(dp_count)
        ],
        axis=0,
    )
    ranking = jnp.sum(before * holds, axis=1, keepdims=True).astype(jnp.int32)
    owner_ref[...] = jnp.broadcast_to(owner, (total, LANES))
    rank_ref[...] = jnp.broadcast_to(ranking, (total, LANES))
    block_of = lax.div(lax.broadcasted_iota(jnp.int32, (dp_count, total), 1), groups)
    block = block_of == lax.broadcasted_iota(jnp.int32, (dp_count, total), 0)
    block = jnp.where(block, 1.0, 0.0).astype(bf16)
    loads = jnp.dot(block, holds16, preferred_element_type=f32)
    kept = jnp.where((owner == me) & (ranking == lane), slot, 0).astype(f32).astype(bf16)
    served_ref[...] = jnp.dot(block, kept, preferred_element_type=f32).astype(jnp.int32)
    least = jnp.min(loads, axis=0, keepdims=True)
    row_lane = lax.broadcasted_iota(jnp.int32, (1, LANES), 1)
    hot = jnp.min(jnp.where(least >= MOST, row_lane, LANES), axis=1, keepdims=True)
    spare = jnp.where(row_lane == hot, 0.0, loads)
    most = jnp.max(jnp.max(spare, axis=0, keepdims=True), axis=1, keepdims=True)
    fits = jnp.where(most <= MAIN, 1, 0)
    at = pl.ds(pl.multiple_of(me * groups, groups), groups)
    my_owner = owner_ref[at, :]
    my_rank = rank_ref[at, :]
    late = (my_owner == hot) & (my_rank >= MAIN)
    place = jnp.where(late, dp_count * MAIN + my_rank - MAIN, my_owner * MAIN + my_rank)
    early = jnp.where(late, 0.0, 1.0).astype(bf16)
    ahead = jnp.dot(low, early, preferred_element_type=f32).astype(jnp.int32)
    turn = jnp.where(late, groups - EXTRA + my_rank - MAIN, ahead)
    group_lane = lax.broadcasted_iota(jnp.int32, (groups, LANES), 1)
    group = lax.broadcasted_iota(jnp.int32, (groups, LANES), 0)
    here = turn == group_lane
    mine_ref[...] = jnp.zeros(mine_ref.shape, jnp.int32)
    mine_ref[ORDER : ORDER + 1, :] = jnp.sum(jnp.where(here, group, 0), axis=0, keepdims=True)
    mine_ref[PLACE : PLACE + 1, :] = jnp.sum(jnp.where(here, place, 0), axis=0, keepdims=True)
    side = math.isqrt(dp_count)
    x, y = lax.div(me, side), lax.rem(me, side)
    flags = (
        (HOT, hot),
        (FITS, fits),
        (AT, lax.rem(x - lax.div(hot, side) + side, side)),
        (AT + 1, lax.rem(y - lax.rem(hot, side) + side, side)),
        (CHIP, lax.div(spot_ref[1], 2)),
        (CORE, lax.rem(spot_ref[1], 2)),
        (ME, me),
    )
    row = jnp.zeros((1, LANES), jnp.int32)
    for at, value in flags:
        row = jnp.where(row_lane == at, value, row)
    mine_ref[FLAGS : FLAGS + 1, :] = row


def index_tables(spot, ids, table, dp_count):
    total = ids.shape[0]
    return pl.pallas_call(
        index_kernel,
        out_shape=(
            jax.ShapeDtypeStruct((dp_count, LANES), jnp.int32),
            jax.ShapeDtypeStruct((8, LANES), jnp.int32),
        ),
        in_specs=[SMEM, VMEM, VMEM],
        out_specs=(VMEM, VMEM),
        scratch_shapes=[pltpu.VMEM((total, LANES), jnp.int32)] * 2,
        compiler_params=pltpu.CompilerParams(vmem_limit_bytes=8 << 20),
    )(spot, ids.reshape(total, 1), table.reshape(-1, LANES))


def copy_units(wanted, down, up, up_in, down_sem, up_sem):
    rank = down.shape[1]
    lanes = up.shape[2]
    steps = rank // 16
    downs, ups = [], []
    for i, (dest, index, rows) in enumerate(wanted):
        for half in range(2):
            n = 2 * i + half
            ups.append(pltpu.make_async_copy(up.at[rows[half]], up_in.at[n], up_sem.at[n]))
            ups[-1].start()
            downs.append(
                pltpu.make_async_copy(
                    down.at[rows[half]], dest.at[index, pl.ds(half * rank, rank)], down_sem.at[n]
                )
            )
            downs[-1].start()
    for i, (dest, index, rows) in enumerate(wanted):
        for half in range(2):
            n = 2 * i + half
            ups[n].wait()
            for part in range(steps):
                at = (half * steps + part) * lanes
                dest[index, 2 * rank : 2 * rank + 16, at : at + lanes] = up_in[
                    n, part * 16 : part * 16 + 16, :
                ]
    for copy in downs:
        copy.wait()


def extra_rows(lines, outs, served, mine):
    side = math.isqrt(served.shape[0])
    hot = mine[FLAGS, HOT]
    hot_x, hot_y = lax.div(hot, side), lax.rem(hot, side)
    wanted = []
    for out, (x_first, units) in zip(outs, lines):
        for i, (a, b) in enumerate(units):
            dx, dy = (a, b) if x_first else (b, a)
            peer = lax.rem(hot_x + dx, side) * side + lax.rem(hot_y + dy, side)
            first = MAIN if x_first else MAIN + 2
            wanted.append((out, i, (served[peer, first], served[peer, first + 1])))
    return wanted


def extra_kernel(lines, served, mine, down, up, *refs):
    outs, scratch = refs[: len(lines)], refs[len(lines) :]

    @pl.when((mine[FLAGS, AT] == 0) & (mine[FLAGS, AT + 1] == 0))
    def _():
        copy_units(extra_rows(lines, outs, served, mine), down, up, *scratch)


def gather_kernel(lines, served, mine, down, up, main, *refs):
    extra_kernel(lines, served, mine, down, up, *refs)
    rows = [(served[p, 0], served[p, 1]) for p in range(main.shape[0])]
    wanted = [(main, p, pair) for p, pair in enumerate(rows)]
    copy_units(wanted, down, up, *refs[len(lines) :])


def gather_units(kernel, shapes, served, mine, down, up):
    _, rank, width = down.shape
    lanes = up.shape[2]
    count = 16
    return pl.pallas_call(
        kernel,
        out_shape=[jax.ShapeDtypeStruct((n, 2 * rank + 16, width), down.dtype) for n in shapes],
        in_specs=[SMEM, SMEM, HBM, HBM],
        out_specs=[VMEM] * len(shapes),
        scratch_shapes=[
            pltpu.VMEM((2 * count, rank, lanes), up.dtype),
            pltpu.SemaphoreType.DMA((2 * count,)),
            pltpu.SemaphoreType.DMA((2 * count,)),
        ],
        compiler_params=pltpu.CompilerParams(vmem_limit_bytes=14 << 20),
        cost_estimate=pl.CostEstimate(
            flops=0, bytes_accessed=count * rank * (width + lanes) * 8, transcendentals=0
        ),
    )(served, mine, down, up)


def vmem_call(kernel, shapes, dtype, scalars, arrays, limit=10):
    return pl.pallas_call(
        kernel,
        out_shape=[jax.ShapeDtypeStruct(shape, dtype) for shape in shapes],
        in_specs=[SMEM] * len(scalars) + [VMEM] * len(arrays),
        out_specs=[VMEM] * len(shapes),
        compiler_params=pltpu.CompilerParams(vmem_limit_bytes=limit << 20),
        cost_estimate=pl.CostEstimate(
            flops=0,
            bytes_accessed=sum(math.prod(shape) for shape in shapes) * 4,
            transcendentals=0,
        ),
    )(*scalars, *arrays)


def move(dst, src):
    rows = src.shape[0]

    def body(i, carry):
        at = pl.ds(pl.multiple_of(i * 16, 16), 16)
        dst[at, :] = src[at, :]
        return carry

    lax.fori_loop(0, rows // 16, body, 0, unroll=3)


def relay_kernel(mine, *refs):
    fresh, near, outs = refs[:4], refs[4:8], refs[8:]
    for i in range(4):
        at = mine[FLAGS, AT + i // 2]
        close = 1 if i % 2 == 0 else 3
        for source, when in ((near[i], at != close), (fresh[i], at == close)):

            @pl.when(when)
            def _(source=source, out=outs[i]):
                for u in range(2):
                    move(out.at[u], source.at[u])


def line_kernel(mine, *refs):
    outs = refs[10:]
    for h in range(2):
        own, plus_a, minus_a, plus_b, minus_b = refs[5 * h : 5 * h + 5]
        out = outs[4 * h : 4 * h + 4]
        at = mine[FLAGS, AT + h]
        low, high = own.at[pl.ds(0, 2)], own.at[pl.ds(2, 2)]
        plus_b, minus_b = plus_b.at[pl.ds(2, 2)], minus_b.at[pl.ds(2, 2)]
        picks = ((low, high), (plus_a, plus_b), (plus_a, minus_a), (minus_a, minus_b))
        for offset, (first, second) in enumerate(picks):

            @pl.when(at == offset)
            def _(first=first, second=second, out=out):
                for u in range(2):
                    move(out[u], first.at[u])
                    move(out[2 + u], second.at[u])


def pick_kernel(mine, *refs):
    for h in range(2):
        at = mine[FLAGS, AT + 1 - h]
        for offset, source in enumerate(refs[4 * h : 4 * h + 4]):

            @pl.when(at == offset)
            def _(source=source, out=refs[8 + h]):
                move(out, source)


def base_kernel(hidden, weight, out):
    out[...] = jnp.dot(hidden[...], weight[...], preferred_element_type=jnp.float32)


def base_product(hidden, weight, block=256):
    rows, width = hidden.shape
    columns = weight.shape[1]
    return pl.pallas_call(
        base_kernel,
        grid=(rows // block,),
        out_shape=jax.ShapeDtypeStruct((rows, columns), jnp.float32),
        in_specs=[
            pl.BlockSpec((block, width), lambda i: (i, 0)),
            pl.BlockSpec((width, columns), lambda i: (0, 0)),
        ],
        out_specs=pl.BlockSpec((block, columns), lambda i: (i, 0)),
        compiler_params=pltpu.CompilerParams(vmem_limit_bytes=14 << 20),
        cost_estimate=pl.CostEstimate(
            flops=2 * rows * width * columns,
            bytes_accessed=hidden.size * 2 + weight.size * 2 + rows * columns * 4,
            transcendentals=0,
        ),
    )(hidden, weight)


def paired(hidden, mine, groups, cap, first, second):
    spots = [pl.multiple_of(mine[ORDER, j] * cap, cap) for j in groups]
    rows = jnp.concatenate([hidden[pl.ds(spot, cap), :] for spot in spots], axis=0)
    product = lax.dot_general(
        rows,
        jnp.concatenate([first, second], axis=0),
        (((1,), (1,)), ((), ())),
        preferred_element_type=jnp.float32,
    )
    lane = lax.broadcasted_iota(jnp.int32, (cap, product.shape[1]), 1)
    return jnp.where(lane < first.shape[0], product[:cap], product[cap:])


def low_main_kernel(cap, mine, hidden, main, out):
    rank = out.shape[1] // 2
    pairs = out.shape[0] // cap - EXTRA // 2

    def weights(j):
        place = mine[PLACE, j]
        unit = lax.div(place, 2)
        return main[unit, pl.ds(pl.multiple_of((place - 2 * unit) * rank, rank), rank), :]

    def rows(j):
        return hidden[pl.ds(pl.multiple_of(mine[ORDER, j] * cap, cap), cap), :]

    def body(i, carry):
        spots = (2 * i, 2 * i + pairs, 2 * i + 1, 2 * i + 1 + pairs)
        product = lax.dot_general(
            jnp.concatenate([rows(j) for j in spots], axis=0),
            jnp.concatenate([weights(j) for j in spots], axis=0),
            (((1,), (1,)), ((), ())),
            preferred_element_type=jnp.float32,
        )
        lane = lax.broadcasted_iota(jnp.int32, (cap, 2 * rank), 1)
        for n in range(2):
            part = product[2 * n * cap : 2 * (n + 1) * cap, 2 * n * rank : 2 * (n + 1) * rank]
            at = pl.ds(pl.multiple_of((2 * i + n) * cap, cap), cap)
            out[at, :] = jnp.where(lane < rank, part[:cap], part[cap:])
        return carry

    lax.fori_loop(0, pairs // 2, body, 0)


def low_extra_kernel(cap, mine, hidden, first, second, _, out):
    rank = out.shape[1] // 2
    pairs = out.shape[0] // cap
    for e in range(EXTRA // 2):
        spots = (2 * pairs - EXTRA + e, 2 * pairs - EXTRA // 2 + e)
        at = (pairs - EXTRA // 2 + e) * cap
        part = slice(e * rank, (e + 1) * rank)
        out[at : at + cap, :] = paired(
            hidden, mine, spots, cap, first[part, :], second[part, :]
        )


def low_call(kernel, cap, rank, mine, hidden, arrays, aliases):
    pairs = hidden.shape[0] // cap // 2
    return pl.pallas_call(
        functools.partial(kernel, cap),
        out_shape=jax.ShapeDtypeStruct((pairs * cap, 2 * rank), jnp.float32),
        in_specs=[SMEM] + [VMEM] * (1 + len(arrays)),
        out_specs=VMEM,
        input_output_aliases=aliases,
        compiler_params=pltpu.CompilerParams(vmem_limit_bytes=12 << 20),
        cost_estimate=pl.CostEstimate(
            flops=pairs * cap * rank * 4 * hidden.shape[1],
            bytes_accessed=sum(array.size for array in arrays) * 2,
            transcendentals=0,
        ),
    )(mine, hidden, *arrays)


def turn(step):
    tp_count = lax.axis_size("tp")
    return [(i, (i + 2 * step) % tp_count) for i in range(tp_count)]


def swap():
    return [(i, i ^ 1) for i in range(lax.axis_size("tp"))]


def low_rank_down(partial):
    chips = lax.axis_size("tp") // 2
    t = lax.axis_index("tp")
    z, core = t // 2, t % 2
    half = partial.shape[0] // 2
    piece = half // chips
    cut = lambda array, start, size: lax.dynamic_slice_in_dim(array, start, size, 0)
    total = cut(partial, core * half, half) + lax.ppermute(
        cut(partial, (1 - core) * half, half), "tp", swap()
    )
    pieces = [
        lax.ppermute(cut(total, (z + d) % chips * piece, piece), "tp", turn(d))
        for d in range(1, chips)
    ]
    return (cut(total, z * piece, piece) + sum(pieces)).astype(jnp.bfloat16)


def low_rank_up(summed):
    chips = lax.axis_size("tp") // 2
    own = jnp.stack([summed] + [lax.ppermute(summed, "tp", turn(d)) for d in range(1, chips)])
    return own, lax.ppermute(own, "tp", swap())


def blend(base, out, counts, mine, j, both, ups, cap):
    rank = both.shape[1] // 2
    groups = base.shape[0] // cap
    lane = lax.broadcasted_iota(jnp.int32, both.shape, 1)
    none = jnp.zeros_like(both)
    left = jnp.concatenate(
        [jnp.where(lane < rank, both, none), jnp.where(lane < rank, none, both)], axis=0
    )
    delta = jnp.dot(left, jnp.concatenate(ups, axis=0), preferred_element_type=jnp.float32)
    rows = lax.broadcasted_iota(jnp.int32, (cap, base.shape[1]), 0)
    for n in range(2):
        g = mine[ORDER, j[n]]
        here = pl.ds(pl.multiple_of(g * cap, cap), cap)
        merged = base[here, :] + ADAPTER_SCALE * delta[n * cap : (n + 1) * cap]
        out[here, :] = jnp.where(rows < counts[mine[FLAGS, ME] * groups + g], merged, 0.0).astype(out.dtype)


def out_kernel(cap, mine, counts, base, own, other, main, *refs):
    extras, out, low = refs[:2], refs[2], refs[3]
    groups = base.shape[0] // cap
    chips, piece, rank = own.shape[0], own.shape[1], own.shape[2] // 2
    lanes = base.shape[1]
    z, core = mine[FLAGS, CHIP], mine[FLAGS, CORE]
    steps = rank // 16
    pairs = (groups - EXTRA) // 2
    for d in range(chips):
        quarter = lax.rem(z - d + chips, chips)
        for ref, half in ((own, core), (other, 1 - core)):
            at = pl.multiple_of((half * chips + quarter) * piece, piece)
            low[pl.ds(at, piece), :] = ref[d]

    def up(j):
        place = mine[PLACE, j]
        unit = lax.div(place, 2)
        at = (place - 2 * unit) * steps * lanes
        return [
            main[unit, :, pl.ds(pl.multiple_of(at + part * lanes, lanes), lanes)]
            for part in range(steps)
        ]

    def body(i, carry):
        both = low[pl.ds(pl.multiple_of(i * cap, cap), cap), :]
        blend(base, out, counts, mine, (i, i + pairs), both, up(i) + up(i + pairs), cap)
        return carry

    lax.fori_loop(0, pairs, body, 0, unroll=2)
    for e in range(EXTRA // 2):
        ups = [
            pack[:, (e * steps + part) * lanes : (e * steps + part + 1) * lanes]
            for pack in extras
            for part in range(steps)
        ]
        both = low[(pairs + e) * cap : (pairs + e + 1) * cap, :]
        spots = (groups - EXTRA + e, groups - EXTRA // 2 + e)
        blend(base, out, counts, mine, spots, both, ups, cap)


def whole(array):
    return pl.BlockSpec(array.shape, lambda i: (0,) * array.ndim)


def combine(mine, counts, base, own, other, main, extras, cap, rank):
    packs = pl.BlockSpec((main.shape[0], 16, main.shape[2]), lambda i: (0, rank // 8, 0))
    pack = pl.BlockSpec((16, main.shape[2]), lambda i: (rank // 8, 0))
    return pl.pallas_call(
        functools.partial(out_kernel, cap),
        grid=(1,),
        out_shape=jax.ShapeDtypeStruct(base.shape, jnp.bfloat16),
        in_specs=[SMEM, SMEM, whole(base), whole(own), whole(other), packs, pack, pack],
        out_specs=whole(base),
        scratch_shapes=[
            pltpu.VMEM((2 * own.shape[0] * own.shape[1], own.shape[2]), jnp.bfloat16)
        ],
        compiler_params=pltpu.CompilerParams(vmem_limit_bytes=8 << 20),
        cost_estimate=pl.CostEstimate(
            flops=base.size * rank * 2, bytes_accessed=base.size * 8, transcendentals=0
        ),
    )(mine, counts, base, own, other, main, *extras)


def on_device(
    hidden,
    value_weight,
    down_weights,
    up_weights,
    group_adapter_id,
    adapter_storage_row,
    group_live_count,
):
    dp_count = lax.axis_size("dp")
    me = lax.axis_index("dp")
    owned, rank, width = down_weights.shape
    groups = group_adapter_id.shape[0] // dp_count
    cap = hidden.shape[0] // groups
    spot = jnp.stack([me, lax.axis_index("tp")]).astype(jnp.int32)
    served, mine = index_tables(spot, group_adapter_id, adapter_storage_row, dp_count)

    def wide(hidden, value_weight, down_weights, up_weights):
        stored = adapter_storage_row[group_adapter_id]
        owners = (stored // owned).reshape(dp_count, groups)
        slots = (stored % owned).reshape(dp_count, groups)
        same = owners[:, :, None] == owners[:, None, :]
        earlier = jnp.arange(groups)[None, None, :] < jnp.arange(groups)[None, :, None]
        ranking = jnp.sum(same & earlier, axis=2)
        hits = (owners == me)[:, :, None] & (ranking[:, :, None] == jnp.arange(MOST))
        rows = jnp.sum(jnp.where(hits, slots[:, :, None], 0), axis=1).reshape(-1)
        my_owners = lax.dynamic_index_in_dim(owners, me, 0, keepdims=False)
        my_ranking = lax.dynamic_index_in_dim(ranking, me, 0, keepdims=False)
        base_terms = jnp.dot(hidden, value_weight, preferred_element_type=jnp.float32)
        base = lax.psum_scatter(base_terms, "tp", scatter_dimension=1, tiled=True)
        downs = lax.all_to_all(down_weights[rows], "dp", 0, 0, tiled=True)
        ups = lax.all_to_all(up_weights[rows], "dp", 0, 0, tiled=True)
        picked = my_owners * MOST + my_ranking
        partial = jnp.einsum(
            "gcd,grd->gcr",
            hidden.reshape(groups, cap, width),
            downs[picked],
            preferred_element_type=jnp.float32,
        )
        low = low_rank_sum(partial.reshape(groups * cap, rank))
        counts = lax.dynamic_slice_in_dim(group_live_count, me * groups, groups)
        return finish(base, low, ups[picked], counts)

    def narrow(hidden, value_weight, down_weights, up_weights):
        trees = (True, False)
        soon = [
            (tree, ((2, part[0]), (2, part[1]), (near, 2), (near, 3)))
            for tree in trees
            for near, part in ((1, (0, 1)), (3, (2, 3)))
        ]
        late = [(tree, ((near, 0), (near, 1))) for tree in trees for near in (1, 3)]
        late += [(tree, ((0, 0), (0, 1), (0, 2), (0, 3))) for tree in trees]
        moves = ((1, 0), (-1, 0), (0, 1), (0, -1))
        turned = ((0, 1), (0, 2), (0, -1), (1, 0), (2, 0), (-1, 0))
        send = lambda values, ways: [shift(v, *way) for v, way in zip(values, ways)]
        barrier = lax.optimization_barrier
        gathered = gather_units(
            functools.partial(extra_kernel, soon),
            [len(units) for _, units in soon],
            served,
            mine,
            down_weights,
            up_weights,
        )
        unit, dtype = gathered[0].shape[1:], gathered[0].dtype
        fresh = send(gathered, moves)
        later_served, _ = barrier((served, gathered))
        main_sent, *later = gather_units(
            functools.partial(gather_kernel, late),
            [dp_count] + [len(units) for _, units in late],
            later_served,
            mine,
            down_weights,
            up_weights,
        )
        near, homes = later[:4], later[4:]
        fresh, near, main_sent = barrier((fresh, near, main_sent))
        relayed = vmem_call(
            relay_kernel, ((2,) + unit,) * 4, dtype, (mine,), (*fresh, *near)
        )
        base_hidden, relayed = barrier((hidden, relayed))
        base_terms = base_product(base_hidden, value_weight)
        near_a, main_sent, base_terms = barrier((send(relayed, moves), main_sent, base_terms))
        base = lax.psum_scatter(base_terms, "tp", scatter_dimension=1, tiled=True)
        main = lax.all_to_all(main_sent, "dp", 0, 0, tiled=True)
        tree_arrays = [
            (homes[h], near_a[2 * h], near_a[2 * h + 1], fresh[2 * h], fresh[2 * h + 1])
            for h in range(2)
        ]
        lines = vmem_call(
            line_kernel, (unit,) * 8, dtype, (mine,), tree_arrays[0] + tree_arrays[1]
        )
        got = send(lines[1:4] + lines[5:8], turned)
        partial = low_call(low_main_kernel, cap, rank, mine, hidden, (main,), {})
        got, partial = barrier((got, partial))
        extras = vmem_call(
            pick_kernel, (unit,) * 2, dtype, (mine,), (lines[0], *got[:3], lines[4], *got[3:])
        )
        partial = low_call(
            low_extra_kernel, cap, rank, mine, hidden, (*extras, partial), {4: 0}
        )
        own, other = low_rank_up(low_rank_down(partial))
        return combine(mine, group_live_count, base, own, other, main, extras, cap, rank)

    return lax.cond(
        mine[FLAGS, FITS] == 1, narrow, wide, hidden, value_weight, down_weights, up_weights
    )


def solution(mesh):
    return jax.shard_map(
        on_device,
        mesh=mesh,
        in_specs=(
            P("dp", "tp"),
            P("tp", None),
            P("dp", None, "tp"),
            P("dp", None, "tp"),
            P(),
            P(),
            P(),
        ),
        out_specs=P("dp", "tp"),
        check_vma=False,
    )
```

```python
import functools
import math

import jax
import jax.numpy as jnp
from jax import lax
from jax.experimental import pallas as pl
from jax.experimental.pallas import tpu as pltpu
from jax.sharding import PartitionSpec as P

ADAPTER_SCALE = 0.5
MAIN = 2
MOST = 6
EXTRA = MOST - MAIN


def low_rank_sum(partial):
    rows, rank = partial.shape
    tp_count = lax.axis_size("tp")
    pieces = lax.all_to_all(partial, "tp", split_axis=0, concat_axis=0, tiled=True)
    mine = jnp.sum(pieces.reshape(tp_count, rows // tp_count, rank), axis=0).astype(jnp.bfloat16)
    return lax.all_gather(mine, "tp", axis=0, tiled=True)


def finish(base, low, ups, counts):
    groups = counts.shape[0]
    cap = base.shape[0] // groups
    delta = jnp.einsum(
        "gcr,grv->gcv", low.reshape(groups, cap, -1), ups, preferred_element_type=jnp.float32
    )
    merged = base.reshape(groups, cap, -1) + ADAPTER_SCALE * delta
    active = jnp.arange(cap)[None, :, None] < counts[:, None, None]
    out = jnp.where(active, merged, jnp.float32(0.0)).astype(jnp.bfloat16)
    return out.reshape(base.shape)


SMEM = pl.BlockSpec(memory_space=pltpu.SMEM)
VMEM = pl.BlockSpec(memory_space=pltpu.VMEM)
HBM = pl.BlockSpec(memory_space=pltpu.HBM)
LANES = 128
ORDER, PLACE, FLAGS = 0, 1, 2
HOT, FITS, AT, CHIP, CORE, ME = 0, 1, 2, 4, 5, 6


def shift(value, dx, dy):
    side = math.isqrt(lax.axis_size("dp"))
    pairs = [
        (x * side + y, (x + dx) % side * side + (y + dy) % side)
        for x in range(side)
        for y in range(side)
    ]
    return lax.ppermute(value, "dp", pairs)


def index_kernel(spot_ref, ids_ref, table_ref, served_ref, mine_ref, owner_ref, rank_ref):
    total = ids_ref.shape[0]
    dp_count = served_ref.shape[0]
    groups = total // dp_count
    chunks = table_ref.shape[0]
    owned = chunks * LANES // dp_count
    me = spot_ref[0]
    f32, bf16 = jnp.float32, jnp.bfloat16
    ids = ids_ref[...]
    lane = lax.broadcasted_iota(jnp.int32, (total, LANES), 1)
    found = jnp.zeros((total, LANES), jnp.int32)
    for c in range(chunks):
        found += jnp.where(ids == lane + c * LANES, table_ref[c : c + 1, :], 0)
    stored = jnp.sum(found, axis=1, keepdims=True)
    owner = lax.div(stored, owned)
    slot = stored - owner * owned
    holds = jnp.where(owner == lane, 1.0, 0.0)
    low = lax.broadcasted_iota(jnp.int32, (groups, groups), 0)
    low = jnp.where(low > lax.broadcasted_iota(jnp.int32, (groups, groups), 1), 1.0, 0.0)
    low = low.astype(bf16)
    holds16 = holds.astype(bf16)
    before = jnp.concatenate(
        [
            jnp.dot(low, holds16[r * groups : (r + 1) * groups], preferred_element_type=f32)
            for r in range(dp_count)
        ],
        axis=0,
    )
    ranking = jnp.sum(before * holds, axis=1, keepdims=True).astype(jnp.int32)
    owner_ref[...] = jnp.broadcast_to(owner, (total, LANES))
    rank_ref[...] = jnp.broadcast_to(ranking, (total, LANES))
    block_of = lax.div(lax.broadcasted_iota(jnp.int32, (dp_count, total), 1), groups)
    block = block_of == lax.broadcasted_iota(jnp.int32, (dp_count, total), 0)
    block = jnp.where(block, 1.0, 0.0).astype(bf16)
    loads = jnp.dot(block, holds16, preferred_element_type=f32)
    kept = jnp.where((owner == me) & (ranking == lane), slot, 0).astype(f32).astype(bf16)
    served_ref[...] = jnp.dot(block, kept, preferred_element_type=f32).astype(jnp.int32)
    least = jnp.min(loads, axis=0, keepdims=True)
    row_lane = lax.broadcasted_iota(jnp.int32, (1, LANES), 1)
    hot = jnp.min(jnp.where(least >= MOST, row_lane, LANES), axis=1, keepdims=True)
    spare = jnp.where(row_lane == hot, 0.0, loads)
    most = jnp.max(jnp.max(spare, axis=0, keepdims=True), axis=1, keepdims=True)
    fits = jnp.where(most <= MAIN, 1, 0)
    at = pl.ds(pl.multiple_of(me * groups, groups), groups)
    my_owner = owner_ref[at, :]
    my_rank = rank_ref[at, :]
    late = (my_owner == hot) & (my_rank >= MAIN)
    place = jnp.where(late, dp_count * MAIN + my_rank - MAIN, my_owner * MAIN + my_rank)
    early = jnp.where(late, 0.0, 1.0).astype(bf16)
    ahead = jnp.dot(low, early, preferred_element_type=f32).astype(jnp.int32)
    turn = jnp.where(late, groups - EXTRA + my_rank - MAIN, ahead)
    group_lane = lax.broadcasted_iota(jnp.int32, (groups, LANES), 1)
    group = lax.broadcasted_iota(jnp.int32, (groups, LANES), 0)
    here = turn == group_lane
    mine_ref[...] = jnp.zeros(mine_ref.shape, jnp.int32)
    mine_ref[ORDER : ORDER + 1, :] = jnp.sum(jnp.where(here, group, 0), axis=0, keepdims=True)
    mine_ref[PLACE : PLACE + 1, :] = jnp.sum(jnp.where(here, place, 0), axis=0, keepdims=True)
    side = math.isqrt(dp_count)
    x, y = lax.div(me, side), lax.rem(me, side)
    flags = (
        (HOT, hot),
        (FITS, fits),
        (AT, lax.rem(x - lax.div(hot, side) + side, side)),
        (AT + 1, lax.rem(y - lax.rem(hot, side) + side, side)),
        (CHIP, lax.div(spot_ref[1], 2)),
        (CORE, lax.rem(spot_ref[1], 2)),
        (ME, me),
    )
    row = jnp.zeros((1, LANES), jnp.int32)
    for at, value in flags:
        row = jnp.where(row_lane == at, value, row)
    mine_ref[FLAGS : FLAGS + 1, :] = row


def index_tables(spot, ids, table, dp_count):
    total = ids.shape[0]
    return pl.pallas_call(
        index_kernel,
        out_shape=(
            jax.ShapeDtypeStruct((dp_count, LANES), jnp.int32),
            jax.ShapeDtypeStruct((8, LANES), jnp.int32),
        ),
        in_specs=[SMEM, VMEM, VMEM],
        out_specs=(VMEM, VMEM),
        scratch_shapes=[pltpu.VMEM((total, LANES), jnp.int32)] * 2,
        compiler_params=pltpu.CompilerParams(vmem_limit_bytes=8 << 20),
    )(spot, ids.reshape(total, 1), table.reshape(-1, LANES))


def copy_units(wanted, down, up, up_in, down_sem, up_sem):
    rank = down.shape[1]
    lanes = up.shape[2]
    steps = rank // 16
    downs, ups = [], []
    for i, (dest, index, rows) in enumerate(wanted):
        for half in range(2):
            n = 2 * i + half
            ups.append(pltpu.make_async_copy(up.at[rows[half]], up_in.at[n], up_sem.at[n]))
            ups[-1].start()
            downs.append(
                pltpu.make_async_copy(
                    down.at[rows[half]], dest.at[index, pl.ds(half * rank, rank)], down_sem.at[n]
                )
            )
            downs[-1].start()
    for i, (dest, index, rows) in enumerate(wanted):
        for half in range(2):
            n = 2 * i + half
            ups[n].wait()
            for part in range(steps):
                at = (half * steps + part) * lanes
                dest[index, 2 * rank : 2 * rank + 16, at : at + lanes] = up_in[
                    n, part * 16 : part * 16 + 16, :
                ]
    for copy in downs:
        copy.wait()


def extra_rows(lines, outs, served, mine):
    side = math.isqrt(served.shape[0])
    hot = mine[FLAGS, HOT]
    hot_x, hot_y = lax.div(hot, side), lax.rem(hot, side)
    wanted = []
    for out, (x_first, units) in zip(outs, lines):
        for i, (a, b) in enumerate(units):
            dx, dy = (a, b) if x_first else (b, a)
            peer = lax.rem(hot_x + dx, side) * side + lax.rem(hot_y + dy, side)
            first = MAIN if x_first else MAIN + 2
            wanted.append((out, i, (served[peer, first], served[peer, first + 1])))
    return wanted


def extra_kernel(lines, served, mine, down, up, *refs):
    outs, scratch = refs[: len(lines)], refs[len(lines) :]

    @pl.when((mine[FLAGS, AT] == 0) & (mine[FLAGS, AT + 1] == 0))
    def _():
        copy_units(extra_rows(lines, outs, served, mine), down, up, *scratch)


def gather_kernel(lines, served, mine, down, up, main, *refs):
    extra_kernel(lines, served, mine, down, up, *refs)
    rows = [(served[p, 0], served[p, 1]) for p in range(main.shape[0])]
    wanted = [(main, p, pair) for p, pair in enumerate(rows)]
    copy_units(wanted, down, up, *refs[len(lines) :])


def gather_units(kernel, shapes, served, mine, down, up):
    _, rank, width = down.shape
    lanes = up.shape[2]
    count = 16
    return pl.pallas_call(
        kernel,
        out_shape=[jax.ShapeDtypeStruct((n, 2 * rank + 16, width), down.dtype) for n in shapes],
        in_specs=[SMEM, SMEM, HBM, HBM],
        out_specs=[VMEM] * len(shapes),
        scratch_shapes=[
            pltpu.VMEM((2 * count, rank, lanes), up.dtype),
            pltpu.SemaphoreType.DMA((2 * count,)),
            pltpu.SemaphoreType.DMA((2 * count,)),
        ],
        compiler_params=pltpu.CompilerParams(vmem_limit_bytes=14 << 20),
        cost_estimate=pl.CostEstimate(
            flops=0, bytes_accessed=count * rank * (width + lanes) * 8, transcendentals=0
        ),
    )(served, mine, down, up)


def vmem_call(kernel, shapes, dtype, scalars, arrays, limit=10):
    return pl.pallas_call(
        kernel,
        out_shape=[jax.ShapeDtypeStruct(shape, dtype) for shape in shapes],
        in_specs=[SMEM] * len(scalars) + [VMEM] * len(arrays),
        out_specs=[VMEM] * len(shapes),
        compiler_params=pltpu.CompilerParams(vmem_limit_bytes=limit << 20),
        cost_estimate=pl.CostEstimate(
            flops=0,
            bytes_accessed=sum(math.prod(shape) for shape in shapes) * 4,
            transcendentals=0,
        ),
    )(*scalars, *arrays)


def move(dst, src):
    rows = src.shape[0]

    def body(i, carry):
        at = pl.ds(pl.multiple_of(i * 16, 16), 16)
        dst[at, :] = src[at, :]
        return carry

    lax.fori_loop(0, rows // 16, body, 0, unroll=3)


def relay_kernel(mine, *refs):
    fresh, near, outs = refs[:4], refs[4:8], refs[8:]
    for i in range(4):
        at = mine[FLAGS, AT + i // 2]
        close = 1 if i % 2 == 0 else 3
        for source, when in ((near[i], at != close), (fresh[i], at == close)):

            @pl.when(when)
            def _(source=source, out=outs[i]):
                for u in range(2):
                    move(out.at[u], source.at[u])


def line_kernel(mine, *refs):
    outs = refs[10:]
    for h in range(2):
        own, plus_a, minus_a, plus_b, minus_b = refs[5 * h : 5 * h + 5]
        out = outs[4 * h : 4 * h + 4]
        at = mine[FLAGS, AT + h]
        low, high = own.at[pl.ds(0, 2)], own.at[pl.ds(2, 2)]
        plus_b, minus_b = plus_b.at[pl.ds(2, 2)], minus_b.at[pl.ds(2, 2)]
        picks = ((low, high), (plus_a, plus_b), (plus_a, minus_a), (minus_a, minus_b))
        for offset, (first, second) in enumerate(picks):

            @pl.when(at == offset)
            def _(first=first, second=second, out=out):
                for u in range(2):
                    move(out[u], first.at[u])
                    move(out[2 + u], second.at[u])


def pick_kernel(mine, *refs):
    for h in range(2):
        at = mine[FLAGS, AT + 1 - h]
        for offset, source in enumerate(refs[4 * h : 4 * h + 4]):

            @pl.when(at == offset)
            def _(source=source, out=refs[8 + h]):
                move(out, source)


def base_kernel(hidden, weight, out):
    out[...] = jnp.dot(hidden[...], weight[...], preferred_element_type=jnp.float32)


def base_product(hidden, weight, block=256):
    rows, width = hidden.shape
    columns = weight.shape[1]
    return pl.pallas_call(
        base_kernel,
        grid=(rows // block,),
        out_shape=jax.ShapeDtypeStruct((rows, columns), jnp.float32),
        in_specs=[
            pl.BlockSpec((block, width), lambda i: (i, 0)),
            pl.BlockSpec((width, columns), lambda i: (0, 0)),
        ],
        out_specs=pl.BlockSpec((block, columns), lambda i: (i, 0)),
        compiler_params=pltpu.CompilerParams(vmem_limit_bytes=14 << 20),
        cost_estimate=pl.CostEstimate(
            flops=2 * rows * width * columns,
            bytes_accessed=hidden.size * 2 + weight.size * 2 + rows * columns * 4,
            transcendentals=0,
        ),
    )(hidden, weight)


def paired(hidden, mine, groups, cap, first, second):
    spots = [pl.multiple_of(mine[ORDER, j] * cap, cap) for j in groups]
    rows = jnp.concatenate([hidden[pl.ds(spot, cap), :] for spot in spots], axis=0)
    product = lax.dot_general(
        rows,
        jnp.concatenate([first, second], axis=0),
        (((1,), (1,)), ((), ())),
        preferred_element_type=jnp.float32,
    )
    lane = lax.broadcasted_iota(jnp.int32, (cap, product.shape[1]), 1)
    return jnp.where(lane < first.shape[0], product[:cap], product[cap:])


def low_main_kernel(cap, mine, hidden, main, out):
    rank = out.shape[1] // 2
    pairs = out.shape[0] // cap - EXTRA // 2

    def weights(j):
        place = mine[PLACE, j]
        unit = lax.div(place, 2)
        return main[unit, pl.ds(pl.multiple_of((place - 2 * unit) * rank, rank), rank), :]

    def rows(j):
        return hidden[pl.ds(pl.multiple_of(mine[ORDER, j] * cap, cap), cap), :]

    def body(i, carry):
        spots = (2 * i, 2 * i + pairs, 2 * i + 1, 2 * i + 1 + pairs)
        product = lax.dot_general(
            jnp.concatenate([rows(j) for j in spots], axis=0),
            jnp.concatenate([weights(j) for j in spots], axis=0),
            (((1,), (1,)), ((), ())),
            preferred_element_type=jnp.float32,
        )
        lane = lax.broadcasted_iota(jnp.int32, (cap, 2 * rank), 1)
        for n in range(2):
            part = product[2 * n * cap : 2 * (n + 1) * cap, 2 * n * rank : 2 * (n + 1) * rank]
            at = pl.ds(pl.multiple_of((2 * i + n) * cap, cap), cap)
            out[at, :] = jnp.where(lane < rank, part[:cap], part[cap:])
        return carry

    lax.fori_loop(0, pairs // 2, body, 0, unroll=True)


def low_extra_kernel(cap, mine, hidden, first, second, _, out):
    rank = out.shape[1] // 2
    pairs = out.shape[0] // cap
    for e in range(EXTRA // 2):
        spots = (2 * pairs - EXTRA + e, 2 * pairs - EXTRA // 2 + e)
        at = (pairs - EXTRA // 2 + e) * cap
        part = slice(e * rank, (e + 1) * rank)
        out[at : at + cap, :] = paired(
            hidden, mine, spots, cap, first[part, :], second[part, :]
        )


def low_call(kernel, cap, rank, mine, hidden, arrays, aliases):
    pairs = hidden.shape[0] // cap // 2
    return pl.pallas_call(
        functools.partial(kernel, cap),
        out_shape=jax.ShapeDtypeStruct((pairs * cap, 2 * rank), jnp.float32),
        in_specs=[SMEM] + [VMEM] * (1 + len(arrays)),
        out_specs=VMEM,
        input_output_aliases=aliases,
        compiler_params=pltpu.CompilerParams(vmem_limit_bytes=12 << 20),
        cost_estimate=pl.CostEstimate(
            flops=pairs * cap * rank * 4 * hidden.shape[1],
            bytes_accessed=sum(array.size for array in arrays) * 2,
            transcendentals=0,
        ),
    )(mine, hidden, *arrays)


def turn(step):
    tp_count = lax.axis_size("tp")
    return [(i, (i + 2 * step) % tp_count) for i in range(tp_count)]


def swap():
    return [(i, i ^ 1) for i in range(lax.axis_size("tp"))]


def low_rank_down(partial):
    chips = lax.axis_size("tp") // 2
    t = lax.axis_index("tp")
    z, core = t // 2, t % 2
    half = partial.shape[0] // 2
    piece = half // chips
    cut = lambda array, start, size: lax.dynamic_slice_in_dim(array, start, size, 0)
    total = cut(partial, core * half, half) + lax.ppermute(
        cut(partial, (1 - core) * half, half), "tp", swap()
    )
    pieces = [
        lax.ppermute(cut(total, (z + d) % chips * piece, piece), "tp", turn(d))
        for d in range(1, chips)
    ]
    return (cut(total, z * piece, piece) + sum(pieces)).astype(jnp.bfloat16)


def low_rank_up(summed):
    chips = lax.axis_size("tp") // 2
    own = jnp.stack([summed] + [lax.ppermute(summed, "tp", turn(d)) for d in range(1, chips)])
    return own, lax.ppermute(own, "tp", swap())


def blend(base, out, counts, mine, j, both, ups, cap):
    rank = both.shape[1] // 2
    groups = base.shape[0] // cap
    lane = lax.broadcasted_iota(jnp.int32, both.shape, 1)
    none = jnp.zeros_like(both)
    left = jnp.concatenate(
        [jnp.where(lane < rank, both, none), jnp.where(lane < rank, none, both)], axis=0
    )
    delta = jnp.dot(left, jnp.concatenate(ups, axis=0), preferred_element_type=jnp.float32)
    rows = lax.broadcasted_iota(jnp.int32, (cap, base.shape[1]), 0)
    for n in range(2):
        g = mine[ORDER, j[n]]
        here = pl.ds(pl.multiple_of(g * cap, cap), cap)
        merged = base[here, :] + ADAPTER_SCALE * delta[n * cap : (n + 1) * cap]
        out[here, :] = jnp.where(rows < counts[mine[FLAGS, ME] * groups + g], merged, 0.0).astype(out.dtype)


def out_kernel(cap, mine, counts, base, own, other, main, *refs):
    extras, out, low = refs[:2], refs[2], refs[3]
    groups = base.shape[0] // cap
    chips, piece, rank = own.shape[0], own.shape[1], own.shape[2] // 2
    lanes = base.shape[1]
    z, core = mine[FLAGS, CHIP], mine[FLAGS, CORE]
    steps = rank // 16
    pairs = (groups - EXTRA) // 2
    for d in range(chips):
        quarter = lax.rem(z - d + chips, chips)
        for ref, half in ((own, core), (other, 1 - core)):
            at = pl.multiple_of((half * chips + quarter) * piece, piece)
            low[pl.ds(at, piece), :] = ref[d]

    def up(j):
        place = mine[PLACE, j]
        unit = lax.div(place, 2)
        at = (place - 2 * unit) * steps * lanes
        return [
            main[unit, :, pl.ds(pl.multiple_of(at + part * lanes, lanes), lanes)]
            for part in range(steps)
        ]

    def body(i, carry):
        both = low[pl.ds(pl.multiple_of(i * cap, cap), cap), :]
        blend(base, out, counts, mine, (i, i + pairs), both, up(i) + up(i + pairs), cap)
        return carry

    lax.fori_loop(0, pairs, body, 0, unroll=True)
    for e in range(EXTRA // 2):
        ups = [
            pack[:, (e * steps + part) * lanes : (e * steps + part + 1) * lanes]
            for pack in extras
            for part in range(steps)
        ]
        both = low[(pairs + e) * cap : (pairs + e + 1) * cap, :]
        spots = (groups - EXTRA + e, groups - EXTRA // 2 + e)
        blend(base, out, counts, mine, spots, both, ups, cap)


def whole(array):
    return pl.BlockSpec(array.shape, lambda i: (0,) * array.ndim)


def combine(mine, counts, base, own, other, main, extras, cap, rank):
    packs = pl.BlockSpec((main.shape[0], 16, main.shape[2]), lambda i: (0, rank // 8, 0))
    pack = pl.BlockSpec((16, main.shape[2]), lambda i: (rank // 8, 0))
    return pl.pallas_call(
        functools.partial(out_kernel, cap),
        grid=(1,),
        out_shape=jax.ShapeDtypeStruct(base.shape, jnp.bfloat16),
        in_specs=[SMEM, SMEM, whole(base), whole(own), whole(other), packs, pack, pack],
        out_specs=whole(base),
        scratch_shapes=[
            pltpu.VMEM((2 * own.shape[0] * own.shape[1], own.shape[2]), jnp.bfloat16)
        ],
        compiler_params=pltpu.CompilerParams(vmem_limit_bytes=8 << 20),
        cost_estimate=pl.CostEstimate(
            flops=base.size * rank * 2, bytes_accessed=base.size * 8, transcendentals=0
        ),
    )(mine, counts, base, own, other, main, *extras)


def on_device(
    hidden,
    value_weight,
    down_weights,
    up_weights,
    group_adapter_id,
    adapter_storage_row,
    group_live_count,
):
    dp_count = lax.axis_size("dp")
    me = lax.axis_index("dp")
    owned, rank, width = down_weights.shape
    groups = group_adapter_id.shape[0] // dp_count
    cap = hidden.shape[0] // groups
    spot = jnp.stack([me, lax.axis_index("tp")]).astype(jnp.int32)
    served, mine = index_tables(spot, group_adapter_id, adapter_storage_row, dp_count)

    def wide(hidden, value_weight, down_weights, up_weights):
        stored = adapter_storage_row[group_adapter_id]
        owners = (stored // owned).reshape(dp_count, groups)
        slots = (stored % owned).reshape(dp_count, groups)
        same = owners[:, :, None] == owners[:, None, :]
        earlier = jnp.arange(groups)[None, None, :] < jnp.arange(groups)[None, :, None]
        ranking = jnp.sum(same & earlier, axis=2)
        hits = (owners == me)[:, :, None] & (ranking[:, :, None] == jnp.arange(MOST))
        rows = jnp.sum(jnp.where(hits, slots[:, :, None], 0), axis=1).reshape(-1)
        my_owners = lax.dynamic_index_in_dim(owners, me, 0, keepdims=False)
        my_ranking = lax.dynamic_index_in_dim(ranking, me, 0, keepdims=False)
        base_terms = jnp.dot(hidden, value_weight, preferred_element_type=jnp.float32)
        base = lax.psum_scatter(base_terms, "tp", scatter_dimension=1, tiled=True)
        downs = lax.all_to_all(down_weights[rows], "dp", 0, 0, tiled=True)
        ups = lax.all_to_all(up_weights[rows], "dp", 0, 0, tiled=True)
        picked = my_owners * MOST + my_ranking
        partial = jnp.einsum(
            "gcd,grd->gcr",
            hidden.reshape(groups, cap, width),
            downs[picked],
            preferred_element_type=jnp.float32,
        )
        low = low_rank_sum(partial.reshape(groups * cap, rank))
        counts = lax.dynamic_slice_in_dim(group_live_count, me * groups, groups)
        return finish(base, low, ups[picked], counts)

    def narrow(hidden, value_weight, down_weights, up_weights):
        trees = (True, False)
        soon = [
            (tree, ((2, part[0]), (2, part[1]), (near, 2), (near, 3)))
            for tree in trees
            for near, part in ((1, (0, 1)), (3, (2, 3)))
        ]
        late = [(tree, ((near, 0), (near, 1))) for tree in trees for near in (1, 3)]
        late += [(tree, ((0, 0), (0, 1), (0, 2), (0, 3))) for tree in trees]
        moves = ((1, 0), (-1, 0), (0, 1), (0, -1))
        turned = ((0, 1), (0, 2), (0, -1), (1, 0), (2, 0), (-1, 0))
        send = lambda values, ways: [shift(v, *way) for v, way in zip(values, ways)]
        barrier = lax.optimization_barrier
        gathered = gather_units(
            functools.partial(extra_kernel, soon),
            [len(units) for _, units in soon],
            served,
            mine,
            down_weights,
            up_weights,
        )
        unit, dtype = gathered[0].shape[1:], gathered[0].dtype
        fresh = send(gathered, moves)
        later_served, _ = barrier((served, gathered))
        main_sent, *later = gather_units(
            functools.partial(gather_kernel, late),
            [dp_count] + [len(units) for _, units in late],
            later_served,
            mine,
            down_weights,
            up_weights,
        )
        near, homes = later[:4], later[4:]
        fresh, near, main_sent = barrier((fresh, near, main_sent))
        relayed = vmem_call(
            relay_kernel, ((2,) + unit,) * 4, dtype, (mine,), (*fresh, *near)
        )
        base_hidden, relayed = barrier((hidden, relayed))
        base_terms = base_product(base_hidden, value_weight)
        near_a, main_sent, base_terms = barrier((send(relayed, moves), main_sent, base_terms))
        base = lax.psum_scatter(base_terms, "tp", scatter_dimension=1, tiled=True)
        main = lax.all_to_all(main_sent, "dp", 0, 0, tiled=True)
        tree_arrays = [
            (homes[h], near_a[2 * h], near_a[2 * h + 1], fresh[2 * h], fresh[2 * h + 1])
            for h in range(2)
        ]
        lines = vmem_call(
            line_kernel, (unit,) * 8, dtype, (mine,), tree_arrays[0] + tree_arrays[1]
        )
        got = send(lines[1:4] + lines[5:8], turned)
        partial = low_call(low_main_kernel, cap, rank, mine, hidden, (main,), {})
        got, partial = barrier((got, partial))
        extras = vmem_call(
            pick_kernel, (unit,) * 2, dtype, (mine,), (lines[0], *got[:3], lines[4], *got[3:])
        )
        partial = low_call(
            low_extra_kernel, cap, rank, mine, hidden, (*extras, partial), {4: 0}
        )
        own, other = low_rank_up(low_rank_down(partial))
        return combine(mine, group_live_count, base, own, other, main, extras, cap, rank)

    return lax.cond(
        mine[FLAGS, FITS] == 1, narrow, wide, hidden, value_weight, down_weights, up_weights
    )


def solution(mesh):
    return jax.shard_map(
        on_device,
        mesh=mesh,
        in_specs=(
            P("dp", "tp"),
            P("tp", None),
            P("dp", None, "tp"),
            P("dp", None, "tp"),
            P(),
            P(),
            P(),
        ),
        out_specs=P("dp", "tp"),
        check_vma=False,
    )
```
